32 devices in a mesh: seq: 8 (over z, x), bin: 4 (over y, core).
Axes of the slice: x: 2, y: 2, z: 4, core: 2. Of those that a mesh axis runs over, the one named last changes fastest.
Arguments:
- tokens: bfloat16 [4, 48, 24, 768], P('bin', 'seq'), may hold values from -8 to 8
- timestep: int32 [1], replicated, may hold values from 0 to 999
- mod_weight: bfloat16 [256, 3072], replicated, may hold values from -0.375 to 0.375
- col_qkv: bfloat16 [768, 2304], replicated, may hold values from -0.41650635 to 0.41650635
- col_out: bfloat16 [768, 768], replicated, may hold values from -0.21875 to 0.21875
- bin_qkv: bfloat16 [768, 2304], replicated, may hold values from -0.41650635 to 0.41650635
- bin_out: bfloat16 [768, 768], replicated, may hold values from -0.21875 to 0.21875
Outputs:
- result: bfloat16 [4, 48, 24, 768], P('bin', 'seq')
The draws below stay inside these ranges and needn't reach their ends.
All inputs are finite; a program needn't handle non-finite values.
Results may differ from the reference program's by a relative error of at most 0.012.
Values may be sent and summed in bfloat16 or wider, within the bound.
No kernel may reach another device: no remote copies, remote signals or barrier semaphores. Data moves between devices by JAX's collectives and lax.ppermute only.
A program may use at most 128 MiB of HBM per device.

```python
import math
import jax
import jax.numpy as jnp
from jax import lax

D = 768
HEADS = 12
HD = 64
FREQ = 256
H = 48
W = 24
BINS = 4


def drawn_weight(key, salt):
    base_key = jax.random.fold_in(key, salt)
    spread = D ** (-0.5)
    base = jax.random.truncated_normal(base_key, -6.0, 6.0, (D, 3 * D), jnp.float32) * spread
    return base.astype(jnp.bfloat16)


def draw_tokens(key, part):
    noise_key = jax.random.fold_in(key, 11)
    values = jax.random.truncated_normal(noise_key, -6.0, 6.0, (BINS, H, W, D), jnp.float32)
    return values.astype(jnp.bfloat16)


def draw_col_qkv(key, part):
    return drawn_weight(key, 21)


def draw_bin_qkv(key, part):
    return drawn_weight(key, 22)


def bell_draw(own_key, shape, scale, limit, held_as=jnp.bfloat16):
    entries = jax.random.normal(own_key, shape, jnp.float32) * scale
    return jnp.minimum(jnp.maximum(entries, -limit), limit).astype(held_as)


def setup_inputs(seed: int = 0) -> dict:
    seeds = jax.random.split(jax.random.key(seed), 8)
    return {
        "tokens": draw_tokens(jax.random.fold_in(seeds[7], 71), 0),
        "timestep": jax.random.randint(seeds[1], (1,), 0, 1000).astype(jnp.int32),
        "mod_weight": bell_draw(seeds[2], (FREQ, 4 * D), FREQ ** -0.5, 0.375),
        "col_qkv": draw_col_qkv(jax.random.fold_in(seeds[7], 71), 0),
        "col_out": bell_draw(seeds[4], (D, D), D ** -0.5, 0.21875),
        "bin_qkv": draw_bin_qkv(jax.random.fold_in(seeds[7], 71), 0),
        "bin_out": bell_draw(seeds[6], (D, D), D ** -0.5, 0.21875),
    }


def modulation(timestep, mod_weight):
    half = FREQ // 2
    freqs = jnp.exp(-math.log(10000.0) * jnp.arange(half, dtype=jnp.float32) / half)
    angle = timestep.astype(jnp.float32)[0] * freqs
    emb = jax.nn.silu(jnp.concatenate([jnp.cos(angle), jnp.sin(angle)])).astype(jnp.bfloat16)
    return jnp.dot(emb[None, :], mod_weight, preferred_element_type=jnp.float32)[0]

def layer_norm(values, shift, scale):
    xf = values.astype(jnp.float32)
    mean = lax.optimization_barrier(jnp.mean(xf, axis=-1, keepdims=True))
    var = lax.optimization_barrier(jnp.mean((xf - mean) ** 2, axis=-1, keepdims=True))
    return ((xf - mean) * lax.rsqrt(var + 1e-06) * (1.0 + scale) + shift).astype(jnp.bfloat16)

def column_bin(normed, col_qkv, col_out):
    qkv = jnp.dot(normed.reshape(-1, D), col_qkv, preferred_element_type=jnp.float32).astype(jnp.bfloat16)
    qkv = qkv.reshape(H, W, 3, HEADS, HD)
    query, key, value = (qkv[:, :, 0], qkv[:, :, 1], qkv[:, :, 2])
    scores = jnp.einsum('iwhd,jwhd->whij', query.astype(jnp.float32), key.astype(jnp.float32)) * HD ** (-0.5)
    weights = jax.nn.softmax(scores, axis=-1).astype(jnp.bfloat16)
    context = jnp.einsum('whij,jwhd->iwhd', weights.astype(jnp.float32), value.astype(jnp.float32)).astype(jnp.bfloat16)
    return jnp.dot(context.reshape(-1, D), col_out, preferred_element_type=jnp.float32).astype(jnp.bfloat16).reshape(H, W, D)

def reference(tokens, timestep, mod_weight, col_qkv, col_out, bin_qkv, bin_out):
    mod = modulation(timestep, mod_weight)
    shift1, scale1, shift2, scale2 = (mod[:D], mod[D:2 * D], mod[2 * D:3 * D], mod[3 * D:])
    normed1 = layer_norm(tokens, shift1, scale1)
    attended = lax.map(lambda one: column_bin(one, col_qkv, col_out), normed1)
    hidden = (tokens.astype(jnp.float32) + attended.astype(jnp.float32)).astype(jnp.bfloat16)
    normed2 = layer_norm(hidden, shift2, scale2)
    qkv = jnp.dot(normed2.reshape(-1, D), bin_qkv, preferred_element_type=jnp.float32).astype(jnp.bfloat16)
    qkv = qkv.reshape(BINS, H, W, 3, HEADS, HD)
    query, key, value = (qkv[:, :, :, 0], qkv[:, :, :, 1], qkv[:, :, :, 2])
    scores = jnp.einsum('bxyhd,cxyhd->bxyhc', query.astype(jnp.float32), key.astype(jnp.float32)) * HD ** (-0.5)
    weights = jax.nn.softmax(scores, axis=-1).astype(jnp.bfloat16)
    context = jnp.einsum('bxyhc,cxyhd->bxyhd', weights.astype(jnp.float32), value.astype(jnp.float32)).astype(jnp.bfloat16)
    projected = jnp.dot(context.reshape(-1, D), bin_out, preferred_element_type=jnp.float32).reshape(BINS, H, W, D)
    return (hidden.astype(jnp.float32) + projected).astype(jnp.bfloat16)
```

```python
import functools
import math

import jax
import jax.numpy as jnp
from jax import lax
from jax.experimental import pallas as pl
from jax.experimental.pallas import tpu as pltpu
from jax.sharding import PartitionSpec as P

D = 768
HEADS = 12
HD = 64
FREQ = 256
PAIR = 2 * HD
BF = jnp.bfloat16
F32 = jnp.float32


def modulation(timestep, mod_weight):
    half = FREQ // 2
    freqs = jnp.exp(-math.log(10000.0) * jnp.arange(half, dtype=jnp.float32) / half)
    angle = timestep.astype(jnp.float32)[0] * freqs
    emb = jax.nn.silu(jnp.concatenate([jnp.cos(angle), jnp.sin(angle)])).astype(jnp.bfloat16)
    return jnp.dot(emb[None, :], mod_weight, preferred_element_type=jnp.float32)[0]


def norm_rows(xf, mod_ref, which):
    shift = mod_ref[2 * which : 2 * which + 1, :]
    scale = mod_ref[2 * which + 1 : 2 * which + 2, :]
    mean = jnp.mean(xf, axis=-1, keepdims=True)
    cent = xf - mean
    var = jnp.mean(cent * cent, axis=-1, keepdims=True)
    return (cent * lax.rsqrt(var + 1e-06) * (1.0 + scale) + shift).astype(BF)


def stacked(refs):
    return jnp.concatenate([r[...].astype(F32) for r in refs], axis=0)


def project(normed, w_ref, which, out_ref, factor=None):
    y = jnp.dot(normed, w_ref[:, which * D : (which + 1) * D], preferred_element_type=F32)
    if factor is not None:
        y = y * factor
    out_ref[...] = y.astype(BF)


def divided(values, by, top):
    total = jnp.zeros_like(values)
    for step in range(by, top, by):
        total = total + (values >= step).astype(jnp.int32)
    return total


def message_rows(shape, row_dim, token_dim, rows, cols, width, owner):
    r = lax.broadcasted_iota(jnp.int32, shape, row_dim)
    t = lax.broadcasted_iota(jnp.int32, shape, token_dim)
    i = divided(r, cols, shape[row_dim])
    source = i * width + owner * cols + (r - i * cols)
    hit = (r < rows * cols) & (t == source)
    return jnp.where(hit, 1.0, 0.0).astype(BF)


def pack_kernel(dims, z_ref, tok_ref, *out_refs):
    rows, cols, width = dims
    x = tok_ref[...]
    for m, out in enumerate(out_refs):
        shape = (out.shape[0], x.shape[0])
        pick = message_rows(shape, 0, 1, rows, cols, width, z_ref[0] ^ m)
        out[...] = jnp.dot(pick, x, preferred_element_type=F32).astype(BF)


def unpack_kernel(dims, groups, z_ref, *refs):
    rows, cols, width = dims
    out = refs[groups]
    total = None
    for m in range(groups):
        shape = (out.shape[0], refs[m].shape[0])
        put = message_rows(shape, 1, 0, rows, cols, width, z_ref[0] ^ m)
        part = jnp.dot(put, refs[m][...], preferred_element_type=F32)
        total = part if total is None else total + part
    out[...] = total.astype(BF)


def col_own_kernel(groups, *refs):
    own, (mod_ref, w_ref, q_ref, k_ref, v_ref) = refs[:groups], refs[groups:]
    normed = norm_rows(stacked(own), mod_ref, 0)
    project(normed, w_ref, 0, q_ref, HD**-0.5)
    project(normed, w_ref, 1, k_ref)
    project(normed, w_ref, 2, v_ref)


def col_attend_kernel(groups, dims, *refs):
    rows, cols, _ = dims
    own, other = refs[:groups], refs[groups : 2 * groups]
    mod_ref, w_ref, wo_ref, q_ref, k_ref, v_ref, h_ref, k2_ref, v2_ref, c_ref = refs[2 * groups :]
    normed = norm_rows(stacked(other), mod_ref, 0)
    project(normed, w_ref, 1, k2_ref)
    project(normed, w_ref, 2, v2_ref)
    n = q_ref.shape[0]
    pad = own[0].shape[0]

    def column(shape, dim):
        r = lax.broadcasted_iota(jnp.int32, shape, dim)
        r = r - pad * divided(r, pad, shape[dim])
        return r, r - cols * divided(r, cols, pad)

    shape = (n, 2 * n)
    _, q_col = column(shape, 0)
    k_row, k_col = column(shape, 1)
    bias = jnp.where((q_col == k_col) & (k_row < rows * cols), 0.0, -1e30).astype(F32)
    bias = jnp.concatenate([bias, bias], axis=0)
    low = lax.broadcasted_iota(jnp.int32, (n, PAIR), 1) < HD
    for j in range(HEADS // 2):
        lanes = slice(j * PAIR, (j + 1) * PAIR)
        q = q_ref[:, lanes]
        zero = jnp.zeros_like(q)
        q = jnp.concatenate([jnp.where(low, q, zero), jnp.where(low, zero, q)], axis=0)
        k = jnp.concatenate([k_ref[:, lanes], k2_ref[:, lanes]], axis=0)
        v = jnp.concatenate([v_ref[:, lanes], v2_ref[:, lanes]], axis=0)
        s = lax.dot_general(q, k, (((1,), (1,)), ((), ())), preferred_element_type=F32) + bias
        e = jnp.exp(s - jnp.max(s, axis=-1, keepdims=True))
        total = jnp.sum(e, axis=-1, keepdims=True)
        c = jnp.dot(e.astype(BF), v, preferred_element_type=F32) / total
        c_ref[:, lanes] = jnp.where(low, c[:n], c[n:]).astype(BF)
    a = jnp.dot(c_ref[...], wo_ref[...], preferred_element_type=F32).astype(BF)
    h_ref[...] = (stacked(own) + a.astype(F32)).astype(BF)


def bin_own_kernel(h_ref, hc_ref, mod_ref, w_ref, q_ref, k_ref, v_ref, kc_ref, vc_ref):
    normed = norm_rows(h_ref[...].astype(F32), mod_ref, 1)
    project(normed, w_ref, 0, q_ref, HD**-0.5)
    project(normed, w_ref, 1, k_ref)
    project(normed, w_ref, 2, v_ref)
    normed = norm_rows(hc_ref[...].astype(F32), mod_ref, 1)
    project(normed, w_ref, 1, kc_ref)
    project(normed, w_ref, 2, vc_ref)


def bin_kv_kernel(h_ref, mod_ref, w_ref, k_ref, v_ref):
    normed = norm_rows(h_ref[...].astype(F32), mod_ref, 1)
    project(normed, w_ref, 1, k_ref)
    project(normed, w_ref, 2, v_ref)


def bin_attend_kernel(groups, hd_ref, mod_ref, w_ref, wo_ref, h_ref, q_ref, *refs):
    keys, values = refs[0:6:2], refs[1:6:2]
    outs, (kd_ref, vd_ref) = refs[6 : 6 + groups], refs[6 + groups :]
    bin_kv_kernel(hd_ref, mod_ref, w_ref, kd_ref, vd_ref)
    lane = lax.broadcasted_iota(jnp.int32, (D, 128), 0)
    head = lax.broadcasted_iota(jnp.int32, (D, 128), 1)
    gather = ((lane >= head * HD) & (lane < (head + 1) * HD)).astype(F32).astype(BF)
    lane = lax.broadcasted_iota(jnp.int32, (128, D), 1)
    head = lax.broadcasted_iota(jnp.int32, (128, D), 0)
    spread = ((lane >= head * HD) & (lane < (head + 1) * HD)).astype(F32).astype(BF)
    q = q_ref[...].astype(F32)
    scores = [
        jnp.dot((q * k[...].astype(F32)).astype(BF), gather, preferred_element_type=F32)
        for k in (*keys, kd_ref)
    ]
    top = functools.reduce(jnp.maximum, scores)
    exps = [jnp.exp(s - top) for s in scores]
    scale = 1.0 / functools.reduce(jnp.add, exps)
    c = None
    for e, v in zip(exps, (*values, vd_ref)):
        p = jnp.dot((e * scale).astype(BF), spread, preferred_element_type=F32)
        part = p * v[...].astype(F32)
        c = part if c is None else c + part
    out = jnp.dot(c.astype(BF), wo_ref[...], preferred_element_type=F32)
    out = h_ref[...].astype(F32) + out
    pad = outs[0].shape[0]
    for m, o in enumerate(outs):
        o[...] = out[m * pad : (m + 1) * pad].astype(BF)


def call(kernel, outs, scratch, *args, flops=0):
    def space(a):
        return pl.BlockSpec(memory_space=pltpu.SMEM if a.dtype == jnp.int32 else pltpu.VMEM)

    moved = sum(a.size * a.dtype.itemsize for a in args)
    return pl.pallas_call(
        kernel,
        out_shape=[jax.ShapeDtypeStruct(o, BF) for o in outs],
        in_specs=[space(a) for a in args],
        out_specs=[pl.BlockSpec(memory_space=pltpu.VMEM)] * len(outs),
        scratch_shapes=[pltpu.VMEM(s, BF) for s in scratch],
        compiler_params=pltpu.CompilerParams(vmem_limit_bytes=24 * 1024 * 1024),
        cost_estimate=pl.CostEstimate(flops=flops, bytes_accessed=moved, transcendentals=0),
    )(*args)


def column_path(tokens, timestep, mod_weight, col_qkv, col_out, bin_qkv, bin_out):
    rows, width = tokens.shape[1], tokens.shape[2]
    owners = lax.axis_size("seq")
    groups = owners // 2
    cols = width // groups
    dims = (rows, cols, width)
    pad = -(-rows * cols // 8) * 8
    n = groups * pad

    def over_group(x, m):
        return lax.ppermute(x, "seq", [(i, i ^ (2 * m)) for i in range(owners)])

    def over_pair(x):
        return lax.ppermute(x, "seq", [(i, i ^ 1) for i in range(owners)])

    def over_bin(x, m):
        return lax.ppermute(x, "bin", [(i, i ^ m) for i in range(4)])

    z = (lax.axis_index("seq") // 2).astype(jnp.int32).reshape(1)
    flat = tokens.reshape(rows * width, D)
    sent = call(functools.partial(pack_kernel, dims), [(pad, D)] * groups, [], z, flat)
    own = [sent[0]] + [over_group(sent[m], m) for m in range(1, groups)]
    other = [over_pair(x) for x in own]
    mod = modulation(timestep, mod_weight).reshape(4, D)

    full = (n, D)
    q, k, v = call(
        functools.partial(col_own_kernel, groups), [full] * 3, [], *own, mod, col_qkv,
        flops=6 * n * D * D,
    )
    (h,) = call(
        functools.partial(col_attend_kernel, groups, dims), [full], [full] * 3,
        *own, *other, mod, col_qkv, col_out, q, k, v,
        flops=8 * n * D * D,
    )
    hy = over_bin(h, 2)
    hc = over_bin(h, 1)
    hd = over_bin(hy, 1)
    q, k, v, kc, vc = call(
        bin_own_kernel, [full] * 5, [], h, hc, mod, bin_qkv, flops=10 * n * D * D
    )
    ky, vy = call(bin_kv_kernel, [full] * 2, [], hy, mod, bin_qkv, flops=4 * n * D * D)
    done = call(
        functools.partial(bin_attend_kernel, groups), [(pad, D)] * groups, [full] * 2,
        hd, mod, bin_qkv, bin_out, h, q, k, v, kc, vc, ky, vy,
        flops=8 * n * D * D,
    )
    back = [done[0]] + [over_group(done[m], m) for m in range(1, groups)]
    (out,) = call(
        functools.partial(unpack_kernel, dims, groups), [(rows * width, D)], [], z, *back
    )
    return out.reshape(tokens.shape)


def layer_norm(values, shift, scale):
    xf = values.astype(jnp.float32)
    mean = jnp.mean(xf, axis=-1, keepdims=True)
    var = jnp.mean((xf - mean) ** 2, axis=-1, keepdims=True)
    return ((xf - mean) * lax.rsqrt(var + 1e-06) * (1.0 + scale) + shift).astype(jnp.bfloat16)


def across_bins(query, key, value):
    scores = jnp.sum(
        query.astype(jnp.float32)[:, None] * key.astype(jnp.float32)[None], axis=-1
    ) * HD ** (-0.5)
    weights = jax.nn.softmax(scores, axis=1).astype(jnp.bfloat16)
    context = jnp.sum(
        weights.astype(jnp.float32)[..., None] * value.astype(jnp.float32)[None], axis=1
    )
    return context.astype(jnp.bfloat16)


def general_path(tokens, timestep, mod_weight, col_qkv, col_out, bin_qkv, bin_out):
    mod = modulation(timestep, mod_weight)
    shift1, scale1, shift2, scale2 = (mod[:D], mod[D : 2 * D], mod[2 * D : 3 * D], mod[3 * D :])
    rows_here = tokens.shape[1]
    width_all = tokens.shape[2]
    owners = lax.axis_size("seq")
    cols_each = width_all // owners
    normed1 = layer_norm(tokens, shift1, scale1)
    grouped = normed1.reshape(1, rows_here, owners, cols_each, D)
    query_weight = col_qkv[:, :D].reshape(D, HEADS, HD)
    key_weight = col_qkv[:, D : 2 * D].reshape(D, HEADS, HD)
    value_weight = col_qkv[:, 2 * D :].reshape(D, HEADS, HD)
    out_weight = col_out.reshape(HEADS, HD, D)
    piece = lax.all_to_all(grouped, "seq", split_axis=2, concat_axis=1, tiled=True)
    height = piece.shape[1]
    count = piece.shape[3]
    local = piece[0, :, 0]
    query = jnp.einsum(
        "iwc,chd->whid", local, query_weight, preferred_element_type=jnp.float32
    ).astype(jnp.bfloat16)
    key = jnp.einsum("iwc,chd->whid", local, key_weight, preferred_element_type=jnp.float32).astype(
        jnp.bfloat16
    )
    value = jnp.einsum(
        "iwc,chd->whid", local, value_weight, preferred_element_type=jnp.float32
    ).astype(jnp.bfloat16)
    scores = jnp.einsum("whid,whjd->whij", query, key, preferred_element_type=jnp.float32) * HD ** (
        -0.5
    )
    weights = jax.nn.softmax(scores, axis=-1).astype(jnp.bfloat16)
    context = jnp.einsum(
        "whij,whjd->whid", weights, value, preferred_element_type=jnp.float32
    ).astype(jnp.bfloat16)
    out = jnp.einsum(
        "whid,hde->iwe", context, out_weight, preferred_element_type=jnp.float32
    ).astype(jnp.bfloat16)
    attended = out.reshape(1, height, 1, count, D)
    back = lax.all_to_all(attended, "seq", split_axis=1, concat_axis=2, tiled=True)
    back = back.reshape(1, rows_here, width_all, D)
    hidden = (tokens.astype(jnp.float32) + back.astype(jnp.float32)).astype(jnp.bfloat16)
    normed2 = layer_norm(hidden, shift2, scale2)
    flat = normed2.reshape(-1, D)
    positions = flat.shape[0]
    every = lax.all_gather(normed2, "bin", axis=0, tiled=True)
    nbins = every.shape[0]
    every_flat = every.reshape(-1, D)
    query = jnp.dot(flat, bin_qkv[:, :D], preferred_element_type=jnp.float32).astype(jnp.bfloat16)
    keys_all = jnp.dot(
        every_flat, bin_qkv[:, D : 2 * D], preferred_element_type=jnp.float32
    ).astype(jnp.bfloat16)
    values_all = jnp.dot(
        every_flat, bin_qkv[:, 2 * D :], preferred_element_type=jnp.float32
    ).astype(jnp.bfloat16)
    context = across_bins(
        query.reshape(1, positions, HEADS, HD),
        keys_all.reshape(nbins, positions, HEADS, HD),
        values_all.reshape(nbins, positions, HEADS, HD),
    )
    projected = jnp.dot(context.reshape(-1, D), bin_out, preferred_element_type=jnp.float32)
    projected = projected.reshape(1, rows_here, width_all, D)
    return (hidden.astype(jnp.float32) + projected).astype(jnp.bfloat16)


def per_device(tokens, *rest):
    owners, width = lax.axis_size("seq"), tokens.shape[2]
    small = owners in (4, 8) and width % (owners // 2) == 0 and lax.axis_size("bin") == 4
    if small and tokens.shape[1] * width <= 256:
        return column_path(tokens, *rest)
    return general_path(tokens, *rest)


def solution(mesh):
    placed = (P("bin", "seq", None, None), P(), P(), P(), P(), P(), P())
    return jax.shard_map(
        per_device,
        mesh=mesh,
        in_specs=placed,
        out_specs=P("bin", "seq", None, None),
        check_vma=False,
    )
```

```python
import functools
import math

import jax
import jax.numpy as jnp
from jax import lax
from jax.experimental import pallas as pl
from jax.experimental.pallas import tpu as pltpu
from jax.sharding import PartitionSpec as P

D = 768
HEADS = 12
HD = 64
FREQ = 256
PAIR = 2 * HD
BF = jnp.bfloat16
F32 = jnp.float32


def modulation(timestep, mod_weight):
    half = FREQ // 2
    freqs = jnp.exp(-math.log(10000.0) * jnp.arange(half, dtype=jnp.float32) / half)
    angle = timestep.astype(jnp.float32)[0] * freqs
    emb = jax.nn.silu(jnp.concatenate([jnp.cos(angle), jnp.sin(angle)])).astype(jnp.bfloat16)
    return jnp.dot(emb[None, :], mod_weight, preferred_element_type=jnp.float32)[0]


def norm_rows(xf, mod_ref, which):
    shift = mod_ref[2 * which : 2 * which + 1, :]
    scale = mod_ref[2 * which + 1 : 2 * which + 2, :]
    mean = jnp.mean(xf, axis=-1, keepdims=True)
    cent = xf - mean
    var = jnp.mean(cent * cent, axis=-1, keepdims=True)
    return (cent * lax.rsqrt(var + 1e-06) * (1.0 + scale) + shift).astype(BF)


def stacked(refs):
    return jnp.concatenate([r[...].astype(F32) for r in refs], axis=0)


def project(normed, w_ref, which, out_ref, factor=None):
    y = jnp.dot(normed, w_ref[:, which * D : (which + 1) * D], preferred_element_type=F32)
    if factor is not None:
        y = y * factor
    out_ref[...] = y.astype(BF)


def divided(values, by, top):
    total = jnp.zeros_like(values)
    for step in range(by, top, by):
        total = total + (values >= step).astype(jnp.int32)
    return total


def message_rows(shape, row_dim, token_dim, rows, cols, width, owner):
    r = lax.broadcasted_iota(jnp.int32, shape, row_dim)
    t = lax.broadcasted_iota(jnp.int32, shape, token_dim)
    i = divided(r, cols, shape[row_dim])
    source = i * width + owner * cols + (r - i * cols)
    hit = (r < rows * cols) & (t == source)
    return jnp.where(hit, 1.0, 0.0).astype(BF)


def pack_kernel(dims, z_ref, tok_ref, *out_refs):
    rows, cols, width = dims
    x = tok_ref[...]
    for m, out in enumerate(out_refs):
        shape = (out.shape[0], x.shape[0])
        pick = message_rows(shape, 0, 1, rows, cols, width, z_ref[0] ^ m)
        out[...] = jnp.dot(pick, x, preferred_element_type=F32).astype(BF)


def unpack_kernel(dims, groups, z_ref, *refs):
    rows, cols, width = dims
    out = refs[groups]
    total = None
    for m in range(groups):
        shape = (out.shape[0], refs[m].shape[0])
        put = message_rows(shape, 1, 0, rows, cols, width, z_ref[0] ^ m)
        part = jnp.dot(put, refs[m][...], preferred_element_type=F32)
        total = part if total is None else total + part
    out[...] = total.astype(BF)


def col_own_kernel(groups, *refs):
    own, (mod_ref, w_ref, q_ref, k_ref, v_ref) = refs[:groups], refs[groups:]
    normed = norm_rows(stacked(own), mod_ref, 0)
    project(normed, w_ref, 0, q_ref, HD**-0.5)
    project(normed, w_ref, 1, k_ref)
    project(normed, w_ref, 2, v_ref)


def col_attend_kernel(groups, dims, *refs):
    rows, cols, _ = dims
    own, other = refs[:groups], refs[groups : 2 * groups]
    mod_ref, w_ref, wo_ref, q_ref, k_ref, v_ref, h_ref, k2_ref, v2_ref, c_ref = refs[2 * groups :]
    normed = norm_rows(stacked(other), mod_ref, 0)
    project(normed, w_ref, 1, k2_ref)
    project(normed, w_ref, 2, v2_ref)
    n = q_ref.shape[0]
    pad = own[0].shape[0]

    def column(shape, dim):
        r = lax.broadcasted_iota(jnp.int32, shape, dim)
        r = r - pad * divided(r, pad, shape[dim])
        return r, r - cols * divided(r, cols, pad)

    shape = (n, 2 * n)
    _, q_col = column(shape, 0)
    k_row, k_col = column(shape, 1)
    bias = jnp.where((q_col == k_col) & (k_row < rows * cols), 0.0, -1e30).astype(F32)
    bias = jnp.concatenate([bias, bias], axis=0)
    low = lax.broadcasted_iota(jnp.int32, (n, PAIR), 1) < HD
    for j in range(HEADS // 2):
        lanes = slice(j * PAIR, (j + 1) * PAIR)
        q = q_ref[:, lanes]
        zero = jnp.zeros_like(q)
        q = jnp.concatenate([jnp.where(low, q, zero), jnp.where(low, zero, q)], axis=0)
        k = jnp.concatenate([k_ref[:, lanes], k2_ref[:, lanes]], axis=0)
        v = jnp.concatenate([v_ref[:, lanes], v2_ref[:, lanes]], axis=0)
        s = lax.dot_general(q, k, (((1,), (1,)), ((), ())), preferred_element_type=F32) + bias
        e = jnp.exp(s - jnp.max(s, axis=-1, keepdims=True))
        total = jnp.sum(e, axis=-1, keepdims=True)
        c = jnp.dot(e.astype(BF), v, preferred_element_type=F32) / total
        c_ref[:, lanes] = jnp.where(low, c[:n], c[n:]).astype(BF)
    a = jnp.dot(c_ref[...], wo_ref[...], preferred_element_type=F32).astype(BF)
    h_ref[...] = (stacked(own) + a.astype(F32)).astype(BF)


def head_lanes(shape, lane_dim):
    lane = lax.broadcasted_iota(jnp.int32, shape, lane_dim)
    head = lax.broadcasted_iota(jnp.int32, shape, 1 - lane_dim)
    return ((lane >= head * HD) & (lane < (head + 1) * HD)).astype(F32).astype(BF)


def key_scores(query, normed, w_ref, s_ref):
    k = jnp.dot(normed, w_ref[:, D : 2 * D], preferred_element_type=F32).astype(BF).astype(F32)
    s_ref[...] = jnp.dot(
        (query * k).astype(BF), head_lanes((D, 128), 0), preferred_element_type=F32
    )


def bin_own_kernel(h_ref, hc_ref, mod_ref, w_ref, q_ref, v_ref, s_ref, vc_ref, sc_ref):
    normed = norm_rows(h_ref[...].astype(F32), mod_ref, 1)
    project(normed, w_ref, 0, q_ref, HD**-0.5)
    query = q_ref[...].astype(F32)
    key_scores(query, normed, w_ref, s_ref)
    project(normed, w_ref, 2, v_ref)
    normed = norm_rows(hc_ref[...].astype(F32), mod_ref, 1)
    key_scores(query, normed, w_ref, sc_ref)
    project(normed, w_ref, 2, vc_ref)


def bin_kv_kernel(h_ref, q_ref, mod_ref, w_ref, v_ref, s_ref):
    normed = norm_rows(h_ref[...].astype(F32), mod_ref, 1)
    key_scores(q_ref[...].astype(F32), normed, w_ref, s_ref)
    project(normed, w_ref, 2, v_ref)


def bin_attend_kernel(groups, hd_ref, q_ref, mod_ref, w_ref, wo_ref, h_ref, *refs):
    values, scores = refs[0:6:2], refs[1:6:2]
    outs, (vd_ref, sd_ref) = refs[6 : 6 + groups], refs[6 + groups :]
    bin_kv_kernel(hd_ref, q_ref, mod_ref, w_ref, vd_ref, sd_ref)
    scores = [s[...] for s in (*scores, sd_ref)]
    top = functools.reduce(jnp.maximum, scores)
    exps = [jnp.exp(s - top) for s in scores]
    scale = 1.0 / functools.reduce(jnp.add, exps)
    spread = head_lanes((128, D), 1)
    c = None
    for e, v in zip(exps, (*values, vd_ref)):
        p = jnp.dot((e * scale).astype(BF), spread, preferred_element_type=F32)
        part = p * v[...].astype(F32)
        c = part if c is None else c + part
    out = jnp.dot(c.astype(BF), wo_ref[...], preferred_element_type=F32)
    out = h_ref[...].astype(F32) + out
    pad = outs[0].shape[0]
    for m, o in enumerate(outs):
        o[...] = out[m * pad : (m + 1) * pad].astype(BF)


def call(kernel, outs, scratch, *args, cost=10**9):
    def space(a):
        return pl.BlockSpec(memory_space=pltpu.SMEM if a.dtype == jnp.int32 else pltpu.VMEM)

    moved = sum(a.size * a.dtype.itemsize for a in args)
    return pl.pallas_call(
        kernel,
        out_shape=[jax.ShapeDtypeStruct(*o) for o in outs],
        in_specs=[space(a) for a in args],
        out_specs=[pl.BlockSpec(memory_space=pltpu.VMEM)] * len(outs),
        scratch_shapes=[pltpu.VMEM(*s) for s in scratch],
        compiler_params=pltpu.CompilerParams(vmem_limit_bytes=24 * 1024 * 1024),
        cost_estimate=pl.CostEstimate(flops=cost, bytes_accessed=moved, transcendentals=0),
    )(*args)


def column_path(tokens, timestep, mod_weight, col_qkv, col_out, bin_qkv, bin_out):
    rows, width = tokens.shape[1], tokens.shape[2]
    owners = lax.axis_size("seq")
    groups = owners // 2
    cols = width // groups
    dims = (rows, cols, width)
    pad = -(-rows * cols // 8) * 8
    n = groups * pad

    def over_group(x, m):
        return lax.ppermute(x, "seq", [(i, i ^ (2 * m)) for i in range(owners)])

    def over_pair(x):
        return lax.ppermute(x, "seq", [(i, i ^ 1) for i in range(owners)])

    def over_bin(x, m):
        return lax.ppermute(x, "bin", [(i, i ^ m) for i in range(4)])

    message, full, lanes = ((pad, D), BF), ((n, D), BF), ((n, 128), F32)
    z = (lax.axis_index("seq") // 2).astype(jnp.int32).reshape(1)
    flat = tokens.reshape(rows * width, D)
    sent = call(
        functools.partial(pack_kernel, dims), [message] * groups, [], z, flat, cost=10**10
    )
    mod = modulation(timestep, mod_weight).reshape(4, D)
    own = [sent[0]] + [over_group(sent[m], m) for m in range(1, groups)]
    own[1], mod = lax.optimization_barrier((own[1], mod))
    other = [over_pair(x) for x in own]

    q, k, v = call(functools.partial(col_own_kernel, groups), [full] * 3, [], *own, mod, col_qkv)
    (h,) = call(
        functools.partial(col_attend_kernel, groups, dims), [full], [full] * 3,
        *own, *other, mod, col_qkv, col_out, q, k, v,
    )
    hy = over_bin(h, 2)
    hc = over_bin(h, 1)
    q, v, s, vc, sc = call(
        bin_own_kernel, [full, full, lanes, full, lanes], [], h, hc, mod, bin_qkv
    )
    hy, q = lax.optimization_barrier((hy, q))
    hd = over_bin(hy, 1)
    vy, sy = call(bin_kv_kernel, [full, lanes], [], hy, q, mod, bin_qkv)
    done = call(
        functools.partial(bin_attend_kernel, groups), [message] * groups, [full, lanes],
        hd, q, mod, bin_qkv, bin_out, h, v, s, vc, sc, vy, sy,
    )
    back = [done[0]] + [over_group(done[m], m) for m in range(1, groups)]
    (out,) = call(
        functools.partial(unpack_kernel, dims, groups), [((rows * width, D), BF)], [], z, *back
    )
    return out.reshape(tokens.shape)


def layer_norm(values, shift, scale):
    xf = values.astype(jnp.float32)
    mean = jnp.mean(xf, axis=-1, keepdims=True)
    var = jnp.mean((xf - mean) ** 2, axis=-1, keepdims=True)
    return ((xf - mean) * lax.rsqrt(var + 1e-06) * (1.0 + scale) + shift).astype(jnp.bfloat16)


def across_bins(query, key, value):
    scores = jnp.sum(
        query.astype(jnp.float32)[:, None] * key.astype(jnp.float32)[None], axis=-1
    ) * HD ** (-0.5)
    weights = jax.nn.softmax(scores, axis=1).astype(jnp.bfloat16)
    context = jnp.sum(
        weights.astype(jnp.float32)[..., None] * value.astype(jnp.float32)[None], axis=1
    )
    return context.astype(jnp.bfloat16)


def general_path(tokens, timestep, mod_weight, col_qkv, col_out, bin_qkv, bin_out):
    mod = modulation(timestep, mod_weight)
    shift1, scale1, shift2, scale2 = (mod[:D], mod[D : 2 * D], mod[2 * D : 3 * D], mod[3 * D :])
    rows_here = tokens.shape[1]
    width_all = tokens.shape[2]
    owners = lax.axis_size("seq")
    cols_each = width_all // owners
    normed1 = layer_norm(tokens, shift1, scale1)
    grouped = normed1.reshape(1, rows_here, owners, cols_each, D)
    query_weight = col_qkv[:, :D].reshape(D, HEADS, HD)
    key_weight = col_qkv[:, D : 2 * D].reshape(D, HEADS, HD)
    value_weight = col_qkv[:, 2 * D :].reshape(D, HEADS, HD)
    out_weight = col_out.reshape(HEADS, HD, D)
    piece = lax.all_to_all(grouped, "seq", split_axis=2, concat_axis=1, tiled=True)
    height = piece.shape[1]
    count = piece.shape[3]
    local = piece[0, :, 0]
    query = jnp.einsum(
        "iwc,chd->whid", local, query_weight, preferred_element_type=jnp.float32
    ).astype(jnp.bfloat16)
    key = jnp.einsum("iwc,chd->whid", local, key_weight, preferred_element_type=jnp.float32).astype(
        jnp.bfloat16
    )
    value = jnp.einsum(
        "iwc,chd->whid", local, value_weight, preferred_element_type=jnp.float32
    ).astype(jnp.bfloat16)
    scores = jnp.einsum("whid,whjd->whij", query, key, preferred_element_type=jnp.float32) * HD ** (
        -0.5
    )
    weights = jax.nn.softmax(scores, axis=-1).astype(jnp.bfloat16)
    context = jnp.einsum(
        "whij,whjd->whid", weights, value, preferred_element_type=jnp.float32
    ).astype(jnp.bfloat16)
    out = jnp.einsum(
        "whid,hde->iwe", context, out_weight, preferred_element_type=jnp.float32
    ).astype(jnp.bfloat16)
    attended = out.reshape(1, height, 1, count, D)
    back = lax.all_to_all(attended, "seq", split_axis=1, concat_axis=2, tiled=True)
    back = back.reshape(1, rows_here, width_all, D)
    hidden = (tokens.astype(jnp.float32) + back.astype(jnp.float32)).astype(jnp.bfloat16)
    normed2 = layer_norm(hidden, shift2, scale2)
    flat = normed2.reshape(-1, D)
    positions = flat.shape[0]
    every = lax.all_gather(normed2, "bin", axis=0, tiled=True)
    nbins = every.shape[0]
    every_flat = every.reshape(-1, D)
    query = jnp.dot(flat, bin_qkv[:, :D], preferred_element_type=jnp.float32).astype(jnp.bfloat16)
    keys_all = jnp.dot(
        every_flat, bin_qkv[:, D : 2 * D], preferred_element_type=jnp.float32
    ).astype(jnp.bfloat16)
    values_all = jnp.dot(
        every_flat, bin_qkv[:, 2 * D :], preferred_element_type=jnp.float32
    ).astype(jnp.bfloat16)
    context = across_bins(
        query.reshape(1, positions, HEADS, HD),
        keys_all.reshape(nbins, positions, HEADS, HD),
        values_all.reshape(nbins, positions, HEADS, HD),
    )
    projected = jnp.dot(context.reshape(-1, D), bin_out, preferred_element_type=jnp.float32)
    projected = projected.reshape(1, rows_here, width_all, D)
    return (hidden.astype(jnp.float32) + projected).astype(jnp.bfloat16)


def per_device(tokens, *rest):
    owners, width = lax.axis_size("seq"), tokens.shape[2]
    small = owners in (4, 8) and width % (owners // 2) == 0 and lax.axis_size("bin") == 4
    if small and tokens.shape[1] * width <= 256:
        return column_path(tokens, *rest)
    return general_path(tokens, *rest)


def solution(mesh):
    placed = (P("bin", "seq", None, None), P(), P(), P(), P(), P(), P())
    return jax.shard_map(
        per_device,
        mesh=mesh,
        in_specs=placed,
        out_specs=P("bin", "seq", None, None),
        check_vma=False,
    )
```

```python
import functools
import math

import jax
import jax.numpy as jnp
from jax import lax
from jax.experimental import pallas as pl
from jax.experimental.pallas import tpu as pltpu
from jax.sharding import PartitionSpec as P

D = 768
HEADS = 12
HD = 64
FREQ = 256
PAIR = 2 * HD
BF = jnp.bfloat16
F32 = jnp.float32


def modulation(timestep, mod_weight):
    half = FREQ // 2
    freqs = jnp.exp(-math.log(10000.0) * jnp.arange(half, dtype=jnp.float32) / half)
    angle = timestep.astype(jnp.float32)[0] * freqs
    emb = jax.nn.silu(jnp.concatenate([jnp.cos(angle), jnp.sin(angle)])).astype(jnp.bfloat16)
    return jnp.dot(emb[None, :], mod_weight, preferred_element_type=jnp.float32)[0]


def norm_rows(xf, mod_ref, which):
    shift = mod_ref[2 * which : 2 * which + 1, :]
    scale = mod_ref[2 * which + 1 : 2 * which + 2, :]
    mean = jnp.mean(xf, axis=-1, keepdims=True)
    cent = xf - mean
    var = jnp.mean(cent * cent, axis=-1, keepdims=True)
    return (cent * lax.rsqrt(var + 1e-06) * (1.0 + scale) + shift).astype(BF)


def stacked(refs):
    return jnp.concatenate([r[...].astype(F32) for r in refs], axis=0)


def project(normed, w_ref, which, out_ref, factor=None):
    y = jnp.dot(normed, w_ref[:, which * D : (which + 1) * D], preferred_element_type=F32)
    if factor is not None:
        y = y * factor
    out_ref[...] = y.astype(BF)


def divided(values, by, top):
    total = jnp.zeros_like(values)
    for step in range(by, top, by):
        total = total + (values >= step).astype(jnp.int32)
    return total


def message_rows(shape, row_dim, token_dim, rows, cols, width, owner):
    r = lax.broadcasted_iota(jnp.int32, shape, row_dim)
    t = lax.broadcasted_iota(jnp.int32, shape, token_dim)
    i = divided(r, cols, shape[row_dim])
    source = i * width + owner * cols + (r - i * cols)
    hit = (r < rows * cols) & (t == source)
    return jnp.where(hit, 1.0, 0.0).astype(BF)


def pack_kernel(dims, z_ref, tok_ref, *out_refs):
    rows, cols, width = dims
    x = tok_ref[...]
    for m, out in enumerate(out_refs):
        shape = (out.shape[0], x.shape[0])
        pick = message_rows(shape, 0, 1, rows, cols, width, z_ref[0] ^ m)
        out[...] = jnp.dot(pick, x, preferred_element_type=F32).astype(BF)


def unpack_kernel(dims, groups, z_ref, *refs):
    rows, cols, width = dims
    out = refs[groups]
    total = None
    for m in range(groups):
        shape = (out.shape[0], refs[m].shape[0])
        put = message_rows(shape, 1, 0, rows, cols, width, z_ref[0] ^ m)
        part = jnp.dot(put, refs[m][...], preferred_element_type=F32)
        total = part if total is None else total + part
    out[...] = total.astype(BF)


def column_bias(n, pad, keys, rows, cols):
    def column(shape, dim):
        r = lax.broadcasted_iota(jnp.int32, shape, dim)
        r = r - pad * divided(r, pad, shape[dim])
        return r, r - cols * divided(r, cols, pad)

    _, q_col = column((n, 1), 0)
    k_row, k_col = column((1, keys), 1)
    k_col = jnp.where(k_row < rows * cols, k_col, -1)
    bias = jnp.where(q_col == k_col, 0.0, -1e30).astype(F32)
    return jnp.concatenate([bias, bias], axis=0)


def head_pair(q):
    low = lax.broadcasted_iota(jnp.int32, q.shape, 1) < HD
    zero = jnp.zeros_like(q)
    return jnp.concatenate([jnp.where(low, q, zero), jnp.where(low, zero, q)], axis=0)


def unpaired(c):
    n = c.shape[0] // 2
    low = lax.broadcasted_iota(jnp.int32, (n, PAIR), 1) < HD
    return jnp.where(low, c[:n], c[n:])


def col_early_kernel(groups, dims, *refs):
    rows, cols, _ = dims
    count = 2 * groups - 1
    chunks, (mod_ref, w_ref, q_ref, m_ref, l_ref, acc_ref, k_ref, v_ref) = refs[:count], refs[count:]
    n, pad = q_ref.shape[0], chunks[0].shape[0]
    normed = norm_rows(stacked(chunks), mod_ref, 0)
    project(normed[:n], w_ref, 0, q_ref, HD**-0.5)
    project(normed, w_ref, 1, k_ref)
    project(normed, w_ref, 2, v_ref)
    bias = column_bias(n, pad, count * pad, rows, cols)
    for j in range(HEADS // 2):
        lanes = slice(j * PAIR, (j + 1) * PAIR)
        q = head_pair(q_ref[:, lanes])
        s = lax.dot_general(
            q, k_ref[:, lanes], (((1,), (1,)), ((), ())), preferred_element_type=F32
        ) + bias
        top = jnp.max(s, axis=-1, keepdims=True)
        e = jnp.exp(s - top)
        m_ref[:, j : j + 1] = top
        l_ref[:, j : j + 1] = jnp.sum(e, axis=-1, keepdims=True)
        acc_ref[:, lanes] = unpaired(
            jnp.dot(e.astype(BF), v_ref[:, lanes], preferred_element_type=F32)
        )


def col_late_kernel(groups, dims, *refs):
    rows, cols, _ = dims
    own, last = refs[:groups], refs[groups]
    mod_ref, w_ref, wo_ref, q_ref, m_ref, l_ref, acc_ref, h_ref, k_ref, v_ref, c_ref = refs[groups + 1 :]
    n, pad = q_ref.shape[0], last.shape[0]
    normed = norm_rows(last[...].astype(F32), mod_ref, 0)
    project(normed, w_ref, 1, k_ref)
    project(normed, w_ref, 2, v_ref)
    bias = column_bias(n, pad, pad, rows, cols)
    for j in range(HEADS // 2):
        lanes = slice(j * PAIR, (j + 1) * PAIR)
        q = head_pair(q_ref[:, lanes])
        s = lax.dot_general(
            q, k_ref[:, lanes], (((1,), (1,)), ((), ())), preferred_element_type=F32
        ) + bias
        before = m_ref[:, j : j + 1]
        top = jnp.maximum(before, jnp.max(s, axis=-1, keepdims=True))
        e = jnp.exp(s - top)
        fade = jnp.exp(before - top)
        total = fade * l_ref[:, j : j + 1] + jnp.sum(e, axis=-1, keepdims=True)
        weight = 1.0 / total
        new = jnp.dot(e.astype(BF), v_ref[:, lanes], preferred_element_type=F32) * weight
        wide = jnp.broadcast_to(fade * weight, new.shape)
        c_ref[:, lanes] = (acc_ref[:, lanes] * unpaired(wide) + unpaired(new)).astype(BF)
    a = jnp.dot(c_ref[...], wo_ref[...], preferred_element_type=F32).astype(BF)
    h_ref[...] = (stacked(own) + a.astype(F32)).astype(BF)


def head_lanes(shape, lane_dim):
    lane = lax.broadcasted_iota(jnp.int32, shape, lane_dim)
    head = lax.broadcasted_iota(jnp.int32, shape, 1 - lane_dim)
    return ((lane >= head * HD) & (lane < (head + 1) * HD)).astype(F32).astype(BF)


def key_scores(query, normed, w_ref, s_ref):
    k = jnp.dot(normed, w_ref[:, D : 2 * D], preferred_element_type=F32).astype(BF).astype(F32)
    s_ref[...] = jnp.dot(
        (query * k).astype(BF), head_lanes((D, 128), 0), preferred_element_type=F32
    )


def bin_own_kernel(h_ref, mod_ref, w_ref, q_ref, v_ref, s_ref):
    normed = norm_rows(h_ref[...].astype(F32), mod_ref, 1)
    project(normed, w_ref, 0, q_ref, HD**-0.5)
    key_scores(q_ref[...].astype(F32), normed, w_ref, s_ref)
    project(normed, w_ref, 2, v_ref)


def bin_kv_kernel(h_ref, q_ref, mod_ref, w_ref, v_ref, s_ref):
    normed = norm_rows(h_ref[...].astype(F32), mod_ref, 1)
    key_scores(q_ref[...].astype(F32), normed, w_ref, s_ref)
    project(normed, w_ref, 2, v_ref)


def bin_two_kernel(a_ref, b_ref, q_ref, mod_ref, w_ref, v_ref, s_ref):
    normed = norm_rows(stacked((a_ref, b_ref)), mod_ref, 1)
    q = q_ref[...].astype(F32)
    key_scores(jnp.concatenate([q, q], axis=0), normed, w_ref, s_ref)
    project(normed, w_ref, 2, v_ref)


def bin_attend_kernel(groups, hd_ref, q_ref, mod_ref, w_ref, wo_ref, h_ref, *refs):
    n = h_ref.shape[0]
    (v_ref, s_ref, v2_ref, s2_ref), refs = refs[:4], refs[4:]
    outs, (vd_ref, sd_ref) = refs[:groups], refs[groups:]
    bin_kv_kernel(hd_ref, q_ref, mod_ref, w_ref, vd_ref, sd_ref)
    halves = (slice(0, n), slice(n, 2 * n))
    scores = [s_ref[...], *(s2_ref[half, :] for half in halves), sd_ref[...]]
    values = [v_ref[...], *(v2_ref[half, :] for half in halves), vd_ref[...]]
    top = functools.reduce(jnp.maximum, scores)
    exps = [jnp.exp(s - top) for s in scores]
    scale = 1.0 / functools.reduce(jnp.add, exps)
    spread = head_lanes((128, D), 1)
    c = None
    for e, v in zip(exps, values):
        p = jnp.dot((e * scale).astype(BF), spread, preferred_element_type=F32)
        part = p * v.astype(F32)
        c = part if c is None else c + part
    out = jnp.dot(c.astype(BF), wo_ref[...], preferred_element_type=F32)
    out = h_ref[...].astype(F32) + out
    pad = outs[0].shape[0]
    for m, o in enumerate(outs):
        o[...] = out[m * pad : (m + 1) * pad].astype(BF)


def call(kernel, outs, scratch, *args, cost=10**6):
    def space(a):
        return pl.BlockSpec(memory_space=pltpu.SMEM if a.dtype == jnp.int32 else pltpu.VMEM)

    return pl.pallas_call(
        kernel,
        out_shape=[jax.ShapeDtypeStruct(*o) for o in outs],
        in_specs=[space(a) for a in args],
        out_specs=[pl.BlockSpec(memory_space=pltpu.VMEM)] * len(outs),
        scratch_shapes=[pltpu.VMEM(*s) for s in scratch],
        compiler_params=pltpu.CompilerParams(vmem_limit_bytes=24 * 1024 * 1024),
        cost_estimate=pl.CostEstimate(flops=cost, bytes_accessed=cost // 1000, transcendentals=0),
    )(*args)


def column_path(tokens, timestep, mod_weight, col_qkv, col_out, bin_qkv, bin_out):
    rows, width = tokens.shape[1], tokens.shape[2]
    owners = lax.axis_size("seq")
    groups = owners // 2
    cols = width // groups
    dims = (rows, cols, width)
    pad = -(-rows * cols // 8) * 8
    n = groups * pad

    def over_group(x, m):
        return lax.ppermute(x, "seq", [(i, i ^ (2 * m)) for i in range(owners)])

    def over_pair(x):
        return lax.ppermute(x, "seq", [(i, i ^ 1) for i in range(owners)])

    def over_bin(x, m):
        return lax.ppermute(x, "bin", [(i, i ^ m) for i in range(4)])

    message, full, lanes = ((pad, D), BF), ((n, D), BF), ((n, 128), F32)
    z = (lax.axis_index("seq") // 2).astype(jnp.int32).reshape(1)
    flat = tokens.reshape(rows * width, D)
    sent = call(
        functools.partial(pack_kernel, dims), [message] * groups, [], z, flat, cost=10**10
    )
    mod = modulation(timestep, mod_weight).reshape(4, D)
    own = [sent[0]] + [over_group(sent[m], m) for m in range(1, groups)]
    own[1], mod = lax.optimization_barrier((own[1], mod))
    other = [over_pair(x) for x in own]

    chunks = [*own, *other[:-1]]
    kv = ((len(chunks) * pad, D), BF)
    q, m, l, acc = call(
        functools.partial(col_early_kernel, groups, dims),
        [full, ((2 * n, 128), F32), ((2 * n, 128), F32), ((n, D), F32)], [kv, kv],
        *chunks, mod, col_qkv,
    )
    (h,) = call(
        functools.partial(col_late_kernel, groups, dims), [full], [message, message, full],
        *own, other[-1], mod, col_qkv, col_out, q, m, l, acc,
    )
    hy = over_bin(h, 2)
    hc = over_bin(h, 1)
    q, v, s = call(bin_own_kernel, [full, full, lanes], [], h, mod, bin_qkv)
    hy, hc, q = lax.optimization_barrier((hy, hc, q))
    hd = over_bin(hy, 1)
    v2, s2 = call(
        bin_two_kernel, [((2 * n, D), BF), ((2 * n, 128), F32)], [], hc, hy, q, mod, bin_qkv
    )
    done = call(
        functools.partial(bin_attend_kernel, groups), [message] * groups, [full, lanes],
        hd, q, mod, bin_qkv, bin_out, h, v, s, v2, s2,
    )
    back = [done[0]] + [over_group(done[m], m) for m in range(1, groups)]
    (out,) = call(
        functools.partial(unpack_kernel, dims, groups), [((rows * width, D), BF)], [], z, *back
    )
    return out.reshape(tokens.shape)


def layer_norm(values, shift, scale):
    xf = values.astype(jnp.float32)
    mean = jnp.mean(xf, axis=-1, keepdims=True)
    var = jnp.mean((xf - mean) ** 2, axis=-1, keepdims=True)
    return ((xf - mean) * lax.rsqrt(var + 1e-06) * (1.0 + scale) + shift).astype(jnp.bfloat16)


def across_bins(query, key, value):
    scores = jnp.sum(
        query.astype(jnp.float32)[:, None] * key.astype(jnp.float32)[None], axis=-1
    ) * HD ** (-0.5)
    weights = jax.nn.softmax(scores, axis=1).astype(jnp.bfloat16)
    context = jnp.sum(
        weights.astype(jnp.float32)[..., None] * value.astype(jnp.float32)[None], axis=1
    )
    return context.astype(jnp.bfloat16)


def general_path(tokens, timestep, mod_weight, col_qkv, col_out, bin_qkv, bin_out):
    mod = modulation(timestep, mod_weight)
    shift1, scale1, shift2, scale2 = (mod[:D], mod[D : 2 * D], mod[2 * D : 3 * D], mod[3 * D :])
    rows_here = tokens.shape[1]
    width_all = tokens.shape[2]
    owners = lax.axis_size("seq")
    cols_each = width_all // owners
    normed1 = layer_norm(tokens, shift1, scale1)
    grouped = normed1.reshape(1, rows_here, owners, cols_each, D)
    query_weight = col_qkv[:, :D].reshape(D, HEADS, HD)
    key_weight = col_qkv[:, D : 2 * D].reshape(D, HEADS, HD)
    value_weight = col_qkv[:, 2 * D :].reshape(D, HEADS, HD)
    out_weight = col_out.reshape(HEADS, HD, D)
    piece = lax.all_to_all(grouped, "seq", split_axis=2, concat_axis=1, tiled=True)
    height = piece.shape[1]
    count = piece.shape[3]
    local = piece[0, :, 0]
    query = jnp.einsum(
        "iwc,chd->whid", local, query_weight, preferred_element_type=jnp.float32
    ).astype(jnp.bfloat16)
    key = jnp.einsum("iwc,chd->whid", local, key_weight, preferred_element_type=jnp.float32).astype(
        jnp.bfloat16
    )
    value = jnp.einsum(
        "iwc,chd->whid", local, value_weight, preferred_element_type=jnp.float32
    ).astype(jnp.bfloat16)
    scores = jnp.einsum("whid,whjd->whij", query, key, preferred_element_type=jnp.float32) * HD ** (
        -0.5
    )
    weights = jax.nn.softmax(scores, axis=-1).astype(jnp.bfloat16)
    context = jnp.einsum(
        "whij,whjd->whid", weights, value, preferred_element_type=jnp.float32
    ).astype(jnp.bfloat16)
    out = jnp.einsum(
        "whid,hde->iwe", context, out_weight, preferred_element_type=jnp.float32
    ).astype(jnp.bfloat16)
    attended = out.reshape(1, height, 1, count, D)
    back = lax.all_to_all(attended, "seq", split_axis=1, concat_axis=2, tiled=True)
    back = back.reshape(1, rows_here, width_all, D)
    hidden = (tokens.astype(jnp.float32) + back.astype(jnp.float32)).astype(jnp.bfloat16)
    normed2 = layer_norm(hidden, shift2, scale2)
    flat = normed2.reshape(-1, D)
    positions = flat.shape[0]
    every = lax.all_gather(normed2, "bin", axis=0, tiled=True)
    nbins = every.shape[0]
    every_flat = every.reshape(-1, D)
    query = jnp.dot(flat, bin_qkv[:, :D], preferred_element_type=jnp.float32).astype(jnp.bfloat16)
    keys_all = jnp.dot(
        every_flat, bin_qkv[:, D : 2 * D], preferred_element_type=jnp.float32
    ).astype(jnp.bfloat16)
    values_all = jnp.dot(
        every_flat, bin_qkv[:, 2 * D :], preferred_element_type=jnp.float32
    ).astype(jnp.bfloat16)
    context = across_bins(
        query.reshape(1, positions, HEADS, HD),
        keys_all.reshape(nbins, positions, HEADS, HD),
        values_all.reshape(nbins, positions, HEADS, HD),
    )
    projected = jnp.dot(context.reshape(-1, D), bin_out, preferred_element_type=jnp.float32)
    projected = projected.reshape(1, rows_here, width_all, D)
    return (hidden.astype(jnp.float32) + projected).astype(jnp.bfloat16)


def per_device(tokens, *rest):
    owners, width = lax.axis_size("seq"), tokens.shape[2]
    small = owners in (4, 8) and width % (owners // 2) == 0 and lax.axis_size("bin") == 4
    if small and tokens.shape[1] * width <= 256:
        return column_path(tokens, *rest)
    return general_path(tokens, *rest)


def solution(mesh):
    placed = (P("bin", "seq", None, None), P(), P(), P(), P(), P(), P())
    return jax.shard_map(
        per_device,
        mesh=mesh,
        in_specs=placed,
        out_specs=P("bin", "seq", None, None),
        check_vma=False,
    )
```

```python
import functools
import math

import jax
import jax.numpy as jnp
from jax import lax
from jax.experimental import pallas as pl
from jax.experimental.pallas import tpu as pltpu
from jax.sharding import PartitionSpec as P

D = 768
HEADS = 12
HD = 64
FREQ = 256
PAIR = 2 * HD
BF = jnp.bfloat16
F32 = jnp.float32


def modulation(timestep, mod_weight):
    half = FREQ // 2
    freqs = jnp.exp(-math.log(10000.0) * jnp.arange(half, dtype=jnp.float32) / half)
    angle = timestep.astype(jnp.float32)[0] * freqs
    emb = jax.nn.silu(jnp.concatenate([jnp.cos(angle), jnp.sin(angle)])).astype(jnp.bfloat16)
    return jnp.dot(emb[None, :], mod_weight, preferred_element_type=jnp.float32)[0]


def norm_rows(xf, mod_ref, which):
    shift = mod_ref[2 * which : 2 * which + 1, :]
    scale = mod_ref[2 * which + 1 : 2 * which + 2, :]
    mean = jnp.mean(xf, axis=-1, keepdims=True)
    cent = xf - mean
    var = jnp.mean(cent * cent, axis=-1, keepdims=True)
    return (cent * lax.rsqrt(var + 1e-06) * (1.0 + scale) + shift).astype(BF)


def stacked(refs):
    return jnp.concatenate([r[...].astype(F32) for r in refs], axis=0)


def project(normed, w_ref, which, out_ref, factor=None):
    y = jnp.dot(normed, w_ref[:, which * D : (which + 1) * D], preferred_element_type=F32)
    if factor is not None:
        y = y * factor
    out_ref[...] = y.astype(BF)


def divided(values, by, top):
    total = jnp.zeros_like(values)
    for step in range(by, top, by):
        total = total + (values >= step).astype(jnp.int32)
    return total


def message_rows(shape, row_dim, token_dim, rows, cols, width, owner):
    r = lax.broadcasted_iota(jnp.int32, shape, row_dim)
    t = lax.broadcasted_iota(jnp.int32, shape, token_dim)
    i = divided(r, cols, shape[row_dim])
    source = i * width + owner * cols + (r - i * cols)
    hit = (r < rows * cols) & (t == source)
    return jnp.where(hit, 1.0, 0.0).astype(BF)


def pack_kernel(dims, z_ref, tok_ref, *out_refs):
    rows, cols, width = dims
    x = tok_ref[...]
    for m, out in enumerate(out_refs):
        shape = (out.shape[0], x.shape[0])
        pick = message_rows(shape, 0, 1, rows, cols, width, z_ref[0] ^ m)
        out[...] = jnp.dot(pick, x, preferred_element_type=F32).astype(BF)


def unpack_kernel(dims, groups, z_ref, *refs):
    rows, cols, width = dims
    out = refs[groups]
    total = None
    for m in range(groups):
        shape = (out.shape[0], refs[m].shape[0])
        put = message_rows(shape, 1, 0, rows, cols, width, z_ref[0] ^ m)
        part = jnp.dot(put, refs[m][...], preferred_element_type=F32)
        total = part if total is None else total + part
    out[...] = total.astype(BF)


def column_bias(n, pad, keys, rows, cols):
    def column(shape, dim):
        r = lax.broadcasted_iota(jnp.int32, shape, dim)
        r = r - pad * divided(r, pad, shape[dim])
        return r, r - cols * divided(r, cols, pad)

    _, q_col = column((n, 1), 0)
    k_row, k_col = column((1, keys), 1)
    k_col = jnp.where(k_row < rows * cols, k_col, -1)
    bias = jnp.where(q_col == k_col, 0.0, -1e30).astype(F32)
    return jnp.concatenate([bias, bias], axis=0)


def head_pair(q):
    low = lax.broadcasted_iota(jnp.int32, q.shape, 1) < HD
    zero = jnp.zeros_like(q)
    return jnp.concatenate([jnp.where(low, q, zero), jnp.where(low, zero, q)], axis=0)


def unpaired(c):
    n = c.shape[0] // 2
    low = lax.broadcasted_iota(jnp.int32, (n, PAIR), 1) < HD
    return jnp.where(low, c[:n], c[n:])


def col_own_kernel(groups, *refs):
    own, (mod_ref, w_ref, q_ref, k_ref, v_ref) = refs[:groups], refs[groups:]
    normed = norm_rows(stacked(own), mod_ref, 0)
    project(normed, w_ref, 0, q_ref, HD**-0.5)
    project(normed, w_ref, 1, k_ref)
    project(normed, w_ref, 2, v_ref)


def col_attend_kernel(groups, dims, *refs):
    rows, cols, _ = dims
    own, other = refs[:groups], refs[groups : 2 * groups]
    mod_ref, w_ref, wo_ref, q_ref, k_ref, v_ref, h_ref, k2_ref, v2_ref, c_ref = refs[2 * groups :]
    n, pad = q_ref.shape[0], own[0].shape[0]
    normed = norm_rows(stacked(other), mod_ref, 0)
    project(normed, w_ref, 1, k2_ref)
    project(normed, w_ref, 2, v2_ref)
    bias = column_bias(n, pad, 2 * n, rows, cols)
    ones = jnp.ones((2 * n, PAIR), BF)
    for j in range(HEADS // 2):
        lanes = slice(j * PAIR, (j + 1) * PAIR)
        q = head_pair(q_ref[:, lanes])
        k = jnp.concatenate([k_ref[:, lanes], k2_ref[:, lanes]], axis=0)
        v = jnp.concatenate([v_ref[:, lanes], v2_ref[:, lanes]], axis=0)
        s = lax.dot_general(q, k, (((1,), (1,)), ((), ())), preferred_element_type=F32) + bias
        e = jnp.exp(s - jnp.max(s, axis=-1, keepdims=True)).astype(BF)
        c = jnp.dot(e, jnp.concatenate([v, ones], axis=1), preferred_element_type=F32)
        c_ref[:, lanes] = (unpaired(c[:, :PAIR]) / unpaired(c[:, PAIR:])).astype(BF)
    a = jnp.dot(c_ref[...], wo_ref[...], preferred_element_type=F32).astype(BF)
    h_ref[...] = (stacked(own) + a.astype(F32)).astype(BF)


def head_lanes(shape, lane_dim):
    lane = lax.broadcasted_iota(jnp.int32, shape, lane_dim)
    head = lax.broadcasted_iota(jnp.int32, shape, 1 - lane_dim)
    return ((lane >= head * HD) & (lane < (head + 1) * HD)).astype(F32).astype(BF)


def key_scores(query, normed, w_ref, s_ref):
    k = jnp.dot(normed, w_ref[:, D : 2 * D], preferred_element_type=F32).astype(BF).astype(F32)
    s_ref[...] = jnp.dot(
        (query * k).astype(BF), head_lanes((D, 128), 0), preferred_element_type=F32
    )


def bin_own_kernel(h_ref, mod_ref, w_ref, q_ref, v_ref, s_ref):
    normed = norm_rows(h_ref[...].astype(F32), mod_ref, 1)
    project(normed, w_ref, 0, q_ref, HD**-0.5)
    key_scores(q_ref[...].astype(F32), normed, w_ref, s_ref)
    project(normed, w_ref, 2, v_ref)


def bin_kv_kernel(h_ref, q_ref, mod_ref, w_ref, v_ref, s_ref):
    normed = norm_rows(h_ref[...].astype(F32), mod_ref, 1)
    key_scores(q_ref[...].astype(F32), normed, w_ref, s_ref)
    project(normed, w_ref, 2, v_ref)


def bin_two_kernel(a_ref, b_ref, q_ref, mod_ref, w_ref, v_ref, s_ref):
    normed = norm_rows(stacked((a_ref, b_ref)), mod_ref, 1)
    q = q_ref[...].astype(F32)
    key_scores(jnp.concatenate([q, q], axis=0), normed, w_ref, s_ref)
    project(normed, w_ref, 2, v_ref)


def bin_attend_kernel(groups, hd_ref, q_ref, mod_ref, w_ref, wo_ref, h_ref, *refs):
    n = h_ref.shape[0]
    (v_ref, s_ref, v2_ref, s2_ref), refs = refs[:4], refs[4:]
    outs, (vd_ref, sd_ref) = refs[:groups], refs[groups:]
    bin_kv_kernel(hd_ref, q_ref, mod_ref, w_ref, vd_ref, sd_ref)
    halves = (slice(0, n), slice(n, 2 * n))
    scores = [s_ref[...], *(s2_ref[half, :] for half in halves), sd_ref[...]]
    values = [v_ref[...], *(v2_ref[half, :] for half in halves), vd_ref[...]]
    top = functools.reduce(jnp.maximum, scores)
    exps = [jnp.exp(s - top) for s in scores]
    scale = 1.0 / functools.reduce(jnp.add, exps)
    spread = head_lanes((128, D), 1)
    c = None
    for e, v in zip(exps, values):
        p = jnp.dot((e * scale).astype(BF), spread, preferred_element_type=F32)
        part = p * v.astype(F32)
        c = part if c is None else c + part
    out = jnp.dot(c.astype(BF), wo_ref[...], preferred_element_type=F32)
    out = h_ref[...].astype(F32) + out
    pad = outs[0].shape[0]
    for m, o in enumerate(outs):
        o[...] = out[m * pad : (m + 1) * pad].astype(BF)


def call(kernel, outs, scratch, *args, cost=10**6):
    def space(a):
        return pl.BlockSpec(memory_space=pltpu.SMEM if a.dtype == jnp.int32 else pltpu.VMEM)

    return pl.pallas_call(
        kernel,
        out_shape=[jax.ShapeDtypeStruct(*o) for o in outs],
        in_specs=[space(a) for a in args],
        out_specs=[pl.BlockSpec(memory_space=pltpu.VMEM)] * len(outs),
        scratch_shapes=[pltpu.VMEM(*s) for s in scratch],
        compiler_params=pltpu.CompilerParams(vmem_limit_bytes=24 * 1024 * 1024),
        cost_estimate=pl.CostEstimate(flops=cost, bytes_accessed=cost // 1000, transcendentals=0),
    )(*args)


def column_path(tokens, timestep, mod_weight, col_qkv, col_out, bin_qkv, bin_out):
    rows, width = tokens.shape[1], tokens.shape[2]
    owners = lax.axis_size("seq")
    groups = owners // 2
    cols = width // groups
    dims = (rows, cols, width)
    pad = -(-rows * cols // 8) * 8
    n = groups * pad

    def over_group(x, m):
        return lax.ppermute(x, "seq", [(i, i ^ (2 * m)) for i in range(owners)])

    def over_pair(x):
        return lax.ppermute(x, "seq", [(i, i ^ 1) for i in range(owners)])

    def over_bin(x, m):
        return lax.ppermute(x, "bin", [(i, i ^ m) for i in range(4)])

    message, full, lanes = ((pad, D), BF), ((n, D), BF), ((n, 128), F32)
    z = (lax.axis_index("seq") // 2).astype(jnp.int32).reshape(1)
    flat = tokens.reshape(rows * width, D)
    sent = call(
        functools.partial(pack_kernel, dims), [message] * groups, [], z, flat, cost=10**10
    )
    mod = modulation(timestep, mod_weight).reshape(4, D)
    own = [sent[0]] + [over_group(sent[m], m) for m in range(1, groups)]
    own[1], mod = lax.optimization_barrier((own[1], mod))
    other = [over_pair(x) for x in own]

    q, k, v = call(functools.partial(col_own_kernel, groups), [full] * 3, [], *own, mod, col_qkv)
    (h,) = call(
        functools.partial(col_attend_kernel, groups, dims), [full], [full] * 3,
        *own, *other, mod, col_qkv, col_out, q, k, v,
    )
    hy = over_bin(h, 2)
    hc = over_bin(h, 1)
    q, v, s = call(bin_own_kernel, [full, full, lanes], [], h, mod, bin_qkv)
    hy, hc, q = lax.optimization_barrier((hy, hc, q))
    hd = over_bin(hy, 1)
    v2, s2 = call(
        bin_two_kernel, [((2 * n, D), BF), ((2 * n, 128), F32)], [], hc, hy, q, mod, bin_qkv
    )
    done = call(
        functools.partial(bin_attend_kernel, groups), [message] * groups, [full, lanes],
        hd, q, mod, bin_qkv, bin_out, h, v, s, v2, s2,
    )
    back = [done[0]] + [over_group(done[m], m) for m in range(1, groups)]
    (out,) = call(
        functools.partial(unpack_kernel, dims, groups), [((rows * width, D), BF)], [], z, *back
    )
    return out.reshape(tokens.shape)


def layer_norm(values, shift, scale):
    xf = values.astype(jnp.float32)
    mean = jnp.mean(xf, axis=-1, keepdims=True)
    var = jnp.mean((xf - mean) ** 2, axis=-1, keepdims=True)
    return ((xf - mean) * lax.rsqrt(var + 1e-06) * (1.0 + scale) + shift).astype(jnp.bfloat16)


def across_bins(query, key, value):
    scores = jnp.sum(
        query.astype(jnp.float32)[:, None] * key.astype(jnp.float32)[None], axis=-1
    ) * HD ** (-0.5)
    weights = jax.nn.softmax(scores, axis=1).astype(jnp.bfloat16)
    context = jnp.sum(
        weights.astype(jnp.float32)[..., None] * value.astype(jnp.float32)[None], axis=1
    )
    return context.astype(jnp.bfloat16)


def general_path(tokens, timestep, mod_weight, col_qkv, col_out, bin_qkv, bin_out):
    mod = modulation(timestep, mod_weight)
    shift1, scale1, shift2, scale2 = (mod[:D], mod[D : 2 * D], mod[2 * D : 3 * D], mod[3 * D :])
    rows_here = tokens.shape[1]
    width_all = tokens.shape[2]
    owners = lax.axis_size("seq")
    cols_each = width_all // owners
    normed1 = layer_norm(tokens, shift1, scale1)
    grouped = normed1.reshape(1, rows_here, owners, cols_each, D)
    query_weight = col_qkv[:, :D].reshape(D, HEADS, HD)
    key_weight = col_qkv[:, D : 2 * D].reshape(D, HEADS, HD)
    value_weight = col_qkv[:, 2 * D :].reshape(D, HEADS, HD)
    out_weight = col_out.reshape(HEADS, HD, D)
    piece = lax.all_to_all(grouped, "seq", split_axis=2, concat_axis=1, tiled=True)
    height = piece.shape[1]
    count = piece.shape[3]
    local = piece[0, :, 0]
    query = jnp.einsum(
        "iwc,chd->whid", local, query_weight, preferred_element_type=jnp.float32
    ).astype(jnp.bfloat16)
    key = jnp.einsum("iwc,chd->whid", local, key_weight, preferred_element_type=jnp.float32).astype(
        jnp.bfloat16
    )
    value = jnp.einsum(
        "iwc,chd->whid", local, value_weight, preferred_element_type=jnp.float32
    ).astype(jnp.bfloat16)
    scores = jnp.einsum("whid,whjd->whij", query, key, preferred_element_type=jnp.float32) * HD ** (
        -0.5
    )
    weights = jax.nn.softmax(scores, axis=-1).astype(jnp.bfloat16)
    context = jnp.einsum(
        "whij,whjd->whid", weights, value, preferred_element_type=jnp.float32
    ).astype(jnp.bfloat16)
    out = jnp.einsum(
        "whid,hde->iwe", context, out_weight, preferred_element_type=jnp.float32
    ).astype(jnp.bfloat16)
    attended = out.reshape(1, height, 1, count, D)
    back = lax.all_to_all(attended, "seq", split_axis=1, concat_axis=2, tiled=True)
    back = back.reshape(1, rows_here, width_all, D)
    hidden = (tokens.astype(jnp.float32) + back.astype(jnp.float32)).astype(jnp.bfloat16)
    normed2 = layer_norm(hidden, shift2, scale2)
    flat = normed2.reshape(-1, D)
    positions = flat.shape[0]
    every = lax.all_gather(normed2, "bin", axis=0, tiled=True)
    nbins = every.shape[0]
    every_flat = every.reshape(-1, D)
    query = jnp.dot(flat, bin_qkv[:, :D], preferred_element_type=jnp.float32).astype(jnp.bfloat16)
    keys_all = jnp.dot(
        every_flat, bin_qkv[:, D : 2 * D], preferred_element_type=jnp.float32
    ).astype(jnp.bfloat16)
    values_all = jnp.dot(
        every_flat, bin_qkv[:, 2 * D :], preferred_element_type=jnp.float32
    ).astype(jnp.bfloat16)
    context = across_bins(
        query.reshape(1, positions, HEADS, HD),
        keys_all.reshape(nbins, positions, HEADS, HD),
        values_all.reshape(nbins, positions, HEADS, HD),
    )
    projected = jnp.dot(context.reshape(-1, D), bin_out, preferred_element_type=jnp.float32)
    projected = projected.reshape(1, rows_here, width_all, D)
    return (hidden.astype(jnp.float32) + projected).astype(jnp.bfloat16)


def per_device(tokens, *rest):
    owners, width = lax.axis_size("seq"), tokens.shape[2]
    small = owners in (4, 8) and width % (owners // 2) == 0 and lax.axis_size("bin") == 4
    if small and tokens.shape[1] * width <= 256:
        return column_path(tokens, *rest)
    return general_path(tokens, *rest)


def solution(mesh):
    placed = (P("bin", "seq", None, None), P(), P(), P(), P(), P(), P())
    return jax.shard_map(
        per_device,
        mesh=mesh,
        in_specs=placed,
        out_specs=P("bin", "seq", None, None),
        check_vma=False,
    )
```

```python
import functools
import math

import jax
import jax.numpy as jnp
from jax import lax
from jax.experimental import pallas as pl
from jax.experimental.pallas import tpu as pltpu
from jax.sharding import PartitionSpec as P

D = 768
HEADS = 12
HD = 64
FREQ = 256
PAIR = 2 * HD
BF = jnp.bfloat16
F32 = jnp.float32


def modulation(timestep, mod_weight):
    half = FREQ // 2
    freqs = jnp.exp(-math.log(10000.0) * jnp.arange(half, dtype=jnp.float32) / half)
    angle = timestep.astype(jnp.float32)[0] * freqs
    emb = jax.nn.silu(jnp.concatenate([jnp.cos(angle), jnp.sin(angle)])).astype(jnp.bfloat16)
    return jnp.dot(emb[None, :], mod_weight, preferred_element_type=jnp.float32)[0]


def norm_rows(xf, mod_ref, which):
    shift = mod_ref[2 * which : 2 * which + 1, :]
    scale = mod_ref[2 * which + 1 : 2 * which + 2, :]
    mean = jnp.mean(xf, axis=-1, keepdims=True)
    cent = xf - mean
    var = jnp.mean(cent * cent, axis=-1, keepdims=True)
    return (cent * lax.rsqrt(var + 1e-06) * (1.0 + scale) + shift).astype(BF)


def stacked(refs):
    return jnp.concatenate([r[...].astype(F32) for r in refs], axis=0)


def project(normed, w_ref, which, out_ref, factor=None):
    y = jnp.dot(normed, w_ref[:, which * D : (which + 1) * D], preferred_element_type=F32)
    if factor is not None:
        y = y * factor
    out_ref[...] = y.astype(BF)


def divided(values, by, top):
    total = jnp.zeros_like(values)
    for step in range(by, top, by):
        total = total + (values >= step).astype(jnp.int32)
    return total


def message_rows(shape, row_dim, token_dim, rows, cols, width, owner):
    r = lax.broadcasted_iota(jnp.int32, shape, row_dim)
    t = lax.broadcasted_iota(jnp.int32, shape, token_dim)
    i = divided(r, cols, shape[row_dim])
    source = i * width + owner * cols + (r - i * cols)
    hit = (r < rows * cols) & (t == source)
    return jnp.where(hit, 1.0, 0.0).astype(BF)


def pack_kernel(dims, z_ref, tok_ref, *out_refs):
    rows, cols, width = dims
    x = tok_ref[...]
    for m, out in enumerate(out_refs):
        shape = (out.shape[0], x.shape[0])
        pick = message_rows(shape, 0, 1, rows, cols, width, z_ref[0] ^ m)
        out[...] = jnp.dot(pick, x, preferred_element_type=F32).astype(BF)


def unpack_kernel(dims, groups, z_ref, *refs):
    rows, cols, width = dims
    out = refs[groups]
    total = None
    for m in range(groups):
        shape = (out.shape[0], refs[m].shape[0])
        put = message_rows(shape, 1, 0, rows, cols, width, z_ref[0] ^ m)
        part = jnp.dot(put, refs[m][...], preferred_element_type=F32)
        total = part if total is None else total + part
    out[...] = total.astype(BF)


def grouped_rows(dims, groups, pad, shape, row_dim):
    rows, cols, _ = dims
    flat = (shape[0], 1) if row_dim == 0 else (1, shape[1])
    r = lax.broadcasted_iota(jnp.int32, flat, row_dim)
    part, here = groups * rows * 2, rows * 2
    g = divided(r, part, shape[row_dim])
    r = r - g * part
    m = divided(r, here, part)
    r = r - m * here
    i = divided(r, 2, here)
    source = m * pad + i * cols + 2 * g + (r - 2 * i)
    hit = source == lax.broadcasted_iota(jnp.int32, shape, 1 - row_dim)
    return jnp.where(hit, 1.0, 0.0).astype(BF)


def column_marks(n, keys):
    def odd(count):
        return lax.broadcasted_iota(jnp.int32, (count, PAIR), 0) & 1

    lane = lax.broadcasted_iota(jnp.int32, (n, PAIR), 1)
    query = jnp.where(lane == odd(n), 1.0, 0.0).astype(BF)
    lane = lax.broadcasted_iota(jnp.int32, (keys, PAIR), 1)
    return query, jnp.where(lane == odd(keys), 0.0, -(2.0**100)).astype(BF)


def head_pair(q):
    low = lax.broadcasted_iota(jnp.int32, q.shape, 1) < HD
    zero = jnp.zeros_like(q)
    return jnp.concatenate([jnp.where(low, q, zero), jnp.where(low, zero, q)], axis=0)


def unpaired(c):
    n = c.shape[0] // 2
    low = lax.broadcasted_iota(jnp.int32, (n, PAIR), 1) < HD
    return jnp.where(low, c[:n], c[n:])


def regrouped(refs, dims):
    pad = refs[0].shape[0]
    n = len(refs) * dims[0] * dims[1]
    pick = grouped_rows(dims, len(refs), pad, (n, len(refs) * pad), 0)
    return jnp.dot(pick, stacked(refs).astype(BF), preferred_element_type=F32)


def col_own_kernel(groups, dims, *refs):
    own, (mod_ref, w_ref, t_ref, q_ref, k_ref, v_ref) = refs[:groups], refs[groups:]
    rows = regrouped(own, dims)
    t_ref[...] = rows.astype(BF)
    normed = norm_rows(rows, mod_ref, 0)
    project(normed, w_ref, 0, q_ref, HD**-0.5 * math.log2(math.e))
    project(normed, w_ref, 1, k_ref)
    project(normed, w_ref, 2, v_ref)


def col_attend_kernel(groups, dims, *refs):
    other = refs[:groups]
    mod_ref, w_ref, wo_ref, t_ref, q_ref, k_ref, v_ref, h_ref, *refs = refs[groups:]
    low_ref, high_ref, k2_ref, v2_ref, c_ref = refs
    normed = norm_rows(regrouped(other, dims), mod_ref, 0)
    project(normed, w_ref, 1, k2_ref)
    project(normed, w_ref, 2, v2_ref)
    part = groups * dims[0] * 2
    q_mark, k_mark = column_marks(2 * part, 2 * part)
    ones = jnp.ones((2 * part, PAIR), BF)
    for g in range(dims[1] // 2):
        here = slice(g * part, (g + 1) * part)
        for j in range(HEADS // 2):
            lanes = slice(j * PAIR, (j + 1) * PAIR)
            q = jnp.concatenate([head_pair(q_ref[here, lanes]), q_mark], axis=1)
            k = jnp.concatenate([k_ref[here, lanes], k2_ref[here, lanes]], axis=0)
            v = jnp.concatenate([v_ref[here, lanes], v2_ref[here, lanes]], axis=0)
            k = jnp.concatenate([k, k_mark], axis=1)
            s = lax.dot_general(q, k, (((1,), (1,)), ((), ())), preferred_element_type=F32)
            e = jnp.exp2((s - jnp.max(s, axis=-1, keepdims=True)).astype(BF))
            c = jnp.dot(e, jnp.concatenate([v, ones], axis=1), preferred_element_type=F32)
            c_ref[here, lanes] = (unpaired(c[:, :PAIR]) / unpaired(c[:, PAIR:])).astype(BF)
    a = jnp.dot(c_ref[...], wo_ref[...], preferred_element_type=F32).astype(BF)
    h = t_ref[...].astype(F32) + a.astype(F32)
    h_ref[...] = h.astype(BF)
    low_ref[...] = h[: low_ref.shape[0]].astype(BF)
    high_ref[...] = h[low_ref.shape[0] :].astype(BF)


def head_lanes(shape, lane_dim):
    lane = lax.broadcasted_iota(jnp.int32, shape, lane_dim)
    head = lax.broadcasted_iota(jnp.int32, shape, 1 - lane_dim)
    return ((lane >= head * HD) & (lane < (head + 1) * HD)).astype(F32).astype(BF)


def key_scores(query, normed, w_ref, s_ref):
    k = jnp.dot(normed, w_ref[:, D : 2 * D], preferred_element_type=F32).astype(BF).astype(F32)
    s_ref[...] = jnp.dot(
        (query * k).astype(BF), head_lanes((D, 128), 0), preferred_element_type=F32
    )


def bin_own_kernel(h_ref, low_ref, high_ref, mod_ref, w_ref, q_ref, v_ref, s_ref):
    n = h_ref.shape[0]
    normed = norm_rows(stacked((h_ref, low_ref, high_ref)), mod_ref, 1)
    project(normed[:n], w_ref, 0, q_ref, HD**-0.5)
    q = q_ref[...].astype(F32)
    key_scores(jnp.concatenate([q, q], axis=0), normed, w_ref, s_ref)
    project(normed, w_ref, 2, v_ref)


def bin_kv_kernel(h_ref, q_ref, mod_ref, w_ref, v_ref, s_ref):
    normed = norm_rows(h_ref[...].astype(F32), mod_ref, 1)
    key_scores(q_ref[...].astype(F32), normed, w_ref, s_ref)
    project(normed, w_ref, 2, v_ref)


def bin_attend_kernel(groups, dims, hd_ref, q_ref, mod_ref, w_ref, wo_ref, h_ref, *refs):
    n = h_ref.shape[0]
    (v_ref, s_ref, v2_ref, s2_ref), refs = refs[:4], refs[4:]
    outs, (vd_ref, sd_ref) = refs[:groups], refs[groups:]
    bin_kv_kernel(hd_ref, q_ref, mod_ref, w_ref, vd_ref, sd_ref)
    halves = (slice(0, n), slice(n, 2 * n))
    scores = [*(s_ref[half, :] for half in halves), s2_ref[...], sd_ref[...]]
    values = [*(v_ref[half, :] for half in halves), v2_ref[...], vd_ref[...]]
    top = functools.reduce(jnp.maximum, scores)
    exps = [jnp.exp(s - top) for s in scores]
    scale = 1.0 / functools.reduce(jnp.add, exps)
    spread = head_lanes((128, D), 1)
    c = None
    for e, v in zip(exps, values):
        p = jnp.dot((e * scale).astype(BF), spread, preferred_element_type=F32)
        part = p * v.astype(F32)
        c = part if c is None else c + part
    out = jnp.dot(c.astype(BF), wo_ref[...], preferred_element_type=F32)
    out = (h_ref[...].astype(F32) + out).astype(BF)
    pad = outs[0].shape[0]
    put = grouped_rows(dims, groups, pad, (groups * pad, n), 1)
    out = jnp.dot(put, out, preferred_element_type=F32)
    for m, o in enumerate(outs):
        o[...] = out[m * pad : (m + 1) * pad].astype(BF)


def call(kernel, outs, scratch, *args, cost=10**6):
    def space(a):
        return pl.BlockSpec(memory_space=pltpu.SMEM if a.dtype == jnp.int32 else pltpu.VMEM)

    return pl.pallas_call(
        kernel,
        out_shape=[jax.ShapeDtypeStruct(*o) for o in outs],
        in_specs=[space(a) for a in args],
        out_specs=[pl.BlockSpec(memory_space=pltpu.VMEM)] * len(outs),
        scratch_shapes=[pltpu.VMEM(*s) for s in scratch],
        compiler_params=pltpu.CompilerParams(vmem_limit_bytes=24 * 1024 * 1024),
        cost_estimate=pl.CostEstimate(flops=cost, bytes_accessed=cost // 1000, transcendentals=0),
    )(*args)


def column_path(tokens, timestep, mod_weight, col_qkv, col_out, bin_qkv, bin_out):
    rows, width = tokens.shape[1], tokens.shape[2]
    owners = lax.axis_size("seq")
    groups = owners // 2
    cols = width // groups
    dims = (rows, cols, width)
    pad = -(-rows * cols // 8) * 8
    n = rows * width

    def over_group(x, m):
        return lax.ppermute(x, "seq", [(i, i ^ (2 * m)) for i in range(owners)])

    def over_pair(x):
        return lax.ppermute(x, "seq", [(i, i ^ 1) for i in range(owners)])

    def over_bin(x, m):
        return lax.ppermute(x, "bin", [(i, i ^ m) for i in range(4)])

    message, full, lanes = ((pad, D), BF), ((n, D), BF), ((n, 128), F32)
    z = (lax.axis_index("seq") // 2).astype(jnp.int32).reshape(1)
    flat = tokens.reshape(rows * width, D)
    sent = call(
        functools.partial(pack_kernel, dims), [message] * groups, [], z, flat, cost=10**10
    )
    mod = modulation(timestep, mod_weight).reshape(4, D)
    own = [sent[0]] + [over_group(sent[m], m) for m in range(1, groups)]
    own[1], mod = lax.optimization_barrier((own[1], mod))
    other = [over_pair(x) for x in own]

    t, q, k, v = call(
        functools.partial(col_own_kernel, groups, dims), [full] * 4, [], *own, mod, col_qkv
    )
    low = -(-n // 32) * 16
    h, low, high = call(
        functools.partial(col_attend_kernel, groups, dims),
        [full, ((low, D), BF), ((n - low, D), BF)], [full] * 3,
        *other, mod, col_qkv, col_out, t, q, k, v,
    )
    hy = over_bin(h, 2)
    twice = [((2 * n, D), BF), ((2 * n, 128), F32)]
    q, v, s = call(
        bin_own_kernel, [full, *twice], [], h, over_bin(low, 1), over_bin(high, 1), mod, bin_qkv
    )
    hy, q = lax.optimization_barrier((hy, q))
    hd = over_bin(hy, 1)
    v2, s2 = call(bin_kv_kernel, [full, lanes], [], hy, q, mod, bin_qkv)
    done = call(
        functools.partial(bin_attend_kernel, groups, dims), [message] * groups, [full, lanes],
        hd, q, mod, bin_qkv, bin_out, h, v, s, v2, s2,
    )
    back = [done[0]] + [over_group(done[m], m) for m in range(1, groups)]
    (out,) = call(
        functools.partial(unpack_kernel, dims, groups), [((rows * width, D), BF)], [], z, *back
    )
    return out.reshape(tokens.shape)


def layer_norm(values, shift, scale):
    xf = values.astype(jnp.float32)
    mean = jnp.mean(xf, axis=-1, keepdims=True)
    var = jnp.mean((xf - mean) ** 2, axis=-1, keepdims=True)
    return ((xf - mean) * lax.rsqrt(var + 1e-06) * (1.0 + scale) + shift).astype(jnp.bfloat16)


def across_bins(query, key, value):
    scores = jnp.sum(
        query.astype(jnp.float32)[:, None] * key.astype(jnp.float32)[None], axis=-1
    ) * HD ** (-0.5)
    weights = jax.nn.softmax(scores, axis=1).astype(jnp.bfloat16)
    context = jnp.sum(
        weights.astype(jnp.float32)[..., None] * value.astype(jnp.float32)[None], axis=1
    )
    return context.astype(jnp.bfloat16)


def general_path(tokens, timestep, mod_weight, col_qkv, col_out, bin_qkv, bin_out):
    mod = modulation(timestep, mod_weight)
    shift1, scale1, shift2, scale2 = (mod[:D], mod[D : 2 * D], mod[2 * D : 3 * D], mod[3 * D :])
    rows_here = tokens.shape[1]
    width_all = tokens.shape[2]
    owners = lax.axis_size("seq")
    cols_each = width_all // owners
    normed1 = layer_norm(tokens, shift1, scale1)
    grouped = normed1.reshape(1, rows_here, owners, cols_each, D)
    query_weight = col_qkv[:, :D].reshape(D, HEADS, HD)
    key_weight = col_qkv[:, D : 2 * D].reshape(D, HEADS, HD)
    value_weight = col_qkv[:, 2 * D :].reshape(D, HEADS, HD)
    out_weight = col_out.reshape(HEADS, HD, D)
    piece = lax.all_to_all(grouped, "seq", split_axis=2, concat_axis=1, tiled=True)
    height = piece.shape[1]
    count = piece.shape[3]
    local = piece[0, :, 0]
    query = jnp.einsum(
        "iwc,chd->whid", local, query_weight, preferred_element_type=jnp.float32
    ).astype(jnp.bfloat16)
    key = jnp.einsum("iwc,chd->whid", local, key_weight, preferred_element_type=jnp.float32).astype(
        jnp.bfloat16
    )
    value = jnp.einsum(
        "iwc,chd->whid", local, value_weight, preferred_element_type=jnp.float32
    ).astype(jnp.bfloat16)
    scores = jnp.einsum("whid,whjd->whij", query, key, preferred_element_type=jnp.float32) * HD ** (
        -0.5
    )
    weights = jax.nn.softmax(scores, axis=-1).astype(jnp.bfloat16)
    context = jnp.einsum(
        "whij,whjd->whid", weights, value, preferred_element_type=jnp.float32
    ).astype(jnp.bfloat16)
    out = jnp.einsum(
        "whid,hde->iwe", context, out_weight, preferred_element_type=jnp.float32
    ).astype(jnp.bfloat16)
    attended = out.reshape(1, height, 1, count, D)
    back = lax.all_to_all(attended, "seq", split_axis=1, concat_axis=2, tiled=True)
    back = back.reshape(1, rows_here, width_all, D)
    hidden = (tokens.astype(jnp.float32) + back.astype(jnp.float32)).astype(jnp.bfloat16)
    normed2 = layer_norm(hidden, shift2, scale2)
    flat = normed2.reshape(-1, D)
    positions = flat.shape[0]
    every = lax.all_gather(normed2, "bin", axis=0, tiled=True)
    nbins = every.shape[0]
    every_flat = every.reshape(-1, D)
    query = jnp.dot(flat, bin_qkv[:, :D], preferred_element_type=jnp.float32).astype(jnp.bfloat16)
    keys_all = jnp.dot(
        every_flat, bin_qkv[:, D : 2 * D], preferred_element_type=jnp.float32
    ).astype(jnp.bfloat16)
    values_all = jnp.dot(
        every_flat, bin_qkv[:, 2 * D :], preferred_element_type=jnp.float32
    ).astype(jnp.bfloat16)
    context = across_bins(
        query.reshape(1, positions, HEADS, HD),
        keys_all.reshape(nbins, positions, HEADS, HD),
        values_all.reshape(nbins, positions, HEADS, HD),
    )
    projected = jnp.dot(context.reshape(-1, D), bin_out, preferred_element_type=jnp.float32)
    projected = projected.reshape(1, rows_here, width_all, D)
    return (hidden.astype(jnp.float32) + projected).astype(jnp.bfloat16)


def per_device(tokens, *rest):
    owners, width = lax.axis_size("seq"), tokens.shape[2]
    small = owners in (4, 8) and width % owners == 0 and lax.axis_size("bin") == 4
    if small and tokens.shape[1] * owners % 16 == 0 and tokens.shape[1] * width <= 256:
        return column_path(tokens, *rest)
    return general_path(tokens, *rest)


def solution(mesh):
    placed = (P("bin", "seq", None, None), P(), P(), P(), P(), P(), P())
    return jax.shard_map(
        per_device,
        mesh=mesh,
        in_specs=placed,
        out_specs=P("bin", "seq", None, None),
        check_vma=False,
    )
```

```python
import functools
import math

import jax
import jax.numpy as jnp
from jax import lax
from jax.experimental import pallas as pl
from jax.experimental.pallas import tpu as pltpu
from jax.sharding import PartitionSpec as P

D = 768
HEADS = 12
HD = 64
FREQ = 256
PAIR = 2 * HD
BF = jnp.bfloat16
F32 = jnp.float32


def modulation(timestep, mod_weight):
    half = FREQ // 2
    freqs = jnp.exp(-math.log(10000.0) * jnp.arange(half, dtype=jnp.float32) / half)
    angle = timestep.astype(jnp.float32)[0] * freqs
    emb = jax.nn.silu(jnp.concatenate([jnp.cos(angle), jnp.sin(angle)])).astype(jnp.bfloat16)
    return jnp.dot(emb[None, :], mod_weight, preferred_element_type=jnp.float32)[0]


def norm_rows(xf, mod_ref, which):
    shift = mod_ref[2 * which : 2 * which + 1, :]
    scale = mod_ref[2 * which + 1 : 2 * which + 2, :]
    mean = jnp.mean(xf, axis=-1, keepdims=True)
    cent = xf - mean
    var = jnp.mean(cent * cent, axis=-1, keepdims=True)
    return (cent * lax.rsqrt(var + 1e-06) * (1.0 + scale) + shift).astype(BF)


def stacked(refs):
    return jnp.concatenate([r[...].astype(F32) for r in refs], axis=0)


def project(normed, w_ref, which, out_ref, factor=None):
    y = jnp.dot(normed, w_ref[:, which * D : (which + 1) * D], preferred_element_type=F32)
    if factor is not None:
        y = y * factor
    out_ref[...] = y.astype(BF)


def divided(values, by, top):
    total = jnp.zeros_like(values)
    for step in range(by, top, by):
        total = total + (values >= step).astype(jnp.int32)
    return total


def message_rows(shape, row_dim, token_dim, rows, cols, width, owner):
    r = lax.broadcasted_iota(jnp.int32, shape, row_dim)
    t = lax.broadcasted_iota(jnp.int32, shape, token_dim)
    i = divided(r, cols, shape[row_dim])
    source = i * width + owner * cols + (r - i * cols)
    hit = (r < rows * cols) & (t == source)
    return jnp.where(hit, 1.0, 0.0).astype(BF)


def pack_kernel(dims, z_ref, tok_ref, *out_refs):
    rows, cols, width = dims
    x = tok_ref[...]
    for m, out in enumerate(out_refs):
        shape = (out.shape[0], x.shape[0])
        pick = message_rows(shape, 0, 1, rows, cols, width, z_ref[0] ^ m)
        out[...] = jnp.dot(pick, x, preferred_element_type=F32).astype(BF)


def token_rows(dims, pad, shape, z):
    rows, cols, width = dims
    r = lax.broadcasted_iota(jnp.int32, (1, shape[1]), 1)
    m = divided(r, pad, shape[1])
    r = r - m * pad
    i = divided(r, cols, pad)
    source = i * width + (z ^ m) * cols + (r - i * cols)
    source = jnp.where(r < rows * cols, source, -1)
    return jnp.where(source == lax.broadcasted_iota(jnp.int32, shape, 0), 1.0, 0.0).astype(BF)


def grouped_rows(dims, groups, pad, shape, row_dim):
    rows, cols, _ = dims
    flat = (shape[0], 1) if row_dim == 0 else (1, shape[1])
    r = lax.broadcasted_iota(jnp.int32, flat, row_dim)
    part, here = groups * rows * 2, rows * 2
    g = divided(r, part, shape[row_dim])
    r = r - g * part
    m = divided(r, here, part)
    r = r - m * here
    i = divided(r, 2, here)
    source = m * pad + i * cols + 2 * g + (r - 2 * i)
    hit = source == lax.broadcasted_iota(jnp.int32, shape, 1 - row_dim)
    return jnp.where(hit, 1.0, 0.0).astype(BF)


def column_marks(n, keys):
    def odd(count):
        return lax.broadcasted_iota(jnp.int32, (count, PAIR), 0) & 1

    lane = lax.broadcasted_iota(jnp.int32, (n, PAIR), 1)
    query = jnp.where(lane == odd(n), 1.0, 0.0).astype(BF)
    lane = lax.broadcasted_iota(jnp.int32, (keys, PAIR), 1)
    return query, jnp.where(lane == odd(keys), 0.0, -(2.0**100)).astype(BF)


def head_pair(q):
    low = lax.broadcasted_iota(jnp.int32, q.shape, 1) < HD
    zero = jnp.zeros_like(q)
    return jnp.concatenate([jnp.where(low, q, zero), jnp.where(low, zero, q)], axis=0)


def unpaired(c):
    n = c.shape[0] // 2
    low = lax.broadcasted_iota(jnp.int32, (n, PAIR), 1) < HD
    return jnp.where(low, c[:n], c[n:])


def regrouped(refs, dims):
    pad = refs[0].shape[0]
    n = len(refs) * dims[0] * dims[1]
    pick = grouped_rows(dims, len(refs), pad, (n, len(refs) * pad), 0)
    return jnp.dot(pick, stacked(refs).astype(BF), preferred_element_type=F32)


def col_own_kernel(groups, dims, *refs):
    own, (mod_ref, w_ref, t_ref, q_ref, k_ref, v_ref) = refs[:groups], refs[groups:]
    rows = regrouped(own, dims)
    t_ref[...] = rows.astype(BF)
    normed = norm_rows(rows, mod_ref, 0)
    project(normed, w_ref, 0, q_ref, HD**-0.5 * math.log2(math.e))
    project(normed, w_ref, 1, k_ref)
    project(normed, w_ref, 2, v_ref)


def col_attend_kernel(groups, dims, *refs):
    other = refs[:groups]
    mod_ref, w_ref, wo_ref, t_ref, q_ref, k_ref, v_ref, *refs = refs[groups:]
    *outs, k2_ref, v2_ref, c_ref = refs
    normed = norm_rows(regrouped(other, dims), mod_ref, 0)
    project(normed, w_ref, 1, k2_ref)
    project(normed, w_ref, 2, v2_ref)
    part = groups * dims[0] * 2
    q_mark, k_mark = column_marks(2 * part, 2 * part)
    ones = jnp.ones((2 * part, PAIR), BF)
    for g in range(dims[1] // 2):
        here = slice(g * part, (g + 1) * part)
        for j in range(HEADS // 2):
            lanes = slice(j * PAIR, (j + 1) * PAIR)
            q = jnp.concatenate([head_pair(q_ref[here, lanes]), q_mark], axis=1)
            k = jnp.concatenate([k_ref[here, lanes], k2_ref[here, lanes]], axis=0)
            v = jnp.concatenate([v_ref[here, lanes], v2_ref[here, lanes]], axis=0)
            k = jnp.concatenate([k, k_mark], axis=1)
            s = lax.dot_general(q, k, (((1,), (1,)), ((), ())), preferred_element_type=F32)
            e = jnp.exp2((s - jnp.max(s, axis=-1, keepdims=True)).astype(BF))
            c = jnp.dot(e, jnp.concatenate([v, ones], axis=1), preferred_element_type=F32)
            c_ref[here, lanes] = (unpaired(c[:, :PAIR]) / unpaired(c[:, PAIR:])).astype(BF)
    a = jnp.dot(c_ref[...], wo_ref[...], preferred_element_type=F32).astype(BF)
    h = (t_ref[...].astype(F32) + a.astype(F32)).astype(BF)
    pad = outs[0].shape[0]
    put = grouped_rows(dims, groups, pad, (groups * pad, h.shape[0]), 1)
    h = jnp.dot(put, h, preferred_element_type=F32)
    for m, o in enumerate(outs):
        o[...] = h[m * pad : (m + 1) * pad].astype(BF)


def head_lanes(shape, lane_dim):
    lane = lax.broadcasted_iota(jnp.int32, shape, lane_dim)
    head = lax.broadcasted_iota(jnp.int32, shape, 1 - lane_dim)
    return ((lane >= head * HD) & (lane < (head + 1) * HD)).astype(F32).astype(BF)


def key_scores(query, normed, w_ref, s_ref):
    k = jnp.dot(normed, w_ref[:, D : 2 * D], preferred_element_type=F32).astype(BF).astype(F32)
    s_ref[...] = jnp.dot(
        (query * k).astype(BF), head_lanes((D, 128), 0), preferred_element_type=F32
    )


def split_rows(rows, parts):
    start = 0
    for part in parts:
        part[...] = rows[start : start + part.shape[0]].astype(BF)
        start += part.shape[0]


def bin_own_kernel(count, *refs):
    chunks, (mod_ref, w_ref, q_ref, v_ref, s_ref, *parts) = refs[:count], refs[count:]
    rows = stacked(chunks)
    split_rows(rows, parts)
    normed = norm_rows(rows, mod_ref, 1)
    project(normed, w_ref, 0, q_ref, HD**-0.5)
    key_scores(q_ref[...].astype(F32), normed, w_ref, s_ref)
    project(normed, w_ref, 2, v_ref)


def bin_early_kernel(count, own_ref, *refs):
    chunks, (q_ref, mod_ref, w_ref, q2_ref, v_ref, s_ref, *parts) = refs[:count], refs[count:]
    rows = stacked(chunks)
    split_rows(rows, parts)
    rows = jnp.concatenate([rows, own_ref[...].astype(F32)], axis=0)
    normed = norm_rows(rows, mod_ref, 1)
    split = q_ref.shape[0]
    q2 = jnp.dot(normed, w_ref[:, :D], preferred_element_type=F32)[split:] * HD**-0.5
    q2_ref[...] = q2.astype(BF)
    query = jnp.concatenate([q_ref[...].astype(F32), q2_ref[...].astype(F32)], axis=0)
    key_scores(query, normed, w_ref, s_ref)
    project(normed, w_ref, 2, v_ref)


def bin_late_kernel(count, *refs):
    chunks, (q_ref, q2_ref, mod_ref, w_ref, v_ref, s_ref) = refs[:count], refs[count:]
    normed = norm_rows(stacked(chunks), mod_ref, 1)
    q = stacked((q_ref, q2_ref))
    key_scores(jnp.concatenate([q, q], axis=0), normed, w_ref, s_ref)
    project(normed, w_ref, 2, v_ref)


def bin_attend_kernel(groups, dims, z_ref, last_ref, *refs):
    own, refs = refs[:groups], refs[groups:]
    q2_ref, mod_ref, w_ref, wo_ref, v1_ref, s1_ref, v2_ref, s2_ref, v3_ref, s3_ref = refs[:-1]
    out_ref = refs[-1]
    n, m = s2_ref.shape[0], s1_ref.shape[0]
    normed = norm_rows(last_ref[...].astype(F32), mod_ref, 1)
    k = jnp.dot(normed, w_ref[:, D : 2 * D], preferred_element_type=F32).astype(BF).astype(F32)
    s4 = jnp.dot(
        (q2_ref[...].astype(F32) * k).astype(BF), head_lanes((D, 128), 0),
        preferred_element_type=F32,
    )
    v4 = jnp.dot(normed, w_ref[:, 2 * D :], preferred_element_type=F32)

    def of_bins(one, two, three, four):
        return [
            jnp.concatenate([one, two[m:]], axis=0),
            three[:n],
            jnp.concatenate([two[:m], three[n + m :]], axis=0),
            jnp.concatenate([three[n : n + m], four], axis=0),
        ]

    scores = of_bins(s1_ref[...], s2_ref[...], s3_ref[...], s4)
    values = of_bins(*(r[...].astype(F32) for r in (v1_ref, v2_ref, v3_ref)), v4)
    top = functools.reduce(jnp.maximum, scores)
    exps = [jnp.exp(s - top) for s in scores]
    scale = 1.0 / functools.reduce(jnp.add, exps)
    spread = head_lanes((128, D), 1)
    c = None
    for e, v in zip(exps, values):
        p = jnp.dot((e * scale).astype(BF), spread, preferred_element_type=F32)
        part = p * v
        c = part if c is None else c + part
    out = jnp.dot(c.astype(BF), wo_ref[...], preferred_element_type=F32)
    out = (stacked(own) + out).astype(BF)
    put = token_rows(dims, own[0].shape[0], (out_ref.shape[0], n), z_ref[0])
    out_ref[...] = jnp.dot(put, out, preferred_element_type=F32).astype(BF)


def call(kernel, outs, scratch, *args, cost=10**6):
    def space(a):
        return pl.BlockSpec(memory_space=pltpu.SMEM if a.dtype == jnp.int32 else pltpu.VMEM)

    return pl.pallas_call(
        kernel,
        out_shape=[jax.ShapeDtypeStruct(*o) for o in outs],
        in_specs=[space(a) for a in args],
        out_specs=[pl.BlockSpec(memory_space=pltpu.VMEM)] * len(outs),
        scratch_shapes=[pltpu.VMEM(*s) for s in scratch],
        compiler_params=pltpu.CompilerParams(vmem_limit_bytes=24 * 1024 * 1024),
        cost_estimate=pl.CostEstimate(flops=cost, bytes_accessed=cost // 1000, transcendentals=0),
    )(*args)


def column_path(tokens, timestep, mod_weight, col_qkv, col_out, bin_qkv, bin_out):
    rows, width = tokens.shape[1], tokens.shape[2]
    owners = lax.axis_size("seq")
    groups = owners // 2
    cols = width // groups
    dims = (rows, cols, width)
    pad = -(-rows * cols // 8) * 8
    n = rows * width

    def over_group(x, m):
        return lax.ppermute(x, "seq", [(i, i ^ (2 * m)) for i in range(owners)])

    def over_pair(x):
        return lax.ppermute(x, "seq", [(i, i ^ 1) for i in range(owners)])

    def over_bin(x, m):
        return lax.ppermute(x, "bin", [(i, i ^ m) for i in range(4)])

    message, full = ((pad, D), BF), ((n, D), BF)
    z = (lax.axis_index("seq") // 2).astype(jnp.int32).reshape(1)
    flat = tokens.reshape(rows * width, D)
    sent = call(
        functools.partial(pack_kernel, dims), [message] * groups, [], z, flat, cost=10**10
    )
    mod = modulation(timestep, mod_weight).reshape(4, D)
    own = [sent[0]] + [over_group(sent[m], m) for m in range(1, groups)]
    own[1], mod = lax.optimization_barrier((own[1], mod))
    other = [over_pair(x) for x in own]

    t, q, k, v = call(
        functools.partial(col_own_kernel, groups, dims), [full] * 4, [], *own, mod, col_qkv
    )
    sent = call(
        functools.partial(col_attend_kernel, groups, dims), [message] * groups, [full] * 3,
        *other, mod, col_qkv, col_out, t, q, k, v,
    )
    h = [sent[0]] + [over_group(sent[m], m) for m in range(1, groups)]
    hy = [over_bin(x, 2) for x in h]

    def rows_of(count):
        return [((count, D), BF), ((count, 128), F32)]

    padded, early = groups * pad, (groups - 1) * pad
    parts = [((padded // 2, D), BF), ((early - padded // 2, D), BF)]
    q, v1, s1, *h_parts = call(
        functools.partial(bin_own_kernel, groups - 1),
        [((early, D), BF), *rows_of(early), *parts], [], *h[:-1], mod, bin_qkv,
    )
    hc = [over_bin(x, 1) for x in (*h_parts, h[-1])]
    q2, v2, s2, *hy_parts = call(
        functools.partial(bin_early_kernel, groups - 1), [message, *rows_of(padded), *parts], [],
        h[-1], *hy[:-1], q, mod, bin_qkv,
    )
    hd_early = [over_bin(x, 1) for x in hy_parts]
    last, v2 = lax.optimization_barrier((hy[-1], v2))
    hd = over_bin(last, 1)
    others = [*hc, *hd_early, last]
    v3, s3 = call(
        functools.partial(bin_late_kernel, len(others)), rows_of(2 * padded), [],
        *others, q, q2, mod, bin_qkv,
    )
    (out,) = call(
        functools.partial(bin_attend_kernel, groups, dims), [full], [],
        z, hd, *h, q2, mod, bin_qkv, bin_out, v1, s1, v2, s2, v3, s3,
    )
    return out.reshape(tokens.shape)


def layer_norm(values, shift, scale):
    xf = values.astype(jnp.float32)
    mean = jnp.mean(xf, axis=-1, keepdims=True)
    var = jnp.mean((xf - mean) ** 2, axis=-1, keepdims=True)
    return ((xf - mean) * lax.rsqrt(var + 1e-06) * (1.0 + scale) + shift).astype(jnp.bfloat16)


def across_bins(query, key, value):
    scores = jnp.sum(
        query.astype(jnp.float32)[:, None] * key.astype(jnp.float32)[None], axis=-1
    ) * HD ** (-0.5)
    weights = jax.nn.softmax(scores, axis=1).astype(jnp.bfloat16)
    context = jnp.sum(
        weights.astype(jnp.float32)[..., None] * value.astype(jnp.float32)[None], axis=1
    )
    return context.astype(jnp.bfloat16)


def general_path(tokens, timestep, mod_weight, col_qkv, col_out, bin_qkv, bin_out):
    mod = modulation(timestep, mod_weight)
    shift1, scale1, shift2, scale2 = (mod[:D], mod[D : 2 * D], mod[2 * D : 3 * D], mod[3 * D :])
    rows_here = tokens.shape[1]
    width_all = tokens.shape[2]
    owners = lax.axis_size("seq")
    cols_each = width_all // owners
    normed1 = layer_norm(tokens, shift1, scale1)
    grouped = normed1.reshape(1, rows_here, owners, cols_each, D)
    query_weight = col_qkv[:, :D].reshape(D, HEADS, HD)
    key_weight = col_qkv[:, D : 2 * D].reshape(D, HEADS, HD)
    value_weight = col_qkv[:, 2 * D :].reshape(D, HEADS, HD)
    out_weight = col_out.reshape(HEADS, HD, D)
    piece = lax.all_to_all(grouped, "seq", split_axis=2, concat_axis=1, tiled=True)
    height = piece.shape[1]
    count = piece.shape[3]
    local = piece[0, :, 0]
    query = jnp.einsum(
        "iwc,chd->whid", local, query_weight, preferred_element_type=jnp.float32
    ).astype(jnp.bfloat16)
    key = jnp.einsum("iwc,chd->whid", local, key_weight, preferred_element_type=jnp.float32).astype(
        jnp.bfloat16
    )
    value = jnp.einsum(
        "iwc,chd->whid", local, value_weight, preferred_element_type=jnp.float32
    ).astype(jnp.bfloat16)
    scores = jnp.einsum("whid,whjd->whij", query, key, preferred_element_type=jnp.float32) * HD ** (
        -0.5
    )
    weights = jax.nn.softmax(scores, axis=-1).astype(jnp.bfloat16)
    context = jnp.einsum(
        "whij,whjd->whid", weights, value, preferred_element_type=jnp.float32
    ).astype(jnp.bfloat16)
    out = jnp.einsum(
        "whid,hde->iwe", context, out_weight, preferred_element_type=jnp.float32
    ).astype(jnp.bfloat16)
    attended = out.reshape(1, height, 1, count, D)
    back = lax.all_to_all(attended, "seq", split_axis=1, concat_axis=2, tiled=True)
    back = back.reshape(1, rows_here, width_all, D)
    hidden = (tokens.astype(jnp.float32) + back.astype(jnp.float32)).astype(jnp.bfloat16)
    normed2 = layer_norm(hidden, shift2, scale2)
    flat = normed2.reshape(-1, D)
    positions = flat.shape[0]
    every = lax.all_gather(normed2, "bin", axis=0, tiled=True)
    nbins = every.shape[0]
    every_flat = every.reshape(-1, D)
    query = jnp.dot(flat, bin_qkv[:, :D], preferred_element_type=jnp.float32).astype(jnp.bfloat16)
    keys_all = jnp.dot(
        every_flat, bin_qkv[:, D : 2 * D], preferred_element_type=jnp.float32
    ).astype(jnp.bfloat16)
    values_all = jnp.dot(
        every_flat, bin_qkv[:, 2 * D :], preferred_element_type=jnp.float32
    ).astype(jnp.bfloat16)
    context = across_bins(
        query.reshape(1, positions, HEADS, HD),
        keys_all.reshape(nbins, positions, HEADS, HD),
        values_all.reshape(nbins, positions, HEADS, HD),
    )
    projected = jnp.dot(context.reshape(-1, D), bin_out, preferred_element_type=jnp.float32)
    projected = projected.reshape(1, rows_here, width_all, D)
    return (hidden.astype(jnp.float32) + projected).astype(jnp.bfloat16)


def per_device(tokens, *rest):
    owners, width = lax.axis_size("seq"), tokens.shape[2]
    small = owners in (4, 8) and width % owners == 0 and lax.axis_size("bin") == 4
    if small and tokens.shape[1] * owners % 16 == 0 and tokens.shape[1] * width <= 256:
        return column_path(tokens, *rest)
    return general_path(tokens, *rest)


def solution(mesh):
    placed = (P("bin", "seq", None, None), P(), P(), P(), P(), P(), P())
    return jax.shard_map(
        per_device,
        mesh=mesh,
        in_specs=placed,
        out_specs=P("bin", "seq", None, None),
        check_vma=False,
    )
```

```python
import functools
import math

import jax
import jax.numpy as jnp
from jax import lax
from jax.experimental import pallas as pl
from jax.experimental.pallas import tpu as pltpu
from jax.sharding import PartitionSpec as P

D = 768
HEADS = 12
HD = 64
FREQ = 256
PAIR = 2 * HD
BF = jnp.bfloat16
F32 = jnp.float32


def modulation(timestep, mod_weight):
    half = FREQ // 2
    freqs = jnp.exp(-math.log(10000.0) * jnp.arange(half, dtype=jnp.float32) / half)
    angle = timestep.astype(jnp.float32)[0] * freqs
    emb = jax.nn.silu(jnp.concatenate([jnp.cos(angle), jnp.sin(angle)])).astype(jnp.bfloat16)
    return jnp.dot(emb[None, :], mod_weight, preferred_element_type=jnp.float32)[0]


def norm_rows(xf, mod_ref, which):
    shift = mod_ref[2 * which : 2 * which + 1, :]
    scale = mod_ref[2 * which + 1 : 2 * which + 2, :]
    mean = jnp.mean(xf, axis=-1, keepdims=True)
    cent = xf - mean
    var = jnp.mean(cent * cent, axis=-1, keepdims=True)
    return (cent * lax.rsqrt(var + 1e-06) * (1.0 + scale) + shift).astype(BF)


def stacked(refs):
    return jnp.concatenate([r[...].astype(F32) for r in refs], axis=0)


def project(normed, w_ref, which, out_ref, factor=None):
    y = jnp.dot(normed, w_ref[:, which * D : (which + 1) * D], preferred_element_type=F32)
    if factor is not None:
        y = y * factor
    out_ref[...] = y.astype(BF)


def divided(values, by, top):
    total = jnp.zeros_like(values)
    for step in range(by, top, by):
        total = total + (values >= step).astype(jnp.int32)
    return total


def message_rows(shape, row_dim, token_dim, rows, cols, width, owner):
    r = lax.broadcasted_iota(jnp.int32, shape, row_dim)
    t = lax.broadcasted_iota(jnp.int32, shape, token_dim)
    i = divided(r, cols, shape[row_dim])
    source = i * width + owner * cols + (r - i * cols)
    hit = (r < rows * cols) & (t == source)
    return jnp.where(hit, 1.0, 0.0).astype(BF)


def pack_kernel(dims, z_ref, tok_ref, *out_refs):
    rows, cols, width = dims
    x = tok_ref[...]
    for m, out in enumerate(out_refs):
        shape = (out.shape[0], x.shape[0])
        pick = message_rows(shape, 0, 1, rows, cols, width, z_ref[0] ^ m)
        out[...] = jnp.dot(pick, x, preferred_element_type=F32).astype(BF)


def token_rows(dims, pad, shape, z):
    rows, cols, width = dims
    r = lax.broadcasted_iota(jnp.int32, (1, shape[1]), 1)
    m = divided(r, pad, shape[1])
    r = r - m * pad
    i = divided(r, cols, pad)
    source = i * width + (z ^ m) * cols + (r - i * cols)
    source = jnp.where(r < rows * cols, source, -1)
    return jnp.where(source == lax.broadcasted_iota(jnp.int32, shape, 0), 1.0, 0.0).astype(BF)


def grouped_rows(dims, groups, pad, shape, row_dim):
    rows, cols, _ = dims
    flat = (shape[0], 1) if row_dim == 0 else (1, shape[1])
    r = lax.broadcasted_iota(jnp.int32, flat, row_dim)
    part, here = groups * rows * 2, rows * 2
    g = divided(r, part, shape[row_dim])
    r = r - g * part
    m = divided(r, here, part)
    r = r - m * here
    i = divided(r, 2, here)
    source = m * pad + i * cols + 2 * g + (r - 2 * i)
    hit = source == lax.broadcasted_iota(jnp.int32, shape, 1 - row_dim)
    return jnp.where(hit, 1.0, 0.0).astype(BF)


def column_marks(n, keys):
    def odd(count):
        return lax.broadcasted_iota(jnp.int32, (count, PAIR), 0) & 1

    lane = lax.broadcasted_iota(jnp.int32, (n, PAIR), 1)
    query = jnp.where(lane == odd(n), 1.0, 0.0).astype(BF)
    lane = lax.broadcasted_iota(jnp.int32, (keys, PAIR), 1)
    return query, jnp.where(lane == odd(keys), 0.0, -(2.0**100)).astype(BF)


def head_pair(q):
    low = lax.broadcasted_iota(jnp.int32, q.shape, 1) < HD
    zero = jnp.zeros_like(q)
    return jnp.concatenate([jnp.where(low, q, zero), jnp.where(low, zero, q)], axis=0)


def unpaired(c):
    n = c.shape[0] // 2
    low = lax.broadcasted_iota(jnp.int32, (n, PAIR), 1) < HD
    return jnp.where(low, c[:n], c[n:])


def regrouped(refs, dims):
    pad = refs[0].shape[0]
    n = len(refs) * dims[0] * dims[1]
    pick = grouped_rows(dims, len(refs), pad, (n, len(refs) * pad), 0)
    return jnp.dot(pick, stacked(refs).astype(BF), preferred_element_type=F32)


def col_own_kernel(groups, dims, *refs):
    own, (mod_ref, w_ref, t_ref, q_ref, k_ref, v_ref) = refs[:groups], refs[groups:]
    rows = regrouped(own, dims)
    t_ref[...] = rows.astype(BF)
    normed = norm_rows(rows, mod_ref, 0)
    project(normed, w_ref, 0, q_ref, HD**-0.5 * math.log2(math.e))
    project(normed, w_ref, 1, k_ref)
    project(normed, w_ref, 2, v_ref)


def col_attend_kernel(groups, dims, *refs):
    other = refs[:groups]
    mod_ref, w_ref, wo_ref, t_ref, q_ref, k_ref, v_ref, *refs = refs[groups:]
    *outs, k2_ref, v2_ref, c_ref = refs
    normed = norm_rows(regrouped(other, dims), mod_ref, 0)
    project(normed, w_ref, 1, k2_ref)
    project(normed, w_ref, 2, v2_ref)
    part = groups * dims[0] * 2
    q_mark, k_mark = column_marks(2 * part, 2 * part)
    ones = jnp.ones((2 * part, PAIR), BF)
    for g in range(dims[1] // 2):
        here = slice(g * part, (g + 1) * part)
        for j in range(HEADS // 2):
            lanes = slice(j * PAIR, (j + 1) * PAIR)
            q = jnp.concatenate([head_pair(q_ref[here, lanes]), q_mark], axis=1)
            k = jnp.concatenate([k_ref[here, lanes], k2_ref[here, lanes]], axis=0)
            v = jnp.concatenate([v_ref[here, lanes], v2_ref[here, lanes]], axis=0)
            k = jnp.concatenate([k, k_mark], axis=1)
            s = lax.dot_general(q, k, (((1,), (1,)), ((), ())), preferred_element_type=F32)
            e = jnp.exp2((s - jnp.max(s, axis=-1, keepdims=True)).astype(BF))
            c = jnp.dot(e, jnp.concatenate([v, ones], axis=1), preferred_element_type=F32)
            c_ref[here, lanes] = (unpaired(c[:, :PAIR]) / unpaired(c[:, PAIR:])).astype(BF)
    a = jnp.dot(c_ref[...], wo_ref[...], preferred_element_type=F32).astype(BF)
    h = (t_ref[...].astype(F32) + a.astype(F32)).astype(BF)
    pad = outs[0].shape[0]
    put = grouped_rows(dims, groups, pad, (groups * pad, h.shape[0]), 1)
    h = jnp.dot(put, h, preferred_element_type=F32)
    for m, o in enumerate(outs):
        o[...] = h[m * pad : (m + 1) * pad].astype(BF)


def head_lanes(shape, lane_dim):
    lane = lax.broadcasted_iota(jnp.int32, shape, lane_dim)
    head = lax.broadcasted_iota(jnp.int32, shape, 1 - lane_dim)
    return ((lane >= head * HD) & (lane < (head + 1) * HD)).astype(F32).astype(BF)


def key_scores(query, normed, w_ref, s_ref):
    k = jnp.dot(normed, w_ref[:, D : 2 * D], preferred_element_type=F32).astype(BF).astype(F32)
    s_ref[...] = jnp.dot(
        (query * k).astype(BF), head_lanes((D, 128), 0), preferred_element_type=F32
    )


def split_rows(rows, parts):
    start = 0
    for part in parts:
        part[...] = rows[start : start + part.shape[0]].astype(BF)
        start += part.shape[0]


def bin_own_kernel(count, *refs):
    chunks, (mod_ref, w_ref, q_ref, v_ref, s_ref, *parts) = refs[:count], refs[count:]
    rows = stacked(chunks)
    split_rows(rows, parts)
    normed = norm_rows(rows, mod_ref, 1)
    project(normed, w_ref, 0, q_ref, HD**-0.5)
    key_scores(q_ref[...].astype(F32), normed, w_ref, s_ref)
    project(normed, w_ref, 2, v_ref)


def bin_early_kernel(count, own_ref, *refs):
    chunks, (q_ref, mod_ref, w_ref, q2_ref, v_ref, s_ref, *parts) = refs[:count], refs[count:]
    rows = stacked(chunks)
    split_rows(rows, parts)
    rows = jnp.concatenate([rows, own_ref[...].astype(F32)], axis=0)
    normed = norm_rows(rows, mod_ref, 1)
    split = q_ref.shape[0]
    q2 = jnp.dot(normed, w_ref[:, :D], preferred_element_type=F32)[split:] * HD**-0.5
    q2_ref[...] = q2.astype(BF)
    query = jnp.concatenate([q_ref[...].astype(F32), q2_ref[...].astype(F32)], axis=0)
    key_scores(query, normed, w_ref, s_ref)
    project(normed, w_ref, 2, v_ref)


def bin_late_kernel(count, *refs):
    chunks, (q_ref, q2_ref, mod_ref, w_ref, v_ref, s_ref) = refs[:count], refs[count:]
    normed = norm_rows(stacked(chunks), mod_ref, 1)
    q = stacked((q_ref, q2_ref))
    key_scores(jnp.concatenate([q, q], axis=0), normed, w_ref, s_ref)
    project(normed, w_ref, 2, v_ref)


def bin_attend_kernel(groups, dims, z_ref, last_ref, *refs):
    own, refs = refs[:groups], refs[groups:]
    q2_ref, mod_ref, w_ref, wo_ref, v1_ref, s1_ref, v2_ref, s2_ref, v3_ref, s3_ref = refs[:-1]
    out_ref = refs[-1]
    n, m = s2_ref.shape[0], s1_ref.shape[0]
    normed = norm_rows(last_ref[...].astype(F32), mod_ref, 1)
    k = jnp.dot(normed, w_ref[:, D : 2 * D], preferred_element_type=F32).astype(BF).astype(F32)
    s4 = jnp.dot(
        (q2_ref[...].astype(F32) * k).astype(BF), head_lanes((D, 128), 0),
        preferred_element_type=F32,
    )
    v4 = jnp.dot(normed, w_ref[:, 2 * D :], preferred_element_type=F32)

    def of_bins(one, two, three, four):
        return [
            jnp.concatenate([one, two[m:]], axis=0),
            three[:n],
            jnp.concatenate([two[:m], three[n + m :]], axis=0),
            jnp.concatenate([three[n : n + m], four], axis=0),
        ]

    scores = of_bins(s1_ref[...], s2_ref[...], s3_ref[...], s4)
    values = of_bins(*(r[...].astype(F32) for r in (v1_ref, v2_ref, v3_ref)), v4)
    top = functools.reduce(jnp.maximum, scores)
    exps = [jnp.exp(s - top) for s in scores]
    scale = 1.0 / functools.reduce(jnp.add, exps)
    spread = head_lanes((128, D), 1)
    c = None
    for e, v in zip(exps, values):
        p = jnp.dot((e * scale).astype(BF), spread, preferred_element_type=F32)
        part = p * v
        c = part if c is None else c + part
    out = jnp.dot(c.astype(BF), wo_ref[...], preferred_element_type=F32)
    out = (stacked(own) + out).astype(BF)
    put = token_rows(dims, own[0].shape[0], (out_ref.shape[0], n), z_ref[0])
    out_ref[...] = jnp.dot(put, out, preferred_element_type=F32).astype(BF)


def call(kernel, outs, scratch, *args, cost=10**6):
    def space(a):
        return pl.BlockSpec(memory_space=pltpu.SMEM if a.dtype == jnp.int32 else pltpu.VMEM)

    return pl.pallas_call(
        kernel,
        out_shape=[jax.ShapeDtypeStruct(*o) for o in outs],
        in_specs=[space(a) for a in args],
        out_specs=[pl.BlockSpec(memory_space=pltpu.VMEM)] * len(outs),
        scratch_shapes=[pltpu.VMEM(*s) for s in scratch],
        compiler_params=pltpu.CompilerParams(vmem_limit_bytes=24 * 1024 * 1024),
        cost_estimate=pl.CostEstimate(flops=cost, bytes_accessed=cost // 1000, transcendentals=0),
    )(*args)


def column_path(tokens, timestep, mod_weight, col_qkv, col_out, bin_qkv, bin_out):
    rows, width = tokens.shape[1], tokens.shape[2]
    owners = lax.axis_size("seq")
    groups = owners // 2
    cols = width // groups
    dims = (rows, cols, width)
    pad = -(-rows * cols // 8) * 8
    n = rows * width

    def over_group(x, m):
        return lax.ppermute(x, "seq", [(i, i ^ (2 * m)) for i in range(owners)])

    def over_pair(x):
        return lax.ppermute(x, "seq", [(i, i ^ 1) for i in range(owners)])

    def over_bin(x, m):
        return lax.ppermute(x, "bin", [(i, i ^ m) for i in range(4)])

    message, full = ((pad, D), BF), ((n, D), BF)
    z = (lax.axis_index("seq") // 2).astype(jnp.int32).reshape(1)
    flat = tokens.reshape(rows * width, D)
    sent = call(
        functools.partial(pack_kernel, dims), [message] * groups, [], z, flat, cost=10**10
    )
    mod = modulation(timestep, mod_weight).reshape(4, D)
    own = [sent[0]] + [over_group(sent[m], m) for m in range(1, groups)]
    own[1], mod = lax.optimization_barrier((own[1], mod))
    other = [over_pair(x) for x in own]

    t, q, k, v = call(
        functools.partial(col_own_kernel, groups, dims), [full] * 4, [], *own, mod, col_qkv
    )
    sent = call(
        functools.partial(col_attend_kernel, groups, dims), [message] * groups, [full] * 3,
        *other, mod, col_qkv, col_out, t, q, k, v,
    )
    h = [sent[0]] + [over_group(sent[m], m) for m in range(1, groups)]
    hy = [over_bin(x, 2) for x in h]

    def rows_of(count):
        return [((count, D), BF), ((count, 128), F32)]

    padded, early = groups * pad, (groups - 1) * pad
    parts = [((padded // 2, D), BF), ((early - padded // 2, D), BF)]
    q, v1, s1, *h_parts = call(
        functools.partial(bin_own_kernel, groups - 1),
        [((early, D), BF), *rows_of(early), ((early, D), BF)], [], *h[:-1], mod, bin_qkv,
    )
    hc = [over_bin(x, 1) for x in (*h_parts, h[-1])]
    q2, v2, s2, *hy_parts = call(
        functools.partial(bin_early_kernel, groups - 1), [message, *rows_of(padded), *parts], [],
        h[-1], *hy[:-1], q, mod, bin_qkv,
    )
    hd_early = [over_bin(x, 1) for x in hy_parts]
    last, v2 = lax.optimization_barrier((hy[-1], v2))
    hd = over_bin(last, 1)
    others = [*hc, *hd_early, last]
    v3, s3 = call(
        functools.partial(bin_late_kernel, len(others)), rows_of(2 * padded), [],
        *others, q, q2, mod, bin_qkv,
    )
    (out,) = call(
        functools.partial(bin_attend_kernel, groups, dims), [full], [],
        z, hd, *h, q2, mod, bin_qkv, bin_out, v1, s1, v2, s2, v3, s3,
    )
    return out.reshape(tokens.shape)


def layer_norm(values, shift, scale):
    xf = values.astype(jnp.float32)
    mean = jnp.mean(xf, axis=-1, keepdims=True)
    var = jnp.mean((xf - mean) ** 2, axis=-1, keepdims=True)
    return ((xf - mean) * lax.rsqrt(var + 1e-06) * (1.0 + scale) + shift).astype(jnp.bfloat16)


def across_bins(query, key, value):
    scores = jnp.sum(
        query.astype(jnp.float32)[:, None] * key.astype(jnp.float32)[None], axis=-1
    ) * HD ** (-0.5)
    weights = jax.nn.softmax(scores, axis=1).astype(jnp.bfloat16)
    context = jnp.sum(
        weights.astype(jnp.float32)[..., None] * value.astype(jnp.float32)[None], axis=1
    )
    return context.astype(jnp.bfloat16)


def general_path(tokens, timestep, mod_weight, col_qkv, col_out, bin_qkv, bin_out):
    mod = modulation(timestep, mod_weight)
    shift1, scale1, shift2, scale2 = (mod[:D], mod[D : 2 * D], mod[2 * D : 3 * D], mod[3 * D :])
    rows_here = tokens.shape[1]
    width_all = tokens.shape[2]
    owners = lax.axis_size("seq")
    cols_each = width_all // owners
    normed1 = layer_norm(tokens, shift1, scale1)
    grouped = normed1.reshape(1, rows_here, owners, cols_each, D)
    query_weight = col_qkv[:, :D].reshape(D, HEADS, HD)
    key_weight = col_qkv[:, D : 2 * D].reshape(D, HEADS, HD)
    value_weight = col_qkv[:, 2 * D :].reshape(D, HEADS, HD)
    out_weight = col_out.reshape(HEADS, HD, D)
    piece = lax.all_to_all(grouped, "seq", split_axis=2, concat_axis=1, tiled=True)
    height = piece.shape[1]
    count = piece.shape[3]
    local = piece[0, :, 0]
    query = jnp.einsum(
        "iwc,chd->whid", local, query_weight, preferred_element_type=jnp.float32
    ).astype(jnp.bfloat16)
    key = jnp.einsum("iwc,chd->whid", local, key_weight, preferred_element_type=jnp.float32).astype(
        jnp.bfloat16
    )
    value = jnp.einsum(
        "iwc,chd->whid", local, value_weight, preferred_element_type=jnp.float32
    ).astype(jnp.bfloat16)
    scores = jnp.einsum("whid,whjd->whij", query, key, preferred_element_type=jnp.float32) * HD ** (
        -0.5
    )
    weights = jax.nn.softmax(scores, axis=-1).astype(jnp.bfloat16)
    context = jnp.einsum(
        "whij,whjd->whid", weights, value, preferred_element_type=jnp.float32
    ).astype(jnp.bfloat16)
    out = jnp.einsum(
        "whid,hde->iwe", context, out_weight, preferred_element_type=jnp.float32
    ).astype(jnp.bfloat16)
    attended = out.reshape(1, height, 1, count, D)
    back = lax.all_to_all(attended, "seq", split_axis=1, concat_axis=2, tiled=True)
    back = back.reshape(1, rows_here, width_all, D)
    hidden = (tokens.astype(jnp.float32) + back.astype(jnp.float32)).astype(jnp.bfloat16)
    normed2 = layer_norm(hidden, shift2, scale2)
    flat = normed2.reshape(-1, D)
    positions = flat.shape[0]
    every = lax.all_gather(normed2, "bin", axis=0, tiled=True)
    nbins = every.shape[0]
    every_flat = every.reshape(-1, D)
    query = jnp.dot(flat, bin_qkv[:, :D], preferred_element_type=jnp.float32).astype(jnp.bfloat16)
    keys_all = jnp.dot(
        every_flat, bin_qkv[:, D : 2 * D], preferred_element_type=jnp.float32
    ).astype(jnp.bfloat16)
    values_all = jnp.dot(
        every_flat, bin_qkv[:, 2 * D :], preferred_element_type=jnp.float32
    ).astype(jnp.bfloat16)
    context = across_bins(
        query.reshape(1, positions, HEADS, HD),
        keys_all.reshape(nbins, positions, HEADS, HD),
        values_all.reshape(nbins, positions, HEADS, HD),
    )
    projected = jnp.dot(context.reshape(-1, D), bin_out, preferred_element_type=jnp.float32)
    projected = projected.reshape(1, rows_here, width_all, D)
    return (hidden.astype(jnp.float32) + projected).astype(jnp.bfloat16)


def per_device(tokens, *rest):
    owners, width = lax.axis_size("seq"), tokens.shape[2]
    small = owners in (4, 8) and width % owners == 0 and lax.axis_size("bin") == 4
    if small and tokens.shape[1] * owners % 16 == 0 and tokens.shape[1] * width <= 256:
        return column_path(tokens, *rest)
    return general_path(tokens, *rest)


def solution(mesh):
    placed = (P("bin", "seq", None, None), P(), P(), P(), P(), P(), P())
    return jax.shard_map(
        per_device,
        mesh=mesh,
        in_specs=placed,
        out_specs=P("bin", "seq", None, None),
        check_vma=False,
    )
```

```python
import functools
import math

import jax
import jax.numpy as jnp
from jax import lax
from jax.experimental import pallas as pl
from jax.experimental.pallas import tpu as pltpu
from jax.sharding import PartitionSpec as P

D = 768
HEADS = 12
HD = 64
FREQ = 256
PAIR = 2 * HD
ORDER = (0, 1, 3, 2)
BF = jnp.bfloat16
F32 = jnp.float32


def modulation(timestep, mod_weight):
    half = FREQ // 2
    freqs = jnp.exp(-math.log(10000.0) * jnp.arange(half, dtype=jnp.float32) / half)
    angle = timestep.astype(jnp.float32)[0] * freqs
    emb = jax.nn.silu(jnp.concatenate([jnp.cos(angle), jnp.sin(angle)])).astype(jnp.bfloat16)
    return jnp.dot(emb[None, :], mod_weight, preferred_element_type=jnp.float32)[0]


def norm_rows(xf, mod_ref, which):
    shift = mod_ref[2 * which : 2 * which + 1, :]
    scale = mod_ref[2 * which + 1 : 2 * which + 2, :]
    mean = jnp.mean(xf, axis=-1, keepdims=True)
    cent = xf - mean
    var = jnp.mean(cent * cent, axis=-1, keepdims=True)
    return (cent * lax.rsqrt(var + 1e-06) * (1.0 + scale) + shift).astype(BF)


def stacked(refs):
    return jnp.concatenate([r[...].astype(F32) for r in refs], axis=0)


def project(normed, w_ref, which, out_ref, factor=None):
    y = jnp.dot(normed, w_ref[:, which * D : (which + 1) * D], preferred_element_type=F32)
    if factor is not None:
        y = y * factor
    out_ref[...] = y.astype(BF)


def divided(values, by, top):
    total = jnp.zeros_like(values)
    for step in range(by, top, by):
        total = total + (values >= step).astype(jnp.int32)
    return total


def partner(m, groups):
    return ORDER[m] if groups == len(ORDER) else m


def message_rows(shape, row_dim, token_dim, rows, cols, width, owner):
    r = lax.broadcasted_iota(jnp.int32, shape, row_dim)
    t = lax.broadcasted_iota(jnp.int32, shape, token_dim)
    i = divided(r, cols, shape[row_dim])
    source = i * width + owner * cols + (r - i * cols)
    hit = (r < rows * cols) & (t == source)
    return jnp.where(hit, 1.0, 0.0).astype(BF)


def pack_kernel(dims, z_ref, tok_ref, *out_refs):
    rows, cols, width = dims
    x = tok_ref[...]
    for m, out in enumerate(out_refs):
        shape = (out.shape[0], x.shape[0])
        pick = message_rows(shape, 0, 1, rows, cols, width, z_ref[0] ^ partner(m, len(out_refs)))
        out[...] = jnp.dot(pick, x, preferred_element_type=F32).astype(BF)


def token_rows(dims, pad, shape, z):
    rows, cols, width = dims
    r = lax.broadcasted_iota(jnp.int32, (1, shape[1]), 1)
    m = divided(r, pad, shape[1])
    r = r - m * pad
    i = divided(r, cols, pad)
    groups = shape[1] // pad
    differs = sum(jnp.where(m == k, partner(k, groups), 0) for k in range(groups))
    source = i * width + (z ^ differs) * cols + (r - i * cols)
    source = jnp.where(r < rows * cols, source, -1)
    return jnp.where(source == lax.broadcasted_iota(jnp.int32, shape, 0), 1.0, 0.0).astype(BF)


def grouped_rows(dims, groups, pad, shape, row_dim):
    rows, cols, _ = dims
    flat = (shape[0], 1) if row_dim == 0 else (1, shape[1])
    r = lax.broadcasted_iota(jnp.int32, flat, row_dim)
    part, here = groups * rows * 2, rows * 2
    g = divided(r, part, shape[row_dim])
    r = r - g * part
    m = divided(r, here, part)
    r = r - m * here
    i = divided(r, 2, here)
    source = m * pad + i * cols + 2 * g + (r - 2 * i)
    hit = source == lax.broadcasted_iota(jnp.int32, shape, 1 - row_dim)
    return jnp.where(hit, 1.0, 0.0).astype(BF)


def column_marks(n, keys):
    def odd(count):
        return lax.broadcasted_iota(jnp.int32, (count, PAIR), 0) & 1

    lane = lax.broadcasted_iota(jnp.int32, (n, PAIR), 1)
    query = jnp.where(lane == odd(n), 1.0, 0.0).astype(BF)
    lane = lax.broadcasted_iota(jnp.int32, (keys, PAIR), 1)
    return query, jnp.where(lane == odd(keys), 0.0, -(2.0**100)).astype(BF)


def head_pair(q):
    low = lax.broadcasted_iota(jnp.int32, q.shape, 1) < HD
    zero = jnp.zeros_like(q)
    return jnp.concatenate([jnp.where(low, q, zero), jnp.where(low, zero, q)], axis=0)


def unpaired(c):
    n = c.shape[0] // 2
    low = lax.broadcasted_iota(jnp.int32, (n, PAIR), 1) < HD
    return jnp.where(low, c[:n], c[n:])


def regrouped(refs, dims):
    pad = refs[0].shape[0]
    n = len(refs) * dims[0] * dims[1]
    pick = grouped_rows(dims, len(refs), pad, (n, len(refs) * pad), 0)
    return jnp.dot(pick, stacked(refs).astype(BF), preferred_element_type=F32)


def col_own_kernel(groups, dims, *refs):
    own, (mod_ref, w_ref, t_ref, q_ref, k_ref, v_ref) = refs[:groups], refs[groups:]
    rows = regrouped(own, dims)
    t_ref[...] = rows.astype(BF)
    normed = norm_rows(rows, mod_ref, 0)
    project(normed, w_ref, 0, q_ref, HD**-0.5 * math.log2(math.e))
    project(normed, w_ref, 1, k_ref)
    project(normed, w_ref, 2, v_ref)


def col_attend_kernel(groups, dims, *refs):
    other = refs[:groups]
    mod_ref, w_ref, wo_ref, t_ref, q_ref, k_ref, v_ref, *refs = refs[groups:]
    *outs, k2_ref, v2_ref, c_ref = refs
    normed = norm_rows(regrouped(other, dims), mod_ref, 0)
    project(normed, w_ref, 1, k2_ref)
    project(normed, w_ref, 2, v2_ref)
    part = groups * dims[0] * 2
    q_mark, k_mark = column_marks(2 * part, 2 * part)
    ones = jnp.ones((2 * part, PAIR), BF)
    for g in range(dims[1] // 2):
        here = slice(g * part, (g + 1) * part)
        for j in range(HEADS // 2):
            lanes = slice(j * PAIR, (j + 1) * PAIR)
            q = jnp.concatenate([head_pair(q_ref[here, lanes]), q_mark], axis=1)
            k = jnp.concatenate([k_ref[here, lanes], k2_ref[here, lanes]], axis=0)
            v = jnp.concatenate([v_ref[here, lanes], v2_ref[here, lanes]], axis=0)
            k = jnp.concatenate([k, k_mark], axis=1)
            s = lax.dot_general(q, k, (((1,), (1,)), ((), ())), preferred_element_type=F32)
            e = jnp.exp2((s - jnp.max(s, axis=-1, keepdims=True)).astype(BF))
            c = jnp.dot(e, jnp.concatenate([v, ones], axis=1), preferred_element_type=F32)
            c_ref[here, lanes] = (unpaired(c[:, :PAIR]) / unpaired(c[:, PAIR:])).astype(BF)
    a = jnp.dot(c_ref[...], wo_ref[...], preferred_element_type=F32).astype(BF)
    h = (t_ref[...].astype(F32) + a.astype(F32)).astype(BF)
    pad = outs[0].shape[0]
    put = grouped_rows(dims, groups, pad, (groups * pad, h.shape[0]), 1)
    h = jnp.dot(put, h, preferred_element_type=F32)
    for m, o in enumerate(outs):
        o[...] = h[m * pad : (m + 1) * pad].astype(BF)


def head_lanes(shape, lane_dim):
    lane = lax.broadcasted_iota(jnp.int32, shape, lane_dim)
    head = lax.broadcasted_iota(jnp.int32, shape, 1 - lane_dim)
    return ((lane >= head * HD) & (lane < (head + 1) * HD)).astype(F32).astype(BF)


def key_scores(query, normed, w_ref, s_ref):
    k = jnp.dot(normed, w_ref[:, D : 2 * D], preferred_element_type=F32).astype(BF).astype(F32)
    s_ref[...] = jnp.dot(
        (query * k).astype(BF), head_lanes((D, 128), 0), preferred_element_type=F32
    )


def split_rows(rows, parts):
    start = 0
    for part in parts:
        part[...] = rows[start : start + part.shape[0]].astype(BF)
        start += part.shape[0]


def bin_own_kernel(count, *refs):
    chunks, (mod_ref, w_ref, q_ref, v_ref, s_ref, *parts) = refs[:count], refs[count:]
    rows = stacked(chunks)
    split_rows(rows, parts)
    normed = norm_rows(rows, mod_ref, 1)
    project(normed, w_ref, 0, q_ref, HD**-0.5)
    key_scores(q_ref[...].astype(F32), normed, w_ref, s_ref)
    project(normed, w_ref, 2, v_ref)


def bin_early_kernel(count, own_ref, *refs):
    chunks, (q_ref, mod_ref, w_ref, q2_ref, v_ref, s_ref, *parts) = refs[:count], refs[count:]
    rows = stacked(chunks)
    split_rows(rows, parts)
    rows = jnp.concatenate([rows, own_ref[...].astype(F32)], axis=0)
    normed = norm_rows(rows, mod_ref, 1)
    split = q_ref.shape[0]
    q2 = jnp.dot(normed, w_ref[:, :D], preferred_element_type=F32)[split:] * HD**-0.5
    q2_ref[...] = q2.astype(BF)
    query = jnp.concatenate([q_ref[...].astype(F32), q2_ref[...].astype(F32)], axis=0)
    key_scores(query, normed, w_ref, s_ref)
    project(normed, w_ref, 2, v_ref)


def bin_late_kernel(count, *refs):
    chunks, (q_ref, q2_ref, mod_ref, w_ref, v_ref, s_ref) = refs[:count], refs[count:]
    normed = norm_rows(stacked(chunks), mod_ref, 1)
    q = stacked((q_ref, q2_ref))
    key_scores(jnp.concatenate([q, q], axis=0), normed, w_ref, s_ref)
    project(normed, w_ref, 2, v_ref)


def bin_attend_kernel(groups, dims, z_ref, last_ref, *refs):
    own, refs = refs[:groups], refs[groups:]
    q2_ref, mod_ref, w_ref, wo_ref, v1_ref, s1_ref, v2_ref, s2_ref, v3_ref, s3_ref = refs[:-1]
    out_ref = refs[-1]
    n, m = s2_ref.shape[0], s1_ref.shape[0]
    normed = norm_rows(last_ref[...].astype(F32), mod_ref, 1)
    k = jnp.dot(normed, w_ref[:, D : 2 * D], preferred_element_type=F32).astype(BF).astype(F32)
    s4 = jnp.dot(
        (q2_ref[...].astype(F32) * k).astype(BF), head_lanes((D, 128), 0),
        preferred_element_type=F32,
    )
    v4 = jnp.dot(normed, w_ref[:, 2 * D :], preferred_element_type=F32)

    def of_bins(one, two, three, four):
        return [
            jnp.concatenate([one, two[m:]], axis=0),
            three[:n],
            jnp.concatenate([two[:m], three[n + m :]], axis=0),
            jnp.concatenate([three[n : n + m], four], axis=0),
        ]

    scores = of_bins(s1_ref[...], s2_ref[...], s3_ref[...], s4)
    values = of_bins(*(r[...].astype(F32) for r in (v1_ref, v2_ref, v3_ref)), v4)
    top = functools.reduce(jnp.maximum, scores)
    exps = [jnp.exp(s - top) for s in scores]
    scale = 1.0 / functools.reduce(jnp.add, exps)
    spread = head_lanes((128, D), 1)
    c = None
    for e, v in zip(exps, values):
        p = jnp.dot((e * scale).astype(BF), spread, preferred_element_type=F32)
        part = p * v
        c = part if c is None else c + part
    out = jnp.dot(c.astype(BF), wo_ref[...], preferred_element_type=F32)
    out = (stacked(own) + out).astype(BF)
    put = token_rows(dims, own[0].shape[0], (out_ref.shape[0], n), z_ref[0])
    out_ref[...] = jnp.dot(put, out, preferred_element_type=F32).astype(BF)


def call(kernel, outs, scratch, *args, cost=10**6):
    def space(a):
        return pl.BlockSpec(memory_space=pltpu.SMEM if a.dtype == jnp.int32 else pltpu.VMEM)

    return pl.pallas_call(
        kernel,
        out_shape=[jax.ShapeDtypeStruct(*o) for o in outs],
        in_specs=[space(a) for a in args],
        out_specs=[pl.BlockSpec(memory_space=pltpu.VMEM)] * len(outs),
        scratch_shapes=[pltpu.VMEM(*s) for s in scratch],
        compiler_params=pltpu.CompilerParams(vmem_limit_bytes=24 * 1024 * 1024),
        cost_estimate=pl.CostEstimate(flops=cost, bytes_accessed=cost // 1000, transcendentals=0),
    )(*args)


def column_path(tokens, timestep, mod_weight, col_qkv, col_out, bin_qkv, bin_out):
    rows, width = tokens.shape[1], tokens.shape[2]
    owners = lax.axis_size("seq")
    groups = owners // 2
    cols = width // groups
    dims = (rows, cols, width)
    pad = -(-rows * cols // 8) * 8
    n = rows * width

    def over_group(x, m):
        return lax.ppermute(x, "seq", [(i, i ^ (2 * partner(m, groups))) for i in range(owners)])

    def over_pair(x):
        return lax.ppermute(x, "seq", [(i, i ^ 1) for i in range(owners)])

    def over_bin(x, m):
        return lax.ppermute(x, "bin", [(i, i ^ m) for i in range(4)])

    message, full = ((pad, D), BF), ((n, D), BF)
    z = (lax.axis_index("seq") // 2).astype(jnp.int32).reshape(1)
    flat = tokens.reshape(rows * width, D)
    sent = call(
        functools.partial(pack_kernel, dims), [message] * groups, [], z, flat, cost=10**10
    )
    mod = modulation(timestep, mod_weight).reshape(4, D)
    own = [sent[0]] + [over_group(sent[m], m) for m in range(1, groups)]
    own[1], mod = lax.optimization_barrier((own[1], mod))
    other = [over_pair(x) for x in own]

    t, q, k, v = call(
        functools.partial(col_own_kernel, groups, dims), [full] * 4, [], *own, mod, col_qkv
    )
    sent = call(
        functools.partial(col_attend_kernel, groups, dims), [message] * groups, [full] * 3,
        *other, mod, col_qkv, col_out, t, q, k, v,
    )
    h = [sent[0]] + [over_group(sent[m], m) for m in range(1, groups)]
    hy = [over_bin(x, 2) for x in h]

    def rows_of(count):
        return [((count, D), BF), ((count, 128), F32)]

    padded, early = groups * pad, (groups - 1) * pad
    parts = [((padded // 2, D), BF), ((early - padded // 2, D), BF)]
    q, v1, s1, *h_parts = call(
        functools.partial(bin_own_kernel, groups - 1),
        [((early, D), BF), *rows_of(early), ((early, D), BF)], [], *h[:-1], mod, bin_qkv,
    )
    hc = [over_bin(x, 1) for x in (*h_parts, h[-1])]
    q2, v2, s2, *hy_parts = call(
        functools.partial(bin_early_kernel, groups - 1), [message, *rows_of(padded), *parts], [],
        h[-1], *hy[:-1], q, mod, bin_qkv,
    )
    hd_early = [over_bin(x, 1) for x in hy_parts]
    last, v2 = lax.optimization_barrier((hy[-1], v2))
    hd = over_bin(last, 1)
    others = [*hc, *hd_early, last]
    v3, s3 = call(
        functools.partial(bin_late_kernel, len(others)), rows_of(2 * padded), [],
        *others, q, q2, mod, bin_qkv,
    )
    (out,) = call(
        functools.partial(bin_attend_kernel, groups, dims), [full], [],
        z, hd, *h, q2, mod, bin_qkv, bin_out, v1, s1, v2, s2, v3, s3,
    )
    return out.reshape(tokens.shape)


def layer_norm(values, shift, scale):
    xf = values.astype(jnp.float32)
    mean = jnp.mean(xf, axis=-1, keepdims=True)
    var = jnp.mean((xf - mean) ** 2, axis=-1, keepdims=True)
    return ((xf - mean) * lax.rsqrt(var + 1e-06) * (1.0 + scale) + shift).astype(jnp.bfloat16)


def across_bins(query, key, value):
    scores = jnp.sum(
        query.astype(jnp.float32)[:, None] * key.astype(jnp.float32)[None], axis=-1
    ) * HD ** (-0.5)
    weights = jax.nn.softmax(scores, axis=1).astype(jnp.bfloat16)
    context = jnp.sum(
        weights.astype(jnp.float32)[..., None] * value.astype(jnp.float32)[None], axis=1
    )
    return context.astype(jnp.bfloat16)


def general_path(tokens, timestep, mod_weight, col_qkv, col_out, bin_qkv, bin_out):
    mod = modulation(timestep, mod_weight)
    shift1, scale1, shift2, scale2 = (mod[:D], mod[D : 2 * D], mod[2 * D : 3 * D], mod[3 * D :])
    rows_here = tokens.shape[1]
    width_all = tokens.shape[2]
    owners = lax.axis_size("seq")
    cols_each = width_all // owners
    normed1 = layer_norm(tokens, shift1, scale1)
    grouped = normed1.reshape(1, rows_here, owners, cols_each, D)
    query_weight = col_qkv[:, :D].reshape(D, HEADS, HD)
    key_weight = col_qkv[:, D : 2 * D].reshape(D, HEADS, HD)
    value_weight = col_qkv[:, 2 * D :].reshape(D, HEADS, HD)
    out_weight = col_out.reshape(HEADS, HD, D)
    piece = lax.all_to_all(grouped, "seq", split_axis=2, concat_axis=1, tiled=True)
    height = piece.shape[1]
    count = piece.shape[3]
    local = piece[0, :, 0]
    query = jnp.einsum(
        "iwc,chd->whid", local, query_weight, preferred_element_type=jnp.float32
    ).astype(jnp.bfloat16)
    key = jnp.einsum("iwc,chd->whid", local, key_weight, preferred_element_type=jnp.float32).astype(
        jnp.bfloat16
    )
    value = jnp.einsum(
        "iwc,chd->whid", local, value_weight, preferred_element_type=jnp.float32
    ).astype(jnp.bfloat16)
    scores = jnp.einsum("whid,whjd->whij", query, key, preferred_element_type=jnp.float32) * HD ** (
        -0.5
    )
    weights = jax.nn.softmax(scores, axis=-1).astype(jnp.bfloat16)
    context = jnp.einsum(
        "whij,whjd->whid", weights, value, preferred_element_type=jnp.float32
    ).astype(jnp.bfloat16)
    out = jnp.einsum(
        "whid,hde->iwe", context, out_weight, preferred_element_type=jnp.float32
    ).astype(jnp.bfloat16)
    attended = out.reshape(1, height, 1, count, D)
    back = lax.all_to_all(attended, "seq", split_axis=1, concat_axis=2, tiled=True)
    back = back.reshape(1, rows_here, width_all, D)
    hidden = (tokens.astype(jnp.float32) + back.astype(jnp.float32)).astype(jnp.bfloat16)
    normed2 = layer_norm(hidden, shift2, scale2)
    flat = normed2.reshape(-1, D)
    positions = flat.shape[0]
    every = lax.all_gather(normed2, "bin", axis=0, tiled=True)
    nbins = every.shape[0]
    every_flat = every.reshape(-1, D)
    query = jnp.dot(flat, bin_qkv[:, :D], preferred_element_type=jnp.float32).astype(jnp.bfloat16)
    keys_all = jnp.dot(
        every_flat, bin_qkv[:, D : 2 * D], preferred_element_type=jnp.float32
    ).astype(jnp.bfloat16)
    values_all = jnp.dot(
        every_flat, bin_qkv[:, 2 * D :], preferred_element_type=jnp.float32
    ).astype(jnp.bfloat16)
    context = across_bins(
        query.reshape(1, positions, HEADS, HD),
        keys_all.reshape(nbins, positions, HEADS, HD),
        values_all.reshape(nbins, positions, HEADS, HD),
    )
    projected = jnp.dot(context.reshape(-1, D), bin_out, preferred_element_type=jnp.float32)
    projected = projected.reshape(1, rows_here, width_all, D)
    return (hidden.astype(jnp.float32) + projected).astype(jnp.bfloat16)


def per_device(tokens, *rest):
    owners, width = lax.axis_size("seq"), tokens.shape[2]
    small = owners in (4, 8) and width % owners == 0 and lax.axis_size("bin") == 4
    if small and tokens.shape[1] * owners % 16 == 0 and tokens.shape[1] * width <= 256:
        return column_path(tokens, *rest)
    return general_path(tokens, *rest)


def solution(mesh):
    placed = (P("bin", "seq", None, None), P(), P(), P(), P(), P(), P())
    return jax.shard_map(
        per_device,
        mesh=mesh,
        in_specs=placed,
        out_specs=P("bin", "seq", None, None),
        check_vma=False,
    )
```

```python
import functools
import math

import jax
import jax.numpy as jnp
from jax import lax
from jax.experimental import pallas as pl
from jax.experimental.pallas import tpu as pltpu
from jax.sharding import PartitionSpec as P

D = 768
HEADS = 12
HD = 64
FREQ = 256
PAIR = 2 * HD
ORDER = (0, 1, 2, 3)
RETURN = (0, 1, 3, 2)
BF = jnp.bfloat16
F32 = jnp.float32


def modulation(timestep, mod_weight):
    half = FREQ // 2
    freqs = jnp.exp(-math.log(10000.0) * jnp.arange(half, dtype=jnp.float32) / half)
    angle = timestep.astype(jnp.float32)[0] * freqs
    emb = jax.nn.silu(jnp.concatenate([jnp.cos(angle), jnp.sin(angle)])).astype(jnp.bfloat16)
    return jnp.dot(emb[None, :], mod_weight, preferred_element_type=jnp.float32)[0]


def norm_rows(xf, mod_ref, which):
    shift = mod_ref[2 * which : 2 * which + 1, :]
    scale = mod_ref[2 * which + 1 : 2 * which + 2, :]
    mean = jnp.mean(xf, axis=-1, keepdims=True)
    cent = xf - mean
    var = jnp.mean(cent * cent, axis=-1, keepdims=True)
    return (cent * lax.rsqrt(var + 1e-06) * (1.0 + scale) + shift).astype(BF)


def stacked(refs):
    return jnp.concatenate([r[...].astype(F32) for r in refs], axis=0)


def project(normed, w_ref, which, out_ref, factor=None):
    y = jnp.dot(normed, w_ref[:, which * D : (which + 1) * D], preferred_element_type=F32)
    if factor is not None:
        y = y * factor
    out_ref[...] = y.astype(BF)


def divided(values, by, top):
    total = jnp.zeros_like(values)
    for step in range(by, top, by):
        total = total + (values >= step).astype(jnp.int32)
    return total


def partner(m, groups):
    return ORDER[m] if groups == len(ORDER) else m


def message_rows(shape, row_dim, token_dim, rows, cols, width, owner):
    r = lax.broadcasted_iota(jnp.int32, shape, row_dim)
    t = lax.broadcasted_iota(jnp.int32, shape, token_dim)
    i = divided(r, cols, shape[row_dim])
    source = i * width + owner * cols + (r - i * cols)
    hit = (r < rows * cols) & (t == source)
    return jnp.where(hit, 1.0, 0.0).astype(BF)


def pack_kernel(dims, z_ref, tok_ref, *out_refs):
    rows, cols, width = dims
    x = tok_ref[...]
    for m, out in enumerate(out_refs):
        shape = (out.shape[0], x.shape[0])
        pick = message_rows(shape, 0, 1, rows, cols, width, z_ref[0] ^ partner(m, len(out_refs)))
        out[...] = jnp.dot(pick, x, preferred_element_type=F32).astype(BF)


def token_rows(dims, pad, shape, z):
    rows, cols, width = dims
    r = lax.broadcasted_iota(jnp.int32, (1, shape[1]), 1)
    m = divided(r, pad, shape[1])
    r = r - m * pad
    i = divided(r, cols, pad)
    groups = shape[1] // pad
    back = RETURN if groups == len(RETURN) else range(groups)
    differs = sum(jnp.where(m == k, back[k], 0) for k in range(groups))
    source = i * width + (z ^ differs) * cols + (r - i * cols)
    source = jnp.where(r < rows * cols, source, -1)
    return jnp.where(source == lax.broadcasted_iota(jnp.int32, shape, 0), 1.0, 0.0).astype(BF)


def grouped_rows(dims, groups, pad, shape, row_dim):
    rows, cols, _ = dims
    flat = (shape[0], 1) if row_dim == 0 else (1, shape[1])
    r = lax.broadcasted_iota(jnp.int32, flat, row_dim)
    part, here = groups * rows * 2, rows * 2
    g = divided(r, part, shape[row_dim])
    r = r - g * part
    m = divided(r, here, part)
    r = r - m * here
    i = divided(r, 2, here)
    source = m * pad + i * cols + 2 * g + (r - 2 * i)
    hit = source == lax.broadcasted_iota(jnp.int32, shape, 1 - row_dim)
    return jnp.where(hit, 1.0, 0.0).astype(BF)


def column_marks(n, keys):
    def odd(count):
        return lax.broadcasted_iota(jnp.int32, (count, PAIR), 0) & 1

    lane = lax.broadcasted_iota(jnp.int32, (n, PAIR), 1)
    query = jnp.where(lane == odd(n), 1.0, 0.0).astype(BF)
    lane = lax.broadcasted_iota(jnp.int32, (keys, PAIR), 1)
    return query, jnp.where(lane == odd(keys), 0.0, -(2.0**100)).astype(BF)


def head_pair(q):
    low = lax.broadcasted_iota(jnp.int32, q.shape, 1) < HD
    zero = jnp.zeros_like(q)
    return jnp.concatenate([jnp.where(low, q, zero), jnp.where(low, zero, q)], axis=0)


def unpaired(c):
    n = c.shape[0] // 2
    low = lax.broadcasted_iota(jnp.int32, (n, PAIR), 1) < HD
    return jnp.where(low, c[:n], c[n:])


def regrouped(refs, dims):
    pad = refs[0].shape[0]
    n = len(refs) * dims[0] * dims[1]
    pick = grouped_rows(dims, len(refs), pad, (n, len(refs) * pad), 0)
    return jnp.dot(pick, stacked(refs).astype(BF), preferred_element_type=F32)


def col_own_kernel(groups, dims, *refs):
    own, (mod_ref, w_ref, t_ref, q_ref, k_ref, v_ref) = refs[:groups], refs[groups:]
    rows = regrouped(own, dims)
    t_ref[...] = rows.astype(BF)
    normed = norm_rows(rows, mod_ref, 0)
    project(normed, w_ref, 0, q_ref, HD**-0.5 * math.log2(math.e))
    project(normed, w_ref, 1, k_ref)
    project(normed, w_ref, 2, v_ref)


def col_attend_kernel(groups, dims, *refs):
    other = refs[:groups]
    mod_ref, w_ref, wo_ref, t_ref, q_ref, k_ref, v_ref, *refs = refs[groups:]
    *outs, k2_ref, v2_ref, c_ref = refs
    normed = norm_rows(regrouped(other, dims), mod_ref, 0)
    project(normed, w_ref, 1, k2_ref)
    project(normed, w_ref, 2, v2_ref)
    part = groups * dims[0] * 2
    q_mark, k_mark = column_marks(2 * part, 2 * part)
    ones = jnp.ones((2 * part, PAIR), BF)
    for g in range(dims[1] // 2):
        here = slice(g * part, (g + 1) * part)
        for j in range(HEADS // 2):
            lanes = slice(j * PAIR, (j + 1) * PAIR)
            q = jnp.concatenate([head_pair(q_ref[here, lanes]), q_mark], axis=1)
            k = jnp.concatenate([k_ref[here, lanes], k2_ref[here, lanes]], axis=0)
            v = jnp.concatenate([v_ref[here, lanes], v2_ref[here, lanes]], axis=0)
            k = jnp.concatenate([k, k_mark], axis=1)
            s = lax.dot_general(q, k, (((1,), (1,)), ((), ())), preferred_element_type=F32)
            e = jnp.exp2((s - jnp.max(s, axis=-1, keepdims=True)).astype(BF))
            c = jnp.dot(e, jnp.concatenate([v, ones], axis=1), preferred_element_type=F32)
            c_ref[here, lanes] = (unpaired(c[:, :PAIR]) / unpaired(c[:, PAIR:])).astype(BF)
    a = jnp.dot(c_ref[...], wo_ref[...], preferred_element_type=F32).astype(BF)
    h = (t_ref[...].astype(F32) + a.astype(F32)).astype(BF)
    pad = outs[0].shape[0]
    put = grouped_rows(dims, groups, pad, (groups * pad, h.shape[0]), 1)
    h = jnp.dot(put, h, preferred_element_type=F32)
    for m, o in enumerate(outs):
        o[...] = h[m * pad : (m + 1) * pad].astype(BF)


def head_lanes(shape, lane_dim):
    lane = lax.broadcasted_iota(jnp.int32, shape, lane_dim)
    head = lax.broadcasted_iota(jnp.int32, shape, 1 - lane_dim)
    return ((lane >= head * HD) & (lane < (head + 1) * HD)).astype(F32).astype(BF)


def key_scores(query, normed, w_ref, s_ref):
    k = jnp.dot(normed, w_ref[:, D : 2 * D], preferred_element_type=F32).astype(BF).astype(F32)
    s_ref[...] = jnp.dot(
        (query * k).astype(BF), head_lanes((D, 128), 0), preferred_element_type=F32
    )


def split_rows(rows, parts):
    start = 0
    for part in parts:
        part[...] = rows[start : start + part.shape[0]].astype(BF)
        start += part.shape[0]


def bin_own_kernel(count, *refs):
    chunks, (mod_ref, w_ref, q_ref, v_ref, s_ref, *parts) = refs[:count], refs[count:]
    rows = stacked(chunks)
    split_rows(rows, parts)
    normed = norm_rows(rows, mod_ref, 1)
    project(normed, w_ref, 0, q_ref, HD**-0.5)
    key_scores(q_ref[...].astype(F32), normed, w_ref, s_ref)
    project(normed, w_ref, 2, v_ref)


def bin_early_kernel(count, own_ref, *refs):
    chunks, (q_ref, mod_ref, w_ref, q2_ref, v_ref, s_ref, *parts) = refs[:count], refs[count:]
    rows = stacked(chunks)
    split_rows(rows, parts)
    rows = jnp.concatenate([rows, own_ref[...].astype(F32)], axis=0)
    normed = norm_rows(rows, mod_ref, 1)
    split = q_ref.shape[0]
    q2 = jnp.dot(normed, w_ref[:, :D], preferred_element_type=F32)[split:] * HD**-0.5
    q2_ref[...] = q2.astype(BF)
    query = jnp.concatenate([q_ref[...].astype(F32), q2_ref[...].astype(F32)], axis=0)
    key_scores(query, normed, w_ref, s_ref)
    project(normed, w_ref, 2, v_ref)


def bin_late_kernel(count, *refs):
    chunks, (q_ref, q2_ref, mod_ref, w_ref, v_ref, s_ref) = refs[:count], refs[count:]
    normed = norm_rows(stacked(chunks), mod_ref, 1)
    q = stacked((q_ref, q2_ref))
    key_scores(jnp.concatenate([q, q], axis=0), normed, w_ref, s_ref)
    project(normed, w_ref, 2, v_ref)


def bin_attend_kernel(groups, dims, z_ref, last_ref, *refs):
    own, refs = refs[:groups], refs[groups:]
    q2_ref, mod_ref, w_ref, wo_ref, v1_ref, s1_ref, v2_ref, s2_ref, v3_ref, s3_ref = refs[:-1]
    out_ref = refs[-1]
    n, m = s2_ref.shape[0], s1_ref.shape[0]
    normed = norm_rows(last_ref[...].astype(F32), mod_ref, 1)
    k = jnp.dot(normed, w_ref[:, D : 2 * D], preferred_element_type=F32).astype(BF).astype(F32)
    s4 = jnp.dot(
        (q2_ref[...].astype(F32) * k).astype(BF), head_lanes((D, 128), 0),
        preferred_element_type=F32,
    )
    v4 = jnp.dot(normed, w_ref[:, 2 * D :], preferred_element_type=F32)

    def of_bins(one, two, three, four):
        return [
            jnp.concatenate([one, two[m:]], axis=0),
            three[:n],
            jnp.concatenate([two[:m], three[n + m :]], axis=0),
            jnp.concatenate([three[n : n + m], four], axis=0),
        ]

    scores = of_bins(s1_ref[...], s2_ref[...], s3_ref[...], s4)
    values = of_bins(*(r[...].astype(F32) for r in (v1_ref, v2_ref, v3_ref)), v4)
    top = functools.reduce(jnp.maximum, scores)
    exps = [jnp.exp(s - top) for s in scores]
    scale = 1.0 / functools.reduce(jnp.add, exps)
    spread = head_lanes((128, D), 1)
    c = None
    for e, v in zip(exps, values):
        p = jnp.dot((e * scale).astype(BF), spread, preferred_element_type=F32)
        part = p * v
        c = part if c is None else c + part
    out = jnp.dot(c.astype(BF), wo_ref[...], preferred_element_type=F32)
    out = (stacked(own) + out).astype(BF)
    put = token_rows(dims, own[0].shape[0], (out_ref.shape[0], n), z_ref[0])
    out_ref[...] = jnp.dot(put, out, preferred_element_type=F32).astype(BF)


def call(kernel, outs, scratch, *args, cost=10**6):
    def space(a):
        return pl.BlockSpec(memory_space=pltpu.SMEM if a.dtype == jnp.int32 else pltpu.VMEM)

    return pl.pallas_call(
        kernel,
        out_shape=[jax.ShapeDtypeStruct(*o) for o in outs],
        in_specs=[space(a) for a in args],
        out_specs=[pl.BlockSpec(memory_space=pltpu.VMEM)] * len(outs),
        scratch_shapes=[pltpu.VMEM(*s) for s in scratch],
        compiler_params=pltpu.CompilerParams(vmem_limit_bytes=24 * 1024 * 1024),
        cost_estimate=pl.CostEstimate(flops=cost, bytes_accessed=cost // 1000, transcendentals=0),
    )(*args)


def column_path(tokens, timestep, mod_weight, col_qkv, col_out, bin_qkv, bin_out):
    rows, width = tokens.shape[1], tokens.shape[2]
    owners = lax.axis_size("seq")
    groups = owners // 2
    cols = width // groups
    dims = (rows, cols, width)
    pad = -(-rows * cols // 8) * 8
    n = rows * width

    def over_group(x, m):
        return lax.ppermute(x, "seq", [(i, i ^ (2 * partner(m, groups))) for i in range(owners)])

    def over_pair(x):
        return lax.ppermute(x, "seq", [(i, i ^ 1) for i in range(owners)])

    def over_bin(x, m):
        return lax.ppermute(x, "bin", [(i, i ^ m) for i in range(4)])

    message, full = ((pad, D), BF), ((n, D), BF)
    z = (lax.axis_index("seq") // 2).astype(jnp.int32).reshape(1)
    flat = tokens.reshape(rows * width, D)
    sent = call(
        functools.partial(pack_kernel, dims), [message] * groups, [], z, flat, cost=10**10
    )
    mod = modulation(timestep, mod_weight).reshape(4, D)
    own = [sent[0]] + [over_group(sent[m], m) for m in range(1, groups)]
    own[1], mod = lax.optimization_barrier((own[1], mod))
    other = [over_pair(x) for x in own]

    t, q, k, v = call(
        functools.partial(col_own_kernel, groups, dims), [full] * 4, [], *own, mod, col_qkv
    )
    sent = call(
        functools.partial(col_attend_kernel, groups, dims), [message] * groups, [full] * 3,
        *other, mod, col_qkv, col_out, t, q, k, v,
    )
    back = RETURN if groups == len(RETURN) else range(groups)
    places = [partner(m, groups) for m in range(groups)]
    places = [places.index(far) for far in back]
    h = [sent[0]] + [over_group(sent[m], m) for m in places[1:]]
    hy = [over_bin(x, 2) for x in h]

    def rows_of(count):
        return [((count, D), BF), ((count, 128), F32)]

    padded, early = groups * pad, (groups - 1) * pad
    parts = [((padded // 2, D), BF), ((early - padded // 2, D), BF)]
    q, v1, s1, *h_parts = call(
        functools.partial(bin_own_kernel, groups - 1),
        [((early, D), BF), *rows_of(early), ((early, D), BF)], [], *h[:-1], mod, bin_qkv,
    )
    hc = [over_bin(x, 1) for x in (*h_parts, h[-1])]
    q2, v2, s2, *hy_parts = call(
        functools.partial(bin_early_kernel, groups - 1), [message, *rows_of(padded), *parts], [],
        h[-1], *hy[:-1], q, mod, bin_qkv,
    )
    hd_early = [over_bin(x, 1) for x in hy_parts]
    last, v2 = lax.optimization_barrier((hy[-1], v2))
    hd = over_bin(last, 1)
    others = [*hc, *hd_early, last]
    v3, s3 = call(
        functools.partial(bin_late_kernel, len(others)), rows_of(2 * padded), [],
        *others, q, q2, mod, bin_qkv,
    )
    (out,) = call(
        functools.partial(bin_attend_kernel, groups, dims), [full], [],
        z, hd, *h, q2, mod, bin_qkv, bin_out, v1, s1, v2, s2, v3, s3,
    )
    return out.reshape(tokens.shape)


def layer_norm(values, shift, scale):
    xf = values.astype(jnp.float32)
    mean = jnp.mean(xf, axis=-1, keepdims=True)
    var = jnp.mean((xf - mean) ** 2, axis=-1, keepdims=True)
    return ((xf - mean) * lax.rsqrt(var + 1e-06) * (1.0 + scale) + shift).astype(jnp.bfloat16)


def across_bins(query, key, value):
    scores = jnp.sum(
        query.astype(jnp.float32)[:, None] * key.astype(jnp.float32)[None], axis=-1
    ) * HD ** (-0.5)
    weights = jax.nn.softmax(scores, axis=1).astype(jnp.bfloat16)
    context = jnp.sum(
        weights.astype(jnp.float32)[..., None] * value.astype(jnp.float32)[None], axis=1
    )
    return context.astype(jnp.bfloat16)


def general_path(tokens, timestep, mod_weight, col_qkv, col_out, bin_qkv, bin_out):
    mod = modulation(timestep, mod_weight)
    shift1, scale1, shift2, scale2 = (mod[:D], mod[D : 2 * D], mod[2 * D : 3 * D], mod[3 * D :])
    rows_here = tokens.shape[1]
    width_all = tokens.shape[2]
    owners = lax.axis_size("seq")
    cols_each = width_all // owners
    normed1 = layer_norm(tokens, shift1, scale1)
    grouped = normed1.reshape(1, rows_here, owners, cols_each, D)
    query_weight = col_qkv[:, :D].reshape(D, HEADS, HD)
    key_weight = col_qkv[:, D : 2 * D].reshape(D, HEADS, HD)
    value_weight = col_qkv[:, 2 * D :].reshape(D, HEADS, HD)
    out_weight = col_out.reshape(HEADS, HD, D)
    piece = lax.all_to_all(grouped, "seq", split_axis=2, concat_axis=1, tiled=True)
    height = piece.shape[1]
    count = piece.shape[3]
    local = piece[0, :, 0]
    query = jnp.einsum(
        "iwc,chd->whid", local, query_weight, preferred_element_type=jnp.float32
    ).astype(jnp.bfloat16)
    key = jnp.einsum("iwc,chd->whid", local, key_weight, preferred_element_type=jnp.float32).astype(
        jnp.bfloat16
    )
    value = jnp.einsum(
        "iwc,chd->whid", local, value_weight, preferred_element_type=jnp.float32
    ).astype(jnp.bfloat16)
    scores = jnp.einsum("whid,whjd->whij", query, key, preferred_element_type=jnp.float32) * HD ** (
        -0.5
    )
    weights = jax.nn.softmax(scores, axis=-1).astype(jnp.bfloat16)
    context = jnp.einsum(
        "whij,whjd->whid", weights, value, preferred_element_type=jnp.float32
    ).astype(jnp.bfloat16)
    out = jnp.einsum(
        "whid,hde->iwe", context, out_weight, preferred_element_type=jnp.float32
    ).astype(jnp.bfloat16)
    attended = out.reshape(1, height, 1, count, D)
    back = lax.all_to_all(attended, "seq", split_axis=1, concat_axis=2, tiled=True)
    back = back.reshape(1, rows_here, width_all, D)
    hidden = (tokens.astype(jnp.float32) + back.astype(jnp.float32)).astype(jnp.bfloat16)
    normed2 = layer_norm(hidden, shift2, scale2)
    flat = normed2.reshape(-1, D)
    positions = flat.shape[0]
    every = lax.all_gather(normed2, "bin", axis=0, tiled=True)
    nbins = every.shape[0]
    every_flat = every.reshape(-1, D)
    query = jnp.dot(flat, bin_qkv[:, :D], preferred_element_type=jnp.float32).astype(jnp.bfloat16)
    keys_all = jnp.dot(
        every_flat, bin_qkv[:, D : 2 * D], preferred_element_type=jnp.float32
    ).astype(jnp.bfloat16)
    values_all = jnp.dot(
        every_flat, bin_qkv[:, 2 * D :], preferred_element_type=jnp.float32
    ).astype(jnp.bfloat16)
    context = across_bins(
        query.reshape(1, positions, HEADS, HD),
        keys_all.reshape(nbins, positions, HEADS, HD),
        values_all.reshape(nbins, positions, HEADS, HD),
    )
    projected = jnp.dot(context.reshape(-1, D), bin_out, preferred_element_type=jnp.float32)
    projected = projected.reshape(1, rows_here, width_all, D)
    return (hidden.astype(jnp.float32) + projected).astype(jnp.bfloat16)


def per_device(tokens, *rest):
    owners, width = lax.axis_size("seq"), tokens.shape[2]
    small = owners in (4, 8) and width % owners == 0 and lax.axis_size("bin") == 4
    if small and tokens.shape[1] * owners % 16 == 0 and tokens.shape[1] * width <= 256:
        return column_path(tokens, *rest)
    return general_path(tokens, *rest)


def solution(mesh):
    placed = (P("bin", "seq", None, None), P(), P(), P(), P(), P(), P())
    return jax.shard_map(
        per_device,
        mesh=mesh,
        in_specs=placed,
        out_specs=P("bin", "seq", None, None),
        check_vma=False,
    )
```

```python
import functools
import math

import jax
import jax.numpy as jnp
from jax import lax
from jax.experimental import pallas as pl
from jax.experimental.pallas import tpu as pltpu
from jax.sharding import PartitionSpec as P

D = 768
HEADS = 12
HD = 64
FREQ = 256
PAIR = 2 * HD
ORDER = (0, 1, 2, 3)
RETURN = (0, 1, 3, 2)
BF = jnp.bfloat16
F32 = jnp.float32


def modulation(timestep, mod_weight):
    half = FREQ // 2
    freqs = jnp.exp(-math.log(10000.0) * jnp.arange(half, dtype=jnp.float32) / half)
    angle = timestep.astype(jnp.float32)[0] * freqs
    emb = jax.nn.silu(jnp.concatenate([jnp.cos(angle), jnp.sin(angle)])).astype(jnp.bfloat16)
    return jnp.dot(emb[None, :], mod_weight, preferred_element_type=jnp.float32)[0]


def norm_rows(xf, mod_ref, which):
    shift = mod_ref[2 * which : 2 * which + 1, :]
    scale = mod_ref[2 * which + 1 : 2 * which + 2, :]
    mean = jnp.mean(xf, axis=-1, keepdims=True)
    cent = xf - mean
    var = jnp.mean(cent * cent, axis=-1, keepdims=True)
    return (cent * lax.rsqrt(var + 1e-06) * (1.0 + scale) + shift).astype(BF)


def stacked(refs):
    return jnp.concatenate([r[...].astype(F32) for r in refs], axis=0)


def project(normed, w_ref, which, out_ref, factor=None):
    y = jnp.dot(normed, w_ref[:, which * D : (which + 1) * D], preferred_element_type=F32)
    if factor is not None:
        y = y * factor
    out_ref[...] = y.astype(BF)


def divided(values, by, top):
    total = jnp.zeros_like(values)
    for step in range(by, top, by):
        total = total + (values >= step).astype(jnp.int32)
    return total


def partner(m, groups):
    return ORDER[m] if groups == len(ORDER) else m


def message_rows(shape, row_dim, token_dim, rows, cols, width, owner):
    r = lax.broadcasted_iota(jnp.int32, shape, row_dim)
    t = lax.broadcasted_iota(jnp.int32, shape, token_dim)
    i = divided(r, cols, shape[row_dim])
    source = i * width + owner * cols + (r - i * cols)
    hit = (r < rows * cols) & (t == source)
    return jnp.where(hit, 1.0, 0.0).astype(BF)


def pack_kernel(dims, z_ref, tok_ref, *out_refs):
    rows, cols, width = dims
    x = tok_ref[...]
    for m, out in enumerate(out_refs):
        shape = (out.shape[0], x.shape[0])
        pick = message_rows(shape, 0, 1, rows, cols, width, z_ref[0] ^ partner(m, len(out_refs)))
        out[...] = jnp.dot(pick, x, preferred_element_type=F32).astype(BF)


def token_rows(dims, pad, shape, z):
    rows, cols, width = dims
    r = lax.broadcasted_iota(jnp.int32, (1, shape[1]), 1)
    m = divided(r, pad, shape[1])
    r = r - m * pad
    i = divided(r, cols, pad)
    groups = shape[1] // pad
    back = RETURN if groups == len(RETURN) else range(groups)
    differs = sum(jnp.where(m == k, back[k], 0) for k in range(groups))
    source = i * width + (z ^ differs) * cols + (r - i * cols)
    source = jnp.where(r < rows * cols, source, -1)
    return jnp.where(source == lax.broadcasted_iota(jnp.int32, shape, 0), 1.0, 0.0).astype(BF)


def grouped_rows(dims, groups, pad, shape, row_dim):
    rows, cols, _ = dims
    flat = (shape[0], 1) if row_dim == 0 else (1, shape[1])
    r = lax.broadcasted_iota(jnp.int32, flat, row_dim)
    part, here = groups * rows * 2, rows * 2
    g = divided(r, part, shape[row_dim])
    r = r - g * part
    m = divided(r, here, part)
    r = r - m * here
    i = divided(r, 2, here)
    source = m * pad + i * cols + 2 * g + (r - 2 * i)
    hit = source == lax.broadcasted_iota(jnp.int32, shape, 1 - row_dim)
    return jnp.where(hit, 1.0, 0.0).astype(BF)


def column_marks(n, keys):
    def odd(count):
        return lax.broadcasted_iota(jnp.int32, (count, PAIR), 0) & 1

    lane = lax.broadcasted_iota(jnp.int32, (n, PAIR), 1)
    query = jnp.where(lane == odd(n), 1.0, 0.0).astype(BF)
    lane = lax.broadcasted_iota(jnp.int32, (keys, PAIR), 1)
    return query, jnp.where(lane == odd(keys), 0.0, -(2.0**100)).astype(BF)


def head_pair(q):
    low = lax.broadcasted_iota(jnp.int32, q.shape, 1) < HD
    zero = jnp.zeros_like(q)
    return jnp.concatenate([jnp.where(low, q, zero), jnp.where(low, zero, q)], axis=0)


def unpaired(c):
    n = c.shape[0] // 2
    low = lax.broadcasted_iota(jnp.int32, (n, PAIR), 1) < HD
    return jnp.where(low, c[:n], c[n:])


def regrouped(refs, dims):
    pad = refs[0].shape[0]
    n = len(refs) * dims[0] * dims[1]
    pick = grouped_rows(dims, len(refs), pad, (n, len(refs) * pad), 0)
    return jnp.dot(pick, stacked(refs).astype(BF), preferred_element_type=F32)


def col_own_kernel(groups, dims, *refs):
    own, (mod_ref, w_ref, t_ref, q_ref, k_ref, v_ref) = refs[:groups], refs[groups:]
    rows = regrouped(own, dims)
    t_ref[...] = rows.astype(BF)
    normed = norm_rows(rows, mod_ref, 0)
    project(normed, w_ref, 0, q_ref, HD**-0.5 * math.log2(math.e))
    project(normed, w_ref, 1, k_ref)
    project(normed, w_ref, 2, v_ref)


def col_attend_kernel(groups, dims, *refs):
    other = refs[:groups]
    mod_ref, w_ref, wo_ref, t_ref, q_ref, k_ref, v_ref, *refs = refs[groups:]
    *outs, k2_ref, v2_ref, c_ref = refs
    normed = norm_rows(regrouped(other, dims), mod_ref, 0)
    project(normed, w_ref, 1, k2_ref)
    project(normed, w_ref, 2, v2_ref)
    part = groups * dims[0] * 2
    q_mark, k_mark = column_marks(2 * part, 2 * part)
    ones = jnp.ones((2 * part, PAIR), BF)
    for g in range(dims[1] // 2):
        here = slice(g * part, (g + 1) * part)
        for j in range(HEADS // 2):
            lanes = slice(j * PAIR, (j + 1) * PAIR)
            q = jnp.concatenate([head_pair(q_ref[here, lanes]), q_mark], axis=1)
            k = jnp.concatenate([k_ref[here, lanes], k2_ref[here, lanes]], axis=0)
            v = jnp.concatenate([v_ref[here, lanes], v2_ref[here, lanes]], axis=0)
            k = jnp.concatenate([k, k_mark], axis=1)
            s = lax.dot_general(q, k, (((1,), (1,)), ((), ())), preferred_element_type=F32)
            e = jnp.exp2((s - jnp.max(s, axis=-1, keepdims=True)).astype(BF))
            c = jnp.dot(e, jnp.concatenate([v, ones], axis=1), preferred_element_type=F32)
            c_ref[here, lanes] = (unpaired(c[:, :PAIR]) / unpaired(c[:, PAIR:])).astype(BF)
    a = jnp.dot(c_ref[...], wo_ref[...], preferred_element_type=F32).astype(BF)
    h = (t_ref[...].astype(F32) + a.astype(F32)).astype(BF)
    pad = outs[0].shape[0]
    put = grouped_rows(dims, groups, pad, (groups * pad, h.shape[0]), 1)
    h = jnp.dot(put, h, preferred_element_type=F32)
    for m, o in enumerate(outs):
        o[...] = h[m * pad : (m + 1) * pad].astype(BF)


def head_lanes(shape, lane_dim):
    lane = lax.broadcasted_iota(jnp.int32, shape, lane_dim)
    head = lax.broadcasted_iota(jnp.int32, shape, 1 - lane_dim)
    return ((lane >= head * HD) & (lane < (head + 1) * HD)).astype(F32).astype(BF)


def key_scores(query, normed, w_ref, s_ref):
    k = jnp.dot(normed, w_ref[:, D : 2 * D], preferred_element_type=F32).astype(BF).astype(F32)
    s_ref[...] = jnp.dot(
        (query * k).astype(BF), head_lanes((D, 128), 0), preferred_element_type=F32
    )


def split_rows(rows, parts):
    start = 0
    for part in parts:
        part[...] = rows[start : start + part.shape[0]].astype(BF)
        start += part.shape[0]


def bin_own_kernel(count, *refs):
    chunks, (mod_ref, w_ref, q_ref, v_ref, s_ref, *parts) = refs[:count], refs[count:]
    normed = norm_rows(stacked(chunks), mod_ref, 1)
    split_rows(normed.astype(F32), parts)
    project(normed, w_ref, 0, q_ref, HD**-0.5)
    key_scores(q_ref[...].astype(F32), normed, w_ref, s_ref)
    project(normed, w_ref, 2, v_ref)


def bin_early_kernel(count, own_ref, *refs):
    chunks, (q_ref, mod_ref, w_ref, q2_ref, v_ref, s_ref, *parts) = refs[:count], refs[count:]
    split = q_ref.shape[0]
    normed = norm_rows(stacked((*chunks, own_ref)), mod_ref, 1)
    split_rows(normed.astype(F32)[:split], parts)
    q2 = jnp.dot(normed, w_ref[:, :D], preferred_element_type=F32)[split:] * HD**-0.5
    q2_ref[...] = q2.astype(BF)
    query = jnp.concatenate([q_ref[...].astype(F32), q2_ref[...].astype(F32)], axis=0)
    key_scores(query, normed, w_ref, s_ref)
    project(normed, w_ref, 2, v_ref)


def bin_late_kernel(count, *refs):
    chunks, (q_ref, q2_ref, mod_ref, w_ref, v_ref, s_ref) = refs[:count], refs[count:]
    core_ref, core_last_ref, *far, last_ref = chunks
    fresh = norm_rows(stacked((core_last_ref, last_ref)), mod_ref, 1).astype(F32)
    pad = last_ref.shape[0]
    pieces = [core_ref[...].astype(F32), fresh[:pad], stacked(far), fresh[pad:]]
    normed = jnp.concatenate(pieces, axis=0).astype(BF)
    q = stacked((q_ref, q2_ref))
    key_scores(jnp.concatenate([q, q], axis=0), normed, w_ref, s_ref)
    project(normed, w_ref, 2, v_ref)


def bin_attend_kernel(groups, dims, z_ref, last_ref, *refs):
    own, refs = refs[:groups], refs[groups:]
    q2_ref, mod_ref, w_ref, wo_ref, v1_ref, s1_ref, v2_ref, s2_ref, v3_ref, s3_ref = refs[:-1]
    out_ref = refs[-1]
    n, m = s2_ref.shape[0], s1_ref.shape[0]
    normed = norm_rows(last_ref[...].astype(F32), mod_ref, 1)
    k = jnp.dot(normed, w_ref[:, D : 2 * D], preferred_element_type=F32).astype(BF).astype(F32)
    s4 = jnp.dot(
        (q2_ref[...].astype(F32) * k).astype(BF), head_lanes((D, 128), 0),
        preferred_element_type=F32,
    )
    v4 = jnp.dot(normed, w_ref[:, 2 * D :], preferred_element_type=F32)

    def of_bins(one, two, three, four):
        return [
            jnp.concatenate([one, two[m:]], axis=0),
            three[:n],
            jnp.concatenate([two[:m], three[n + m :]], axis=0),
            jnp.concatenate([three[n : n + m], four], axis=0),
        ]

    scores = of_bins(s1_ref[...], s2_ref[...], s3_ref[...], s4)
    values = of_bins(*(r[...].astype(F32) for r in (v1_ref, v2_ref, v3_ref)), v4)
    top = functools.reduce(jnp.maximum, scores)
    exps = [jnp.exp(s - top) for s in scores]
    scale = 1.0 / functools.reduce(jnp.add, exps)
    spread = head_lanes((128, D), 1)
    c = None
    for e, v in zip(exps, values):
        p = jnp.dot((e * scale).astype(BF), spread, preferred_element_type=F32)
        part = p * v
        c = part if c is None else c + part
    out = jnp.dot(c.astype(BF), wo_ref[...], preferred_element_type=F32)
    out = (stacked(own) + out).astype(BF)
    put = token_rows(dims, own[0].shape[0], (out_ref.shape[0], n), z_ref[0])
    out_ref[...] = jnp.dot(put, out, preferred_element_type=F32).astype(BF)


def call(kernel, outs, scratch, *args, cost=10**6):
    def space(a):
        return pl.BlockSpec(memory_space=pltpu.SMEM if a.dtype == jnp.int32 else pltpu.VMEM)

    return pl.pallas_call(
        kernel,
        out_shape=[jax.ShapeDtypeStruct(*o) for o in outs],
        in_specs=[space(a) for a in args],
        out_specs=[pl.BlockSpec(memory_space=pltpu.VMEM)] * len(outs),
        scratch_shapes=[pltpu.VMEM(*s) for s in scratch],
        compiler_params=pltpu.CompilerParams(vmem_limit_bytes=24 * 1024 * 1024),
        cost_estimate=pl.CostEstimate(flops=cost, bytes_accessed=cost // 1000, transcendentals=0),
    )(*args)


def column_path(tokens, timestep, mod_weight, col_qkv, col_out, bin_qkv, bin_out):
    rows, width = tokens.shape[1], tokens.shape[2]
    owners = lax.axis_size("seq")
    groups = owners // 2
    cols = width // groups
    dims = (rows, cols, width)
    pad = -(-rows * cols // 8) * 8
    n = rows * width

    def over_group(x, m):
        return lax.ppermute(x, "seq", [(i, i ^ (2 * partner(m, groups))) for i in range(owners)])

    def over_pair(x):
        return lax.ppermute(x, "seq", [(i, i ^ 1) for i in range(owners)])

    def over_bin(x, m):
        return lax.ppermute(x, "bin", [(i, i ^ m) for i in range(4)])

    message, full = ((pad, D), BF), ((n, D), BF)
    z = (lax.axis_index("seq") // 2).astype(jnp.int32).reshape(1)
    flat = tokens.reshape(rows * width, D)
    sent = call(
        functools.partial(pack_kernel, dims), [message] * groups, [], z, flat, cost=10**10
    )
    mod = modulation(timestep, mod_weight).reshape(4, D)
    own = [sent[0]] + [over_group(sent[m], m) for m in range(1, groups)]
    own[1], mod = lax.optimization_barrier((own[1], mod))
    other = [over_pair(x) for x in own]

    t, q, k, v = call(
        functools.partial(col_own_kernel, groups, dims), [full] * 4, [], *own, mod, col_qkv
    )
    sent = call(
        functools.partial(col_attend_kernel, groups, dims), [message] * groups, [full] * 3,
        *other, mod, col_qkv, col_out, t, q, k, v,
    )
    back = RETURN if groups == len(RETURN) else range(groups)
    places = [partner(m, groups) for m in range(groups)]
    places = [places.index(far) for far in back]
    h = [sent[0]] + [over_group(sent[m], m) for m in places[1:]]
    hy = [over_bin(x, 2) for x in h]

    def rows_of(count):
        return [((count, D), BF), ((count, 128), F32)]

    padded, early = groups * pad, (groups - 1) * pad
    parts = [((padded // 2, D), BF), ((early - padded // 2, D), BF)]
    q, v1, s1, *h_parts = call(
        functools.partial(bin_own_kernel, groups - 1),
        [((early, D), BF), *rows_of(early), ((early, D), BF)], [], *h[:-1], mod, bin_qkv,
    )
    hc = [over_bin(x, 1) for x in (*h_parts, h[-1])]
    q2, v2, s2, *hy_parts = call(
        functools.partial(bin_early_kernel, groups - 1), [message, *rows_of(padded), *parts], [],
        h[-1], *hy[:-1], q, mod, bin_qkv,
    )
    hd_early = [over_bin(x, 1) for x in hy_parts]
    last, v2 = lax.optimization_barrier((hy[-1], v2))
    hd = over_bin(last, 1)
    others = [*hc, *hd_early, last]
    v3, s3 = call(
        functools.partial(bin_late_kernel, len(others)), rows_of(2 * padded), [],
        *others, q, q2, mod, bin_qkv,
    )
    (out,) = call(
        functools.partial(bin_attend_kernel, groups, dims), [full], [],
        z, hd, *h, q2, mod, bin_qkv, bin_out, v1, s1, v2, s2, v3, s3,
    )
    return out.reshape(tokens.shape)


def layer_norm(values, shift, scale):
    xf = values.astype(jnp.float32)
    mean = jnp.mean(xf, axis=-1, keepdims=True)
    var = jnp.mean((xf - mean) ** 2, axis=-1, keepdims=True)
    return ((xf - mean) * lax.rsqrt(var + 1e-06) * (1.0 + scale) + shift).astype(jnp.bfloat16)


def across_bins(query, key, value):
    scores = jnp.sum(
        query.astype(jnp.float32)[:, None] * key.astype(jnp.float32)[None], axis=-1
    ) * HD ** (-0.5)
    weights = jax.nn.softmax(scores, axis=1).astype(jnp.bfloat16)
    context = jnp.sum(
        weights.astype(jnp.float32)[..., None] * value.astype(jnp.float32)[None], axis=1
    )
    return context.astype(jnp.bfloat16)


def general_path(tokens, timestep, mod_weight, col_qkv, col_out, bin_qkv, bin_out):
    mod = modulation(timestep, mod_weight)
    shift1, scale1, shift2, scale2 = (mod[:D], mod[D : 2 * D], mod[2 * D : 3 * D], mod[3 * D :])
    rows_here = tokens.shape[1]
    width_all = tokens.shape[2]
    owners = lax.axis_size("seq")
    cols_each = width_all // owners
    normed1 = layer_norm(tokens, shift1, scale1)
    grouped = normed1.reshape(1, rows_here, owners, cols_each, D)
    query_weight = col_qkv[:, :D].reshape(D, HEADS, HD)
    key_weight = col_qkv[:, D : 2 * D].reshape(D, HEADS, HD)
    value_weight = col_qkv[:, 2 * D :].reshape(D, HEADS, HD)
    out_weight = col_out.reshape(HEADS, HD, D)
    piece = lax.all_to_all(grouped, "seq", split_axis=2, concat_axis=1, tiled=True)
    height = piece.shape[1]
    count = piece.shape[3]
    local = piece[0, :, 0]
    query = jnp.einsum(
        "iwc,chd->whid", local, query_weight, preferred_element_type=jnp.float32
    ).astype(jnp.bfloat16)
    key = jnp.einsum("iwc,chd->whid", local, key_weight, preferred_element_type=jnp.float32).astype(
        jnp.bfloat16
    )
    value = jnp.einsum(
        "iwc,chd->whid", local, value_weight, preferred_element_type=jnp.float32
    ).astype(jnp.bfloat16)
    scores = jnp.einsum("whid,whjd->whij", query, key, preferred_element_type=jnp.float32) * HD ** (
        -0.5
    )
    weights = jax.nn.softmax(scores, axis=-1).astype(jnp.bfloat16)
    context = jnp.einsum(
        "whij,whjd->whid", weights, value, preferred_element_type=jnp.float32
    ).astype(jnp.bfloat16)
    out = jnp.einsum(
        "whid,hde->iwe", context, out_weight, preferred_element_type=jnp.float32
    ).astype(jnp.bfloat16)
    attended = out.reshape(1, height, 1, count, D)
    back = lax.all_to_all(attended, "seq", split_axis=1, concat_axis=2, tiled=True)
    back = back.reshape(1, rows_here, width_all, D)
    hidden = (tokens.astype(jnp.float32) + back.astype(jnp.float32)).astype(jnp.bfloat16)
    normed2 = layer_norm(hidden, shift2, scale2)
    flat = normed2.reshape(-1, D)
    positions = flat.shape[0]
    every = lax.all_gather(normed2, "bin", axis=0, tiled=True)
    nbins = every.shape[0]
    every_flat = every.reshape(-1, D)
    query = jnp.dot(flat, bin_qkv[:, :D], preferred_element_type=jnp.float32).astype(jnp.bfloat16)
    keys_all = jnp.dot(
        every_flat, bin_qkv[:, D : 2 * D], preferred_element_type=jnp.float32
    ).astype(jnp.bfloat16)
    values_all = jnp.dot(
        every_flat, bin_qkv[:, 2 * D :], preferred_element_type=jnp.float32
    ).astype(jnp.bfloat16)
    context = across_bins(
        query.reshape(1, positions, HEADS, HD),
        keys_all.reshape(nbins, positions, HEADS, HD),
        values_all.reshape(nbins, positions, HEADS, HD),
    )
    projected = jnp.dot(context.reshape(-1, D), bin_out, preferred_element_type=jnp.float32)
    projected = projected.reshape(1, rows_here, width_all, D)
    return (hidden.astype(jnp.float32) + projected).astype(jnp.bfloat16)


def per_device(tokens, *rest):
    owners, width = lax.axis_size("seq"), tokens.shape[2]
    small = owners in (4, 8) and width % owners == 0 and lax.axis_size("bin") == 4
    if small and tokens.shape[1] * owners % 16 == 0 and tokens.shape[1] * width <= 256:
        return column_path(tokens, *rest)
    return general_path(tokens, *rest)


def solution(mesh):
    placed = (P("bin", "seq", None, None), P(), P(), P(), P(), P(), P())
    return jax.shard_map(
        per_device,
        mesh=mesh,
        in_specs=placed,
        out_specs=P("bin", "seq", None, None),
        check_vma=False,
    )
```

```python
import functools
import math

import jax
import jax.numpy as jnp
from jax import lax
from jax.experimental import pallas as pl
from jax.experimental.pallas import tpu as pltpu
from jax.sharding import PartitionSpec as P

D = 768
HEADS = 12
HD = 64
FREQ = 256
PAIR = 2 * HD
ORDER = (0, 1, 2, 3)
RETURN = (0, 1, 3, 2)
BF = jnp.bfloat16
F32 = jnp.float32


def modulation(timestep, mod_weight):
    half = FREQ // 2
    freqs = jnp.exp(-math.log(10000.0) * jnp.arange(half, dtype=jnp.float32) / half)
    angle = timestep.astype(jnp.float32)[0] * freqs
    emb = jax.nn.silu(jnp.concatenate([jnp.cos(angle), jnp.sin(angle)])).astype(jnp.bfloat16)
    return jnp.dot(emb[None, :], mod_weight, preferred_element_type=jnp.float32)[0]


def norm_rows(xf, mod_ref, which):
    shift = mod_ref[2 * which : 2 * which + 1, :]
    scale = mod_ref[2 * which + 1 : 2 * which + 2, :]
    mean = jnp.mean(xf, axis=-1, keepdims=True)
    cent = xf - mean
    var = jnp.mean(cent * cent, axis=-1, keepdims=True)
    return (cent * lax.rsqrt(var + 1e-06) * (1.0 + scale) + shift).astype(BF)


def stacked(refs):
    return jnp.concatenate([r[...].astype(F32) for r in refs], axis=0)


def project(normed, w_ref, which, out_ref, factor=None):
    y = jnp.dot(normed, w_ref[:, which * D : (which + 1) * D], preferred_element_type=F32)
    if factor is not None:
        y = y * factor
    out_ref[...] = y.astype(BF)


def divided(values, by, top):
    total = jnp.zeros_like(values)
    for step in range(by, top, by):
        total = total + (values >= step).astype(jnp.int32)
    return total


def partner(m, groups):
    return ORDER[m] if groups == len(ORDER) else m


def message_rows(shape, row_dim, token_dim, rows, cols, width, owner):
    r = lax.broadcasted_iota(jnp.int32, shape, row_dim)
    t = lax.broadcasted_iota(jnp.int32, shape, token_dim)
    i = divided(r, cols, shape[row_dim])
    source = i * width + owner * cols + (r - i * cols)
    hit = (r < rows * cols) & (t == source)
    return jnp.where(hit, 1.0, 0.0).astype(BF)


def pack_kernel(dims, z_ref, tok_ref, *out_refs):
    rows, cols, width = dims
    x = tok_ref[...]
    for m, out in enumerate(out_refs):
        shape = (out.shape[0], x.shape[0])
        pick = message_rows(shape, 0, 1, rows, cols, width, z_ref[0] ^ partner(m, len(out_refs)))
        out[...] = jnp.dot(pick, x, preferred_element_type=F32).astype(BF)


def token_rows(dims, pad, shape, z):
    rows, cols, width = dims
    r = lax.broadcasted_iota(jnp.int32, (1, shape[1]), 1)
    m = divided(r, pad, shape[1])
    r = r - m * pad
    i = divided(r, cols, pad)
    groups = shape[1] // pad
    back = RETURN if groups == len(RETURN) else range(groups)
    differs = sum(jnp.where(m == k, back[k], 0) for k in range(groups))
    source = i * width + (z ^ differs) * cols + (r - i * cols)
    source = jnp.where(r < rows * cols, source, -1)
    return jnp.where(source == lax.broadcasted_iota(jnp.int32, shape, 0), 1.0, 0.0).astype(BF)


def grouped_rows(dims, groups, pad, shape, row_dim):
    rows, cols, _ = dims
    flat = (shape[0], 1) if row_dim == 0 else (1, shape[1])
    r = lax.broadcasted_iota(jnp.int32, flat, row_dim)
    part, here = groups * rows * 2, rows * 2
    g = divided(r, part, shape[row_dim])
    r = r - g * part
    m = divided(r, here, part)
    r = r - m * here
    i = divided(r, 2, here)
    source = m * pad + i * cols + 2 * g + (r - 2 * i)
    hit = source == lax.broadcasted_iota(jnp.int32, shape, 1 - row_dim)
    return jnp.where(hit, 1.0, 0.0).astype(BF)


def column_marks(n, keys):
    def odd(count):
        return lax.broadcasted_iota(jnp.int32, (count, PAIR), 0) & 1

    lane = lax.broadcasted_iota(jnp.int32, (n, PAIR), 1)
    query = jnp.where(lane == odd(n), 1.0, 0.0).astype(BF)
    lane = lax.broadcasted_iota(jnp.int32, (keys, PAIR), 1)
    return query, jnp.where(lane == odd(keys), 0.0, -(2.0**100)).astype(BF)


def head_pair(q):
    low = lax.broadcasted_iota(jnp.int32, q.shape, 1) < HD
    zero = jnp.zeros_like(q)
    return jnp.concatenate([jnp.where(low, q, zero), jnp.where(low, zero, q)], axis=0)


def unpaired(c):
    n = c.shape[0] // 2
    low = lax.broadcasted_iota(jnp.int32, (n, PAIR), 1) < HD
    return jnp.where(low, c[:n], c[n:])


def regrouped(refs, dims):
    pad = refs[0].shape[0]
    n = len(refs) * dims[0] * dims[1]
    pick = grouped_rows(dims, len(refs), pad, (n, len(refs) * pad), 0)
    return jnp.dot(pick, stacked(refs).astype(BF), preferred_element_type=F32)


def col_own_kernel(groups, dims, *refs):
    own, (mod_ref, w_ref, t_ref, q_ref, k_ref, v_ref) = refs[:groups], refs[groups:]
    rows = regrouped(own, dims)
    t_ref[...] = rows.astype(BF)
    normed = norm_rows(rows, mod_ref, 0)
    project(normed, w_ref, 0, q_ref, HD**-0.5 * math.log2(math.e))
    project(normed, w_ref, 1, k_ref)
    project(normed, w_ref, 2, v_ref)


def col_attend_kernel(groups, dims, *refs):
    other = refs[:groups]
    mod_ref, w_ref, wo_ref, t_ref, q_ref, k_ref, v_ref, *refs = refs[groups:]
    *outs, k2_ref, v2_ref, c_ref = refs
    normed = norm_rows(regrouped(other, dims), mod_ref, 0)
    project(normed, w_ref, 1, k2_ref)
    project(normed, w_ref, 2, v2_ref)
    part = groups * dims[0] * 2
    q_mark, k_mark = column_marks(2 * part, 2 * part)
    ones = jnp.ones((2 * part, PAIR), BF)
    for g in range(dims[1] // 2):
        here = slice(g * part, (g + 1) * part)
        for j in range(HEADS // 2):
            lanes = slice(j * PAIR, (j + 1) * PAIR)
            q = jnp.concatenate([head_pair(q_ref[here, lanes]), q_mark], axis=1)
            k = jnp.concatenate([k_ref[here, lanes], k2_ref[here, lanes]], axis=0)
            v = jnp.concatenate([v_ref[here, lanes], v2_ref[here, lanes]], axis=0)
            k = jnp.concatenate([k, k_mark], axis=1)
            s = lax.dot_general(q, k, (((1,), (1,)), ((), ())), preferred_element_type=F32)
            e = jnp.exp2((s - jnp.max(s, axis=-1, keepdims=True)).astype(BF))
            c = jnp.dot(e, jnp.concatenate([v, ones], axis=1), preferred_element_type=F32)
            c_ref[here, lanes] = (unpaired(c[:, :PAIR]) / unpaired(c[:, PAIR:])).astype(BF)
    a = jnp.dot(c_ref[...], wo_ref[...], preferred_element_type=F32).astype(BF)
    h = (t_ref[...].astype(F32) + a.astype(F32)).astype(BF)
    pad = outs[0].shape[0]
    put = grouped_rows(dims, groups, pad, (groups * pad, h.shape[0]), 1)
    h = jnp.dot(put, h, preferred_element_type=F32)
    for m, o in enumerate(outs):
        o[...] = h[m * pad : (m + 1) * pad].astype(BF)


def head_lanes(shape, lane_dim):
    lane = lax.broadcasted_iota(jnp.int32, shape, lane_dim)
    head = lax.broadcasted_iota(jnp.int32, shape, 1 - lane_dim)
    return ((lane >= head * HD) & (lane < (head + 1) * HD)).astype(F32).astype(BF)


def key_scores(query, normed, w_ref, s_ref):
    k = jnp.dot(normed, w_ref[:, D : 2 * D], preferred_element_type=F32).astype(BF).astype(F32)
    s_ref[...] = jnp.dot(
        (query * k).astype(BF), head_lanes((D, 128), 0), preferred_element_type=F32
    )


def split_rows(rows, parts):
    start = 0
    for part in parts:
        part[...] = rows[start : start + part.shape[0]].astype(BF)
        start += part.shape[0]


def bin_own_kernel(count, *refs):
    chunks, (mod_ref, w_ref, q_ref, v_ref, s_ref, *parts) = refs[:count], refs[count:]
    normed = norm_rows(stacked(chunks), mod_ref, 1)
    split_rows(normed.astype(F32), parts)
    project(normed, w_ref, 0, q_ref, HD**-0.5)
    key_scores(q_ref[...].astype(F32), normed, w_ref, s_ref)
    project(normed, w_ref, 2, v_ref)


def bin_early_kernel(count, own_ref, *refs):
    chunks, (q_ref, mod_ref, w_ref, q2_ref, v_ref, s_ref, *parts) = refs[:count], refs[count:]
    split = q_ref.shape[0]
    normed = norm_rows(stacked((*chunks, own_ref)), mod_ref, 1)
    split_rows(normed.astype(F32)[:split], parts)
    q2 = jnp.dot(normed, w_ref[:, :D], preferred_element_type=F32)[split:] * HD**-0.5
    q2_ref[...] = q2.astype(BF)
    query = jnp.concatenate([q_ref[...].astype(F32), q2_ref[...].astype(F32)], axis=0)
    key_scores(query, normed, w_ref, s_ref)
    project(normed, w_ref, 2, v_ref)


def bin_late_kernel(count, *refs):
    chunks, (q_ref, q2_ref, mod_ref, w_ref, v_ref, s_ref) = refs[:count], refs[count:]
    core_ref, core_last_ref, *far, last_ref = chunks
    fresh = norm_rows(stacked((core_last_ref, last_ref)), mod_ref, 1).astype(F32)
    pad = last_ref.shape[0]
    pieces = [core_ref[...].astype(F32), fresh[:pad], stacked(far), fresh[pad:]]
    normed = jnp.concatenate(pieces, axis=0).astype(BF)
    q = stacked((q_ref, q2_ref))
    key_scores(jnp.concatenate([q, q], axis=0), normed, w_ref, s_ref)
    project(normed, w_ref, 2, v_ref)


def bin_attend_kernel(groups, dims, z_ref, last_ref, *refs):
    own, refs = refs[:groups], refs[groups:]
    q2_ref, mod_ref, w_ref, wo_ref, v1_ref, s1_ref, v2_ref, s2_ref, v3_ref, s3_ref = refs[:-1]
    out_ref = refs[-1]
    n, m = s2_ref.shape[0], s1_ref.shape[0]
    normed = norm_rows(last_ref[...].astype(F32), mod_ref, 1)
    k = jnp.dot(normed, w_ref[:, D : 2 * D], preferred_element_type=F32).astype(BF).astype(F32)
    s4 = jnp.dot(
        (q2_ref[...].astype(F32) * k).astype(BF), head_lanes((D, 128), 0),
        preferred_element_type=F32,
    )
    v4 = jnp.dot(normed, w_ref[:, 2 * D :], preferred_element_type=F32)

    def of_bins(one, two, three, four):
        return [
            jnp.concatenate([one, two[m:]], axis=0),
            three[:n],
            jnp.concatenate([two[:m], three[n + m :]], axis=0),
            jnp.concatenate([three[n : n + m], four], axis=0),
        ]

    scores = of_bins(s1_ref[...], s2_ref[...], s3_ref[...], s4)
    values = of_bins(*(r[...].astype(F32) for r in (v1_ref, v2_ref, v3_ref)), v4)
    top = functools.reduce(jnp.maximum, scores)
    exps = [jnp.exp(s - top) for s in scores]
    scale = 1.0 / functools.reduce(jnp.add, exps)
    spread = head_lanes((128, D), 1)
    weights = jnp.concatenate([e * scale for e in exps], axis=0).astype(BF)
    weights = jnp.dot(weights, spread, preferred_element_type=F32)
    rows = scale.shape[0]
    parts = (weights[i * rows : (i + 1) * rows] * v for i, v in enumerate(values))
    c = functools.reduce(jnp.add, parts)
    out = jnp.dot(c.astype(BF), wo_ref[...], preferred_element_type=F32)
    out = (stacked(own) + out).astype(BF)
    put = token_rows(dims, own[0].shape[0], (out_ref.shape[0], n), z_ref[0])
    out_ref[...] = jnp.dot(put, out, preferred_element_type=F32).astype(BF)


def call(kernel, outs, scratch, *args, cost=10**6):
    def space(a):
        return pl.BlockSpec(memory_space=pltpu.SMEM if a.dtype == jnp.int32 else pltpu.VMEM)

    return pl.pallas_call(
        kernel,
        out_shape=[jax.ShapeDtypeStruct(*o) for o in outs],
        in_specs=[space(a) for a in args],
        out_specs=[pl.BlockSpec(memory_space=pltpu.VMEM)] * len(outs),
        scratch_shapes=[pltpu.VMEM(*s) for s in scratch],
        compiler_params=pltpu.CompilerParams(vmem_limit_bytes=24 * 1024 * 1024),
        cost_estimate=pl.CostEstimate(flops=cost, bytes_accessed=cost // 1000, transcendentals=0),
    )(*args)


def column_path(tokens, timestep, mod_weight, col_qkv, col_out, bin_qkv, bin_out):
    rows, width = tokens.shape[1], tokens.shape[2]
    owners = lax.axis_size("seq")
    groups = owners // 2
    cols = width // groups
    dims = (rows, cols, width)
    pad = -(-rows * cols // 8) * 8
    n = rows * width

    def over_group(x, m):
        return lax.ppermute(x, "seq", [(i, i ^ (2 * partner(m, groups))) for i in range(owners)])

    def over_pair(x):
        return lax.ppermute(x, "seq", [(i, i ^ 1) for i in range(owners)])

    def over_bin(x, m):
        return lax.ppermute(x, "bin", [(i, i ^ m) for i in range(4)])

    message, full = ((pad, D), BF), ((n, D), BF)
    z = (lax.axis_index("seq") // 2).astype(jnp.int32).reshape(1)
    flat = tokens.reshape(rows * width, D)
    sent = call(
        functools.partial(pack_kernel, dims), [message] * groups, [], z, flat, cost=10**10
    )
    mod = modulation(timestep, mod_weight).reshape(4, D)
    own = [sent[0]] + [over_group(sent[m], m) for m in range(1, groups)]
    own[1], mod = lax.optimization_barrier((own[1], mod))
    other = [over_pair(x) for x in own]

    t, q, k, v = call(
        functools.partial(col_own_kernel, groups, dims), [full] * 4, [], *own, mod, col_qkv
    )
    sent = call(
        functools.partial(col_attend_kernel, groups, dims), [message] * groups, [full] * 3,
        *other, mod, col_qkv, col_out, t, q, k, v,
    )
    back = RETURN if groups == len(RETURN) else range(groups)
    places = [partner(m, groups) for m in range(groups)]
    places = [places.index(far) for far in back]
    h = [sent[0]] + [over_group(sent[m], m) for m in places[1:]]
    hy = [over_bin(x, 2) for x in h]

    def rows_of(count):
        return [((count, D), BF), ((count, 128), F32)]

    padded, early = groups * pad, (groups - 1) * pad
    parts = [((padded // 2, D), BF), ((early - padded // 2, D), BF)]
    q, v1, s1, *h_parts = call(
        functools.partial(bin_own_kernel, groups - 1),
        [((early, D), BF), *rows_of(early), ((early, D), BF)], [], *h[:-1], mod, bin_qkv,
    )
    hc = [over_bin(x, 1) for x in (*h_parts, h[-1])]
    q2, v2, s2, *hy_parts = call(
        functools.partial(bin_early_kernel, groups - 1), [message, *rows_of(padded), *parts], [],
        h[-1], *hy[:-1], q, mod, bin_qkv,
    )
    hd_early = [over_bin(x, 1) for x in hy_parts]
    last, v2 = lax.optimization_barrier((hy[-1], v2))
    hd = over_bin(last, 1)
    others = [*hc, *hd_early, last]
    v3, s3 = call(
        functools.partial(bin_late_kernel, len(others)), rows_of(2 * padded), [],
        *others, q, q2, mod, bin_qkv,
    )
    (out,) = call(
        functools.partial(bin_attend_kernel, groups, dims), [full], [],
        z, hd, *h, q2, mod, bin_qkv, bin_out, v1, s1, v2, s2, v3, s3,
    )
    return out.reshape(tokens.shape)


def layer_norm(values, shift, scale):
    xf = values.astype(jnp.float32)
    mean = jnp.mean(xf, axis=-1, keepdims=True)
    var = jnp.mean((xf - mean) ** 2, axis=-1, keepdims=True)
    return ((xf - mean) * lax.rsqrt(var + 1e-06) * (1.0 + scale) + shift).astype(jnp.bfloat16)


def across_bins(query, key, value):
    scores = jnp.sum(
        query.astype(jnp.float32)[:, None] * key.astype(jnp.float32)[None], axis=-1
    ) * HD ** (-0.5)
    weights = jax.nn.softmax(scores, axis=1).astype(jnp.bfloat16)
    context = jnp.sum(
        weights.astype(jnp.float32)[..., None] * value.astype(jnp.float32)[None], axis=1
    )
    return context.astype(jnp.bfloat16)


def general_path(tokens, timestep, mod_weight, col_qkv, col_out, bin_qkv, bin_out):
    mod = modulation(timestep, mod_weight)
    shift1, scale1, shift2, scale2 = (mod[:D], mod[D : 2 * D], mod[2 * D : 3 * D], mod[3 * D :])
    rows_here = tokens.shape[1]
    width_all = tokens.shape[2]
    owners = lax.axis_size("seq")
    cols_each = width_all // owners
    normed1 = layer_norm(tokens, shift1, scale1)
    grouped = normed1.reshape(1, rows_here, owners, cols_each, D)
    query_weight = col_qkv[:, :D].reshape(D, HEADS, HD)
    key_weight = col_qkv[:, D : 2 * D].reshape(D, HEADS, HD)
    value_weight = col_qkv[:, 2 * D :].reshape(D, HEADS, HD)
    out_weight = col_out.reshape(HEADS, HD, D)
    piece = lax.all_to_all(grouped, "seq", split_axis=2, concat_axis=1, tiled=True)
    height = piece.shape[1]
    count = piece.shape[3]
    local = piece[0, :, 0]
    query = jnp.einsum(
        "iwc,chd->whid", local, query_weight, preferred_element_type=jnp.float32
    ).astype(jnp.bfloat16)
    key = jnp.einsum("iwc,chd->whid", local, key_weight, preferred_element_type=jnp.float32).astype(
        jnp.bfloat16
    )
    value = jnp.einsum(
        "iwc,chd->whid", local, value_weight, preferred_element_type=jnp.float32
    ).astype(jnp.bfloat16)
    scores = jnp.einsum("whid,whjd->whij", query, key, preferred_element_type=jnp.float32) * HD ** (
        -0.5
    )
    weights = jax.nn.softmax(scores, axis=-1).astype(jnp.bfloat16)
    context = jnp.einsum(
        "whij,whjd->whid", weights, value, preferred_element_type=jnp.float32
    ).astype(jnp.bfloat16)
    out = jnp.einsum(
        "whid,hde->iwe", context, out_weight, preferred_element_type=jnp.float32
    ).astype(jnp.bfloat16)
    attended = out.reshape(1, height, 1, count, D)
    back = lax.all_to_all(attended, "seq", split_axis=1, concat_axis=2, tiled=True)
    back = back.reshape(1, rows_here, width_all, D)
    hidden = (tokens.astype(jnp.float32) + back.astype(jnp.float32)).astype(jnp.bfloat16)
    normed2 = layer_norm(hidden, shift2, scale2)
    flat = normed2.reshape(-1, D)
    positions = flat.shape[0]
    every = lax.all_gather(normed2, "bin", axis=0, tiled=True)
    nbins = every.shape[0]
    every_flat = every.reshape(-1, D)
    query = jnp.dot(flat, bin_qkv[:, :D], preferred_element_type=jnp.float32).astype(jnp.bfloat16)
    keys_all = jnp.dot(
        every_flat, bin_qkv[:, D : 2 * D], preferred_element_type=jnp.float32
    ).astype(jnp.bfloat16)
    values_all = jnp.dot(
        every_flat, bin_qkv[:, 2 * D :], preferred_element_type=jnp.float32
    ).astype(jnp.bfloat16)
    context = across_bins(
        query.reshape(1, positions, HEADS, HD),
        keys_all.reshape(nbins, positions, HEADS, HD),
        values_all.reshape(nbins, positions, HEADS, HD),
    )
    projected = jnp.dot(context.reshape(-1, D), bin_out, preferred_element_type=jnp.float32)
    projected = projected.reshape(1, rows_here, width_all, D)
    return (hidden.astype(jnp.float32) + projected).astype(jnp.bfloat16)


def per_device(tokens, *rest):
    owners, width = lax.axis_size("seq"), tokens.shape[2]
    small = owners in (4, 8) and width % owners == 0 and lax.axis_size("bin") == 4
    if small and tokens.shape[1] * owners % 16 == 0 and tokens.shape[1] * width <= 256:
        return column_path(tokens, *rest)
    return general_path(tokens, *rest)


def solution(mesh):
    placed = (P("bin", "seq", None, None), P(), P(), P(), P(), P(), P())
    return jax.shard_map(
        per_device,
        mesh=mesh,
        in_specs=placed,
        out_specs=P("bin", "seq", None, None),
        check_vma=False,
    )
```
